256 devices in a mesh: blk: 128 (over x, y, z_hi, core), rep: 2 (over z_lo).
Axes of the slice: x: 4, y: 4, z: 8 (z_hi: 4, z_lo: 2; z = z_hi * 2 + z_lo), core: 2. Of those that a mesh axis runs over, the one named last changes fastest.
Arguments:
- features: bfloat16 [131072, 128], P('blk'), may hold values from -6 to 6
- tile_index: int32 [128, 2, 3, 64], P('blk', 'rep'), may hold values from 0 to 8, as said below
- tile_counts: int32 [128, 2, 64, 128, 128], P('blk', 'rep'), may hold values from 0 to 3
- w_self: bfloat16 [128, 256], replicated, may hold values from -0.5 to 0.5
- w_neigh: bfloat16 [128, 256], replicated, may hold values from -2.5 to 2.5
- bias: float32 [256], replicated, may hold values from -3 to 3
- pos_pairs: int32 [131072, 2], P('blk'), may hold values from 0 to 1023
- neg_pairs: int32 [131072, 2], P('blk'), may hold values from 0 to 1023
Outputs:
- embeddings: bfloat16 [131072, 256], P('blk')
- d_features: float32 [131072, 128], P('blk')
- d_w_self: float32 [128, 256], replicated
- d_w_neigh: float32 [128, 256], replicated
- d_bias: float32 [256], replicated
The draws below stay inside these ranges and needn't reach their ends.
Inputs may be any that keep to these rules, and one draw needn't show every extreme that they name: `tile_index`: Rows 1 and 2 lie below 8.
All inputs are finite; a program needn't handle non-finite values.
Results may differ from the reference program's by a relative error of at most 0.0085.
Values may be sent and summed in bfloat16 or wider, within the bound.
No kernel may reach another device: no remote copies, remote signals or barrier semaphores. Data moves between devices by JAX's collectives and lax.ppermute only.
A program may use at most 64 MiB of HBM per device.

```python
import math
import jax
import jax.numpy as jnp
from jax import lax

FEAT = 128
HID = 256
TILE = 128
ROWS = 1024
TILES = 64
BLOCKS = 128
REPS = 2
STEPS = 8
NODES = 131072
PAIRS = 1024


def draw_tile_index(key, part):
    key = jax.random.fold_in(key, 3)
    subkeys = jax.random.split(key, 5)
    devices = BLOCKS * REPS
    levels = jax.random.randint(subkeys[0], (devices,), 1, 9)
    used_slots = jnp.maximum(1, levels * levels * TILES // 64)
    fullest = jax.random.randint(subkeys[1], (), 0, devices)
    used_slots = jnp.where(jnp.arange(devices) == fullest, TILES, used_slots)
    slot_ids = jnp.arange(TILES)
    step_ids = jax.random.randint(subkeys[2], (devices, TILES), 0, STEPS)
    step_ids = jnp.where(slot_ids[None, :] < used_slots[:, None], step_ids, STEPS)
    step_ids = jnp.sort(step_ids, axis=1)
    dst_rows = jax.random.randint(subkeys[3], (devices, TILES), 0, ROWS // TILE)
    src_cols = jax.random.randint(subkeys[4], (devices, TILES), 0, ROWS // TILE)
    table = jnp.stack([step_ids, dst_rows, src_cols], axis=1)
    return table.reshape(BLOCKS, REPS, 3, TILES).astype(jnp.int32)


def draw_tile_counts(key, part):
    key = jax.random.fold_in(key, 7)
    ticket = jax.random.randint(key, (BLOCKS, REPS, TILES, TILE, TILE), 0, 1000)
    return ((ticket < 25).astype(jnp.int32) + (ticket < 6).astype(jnp.int32) + (ticket < 1).astype(jnp.int32)).astype(jnp.int32)


def set_ends(values, stream_key, low, high):
    longest = values.shape.index(max(values.shape))
    spots = []
    for shift in (0, 1):
        where = [jax.random.randint(jax.random.fold_in(stream_key, axis), (), 0, length) for axis, length in enumerate(values.shape)]
        where[longest] = (where[longest] + shift) % values.shape[longest]
        spots.append(tuple(where))
    return values.at[spots[0]].set(low).at[spots[1]].set(high)


def steps_of(own_key, dims, shards, low, top_value):
    def one(position, parts):
        steps = jax.random.uniform(jax.random.fold_in(jax.random.fold_in(own_key, 6), position), (parts,), jnp.float32, low / len(shards), top_value / len(shards))
        return jnp.repeat(jnp.exp(steps), dims[position] // parts).reshape((-1,) + (1,) * (len(dims) - position - 1))

    gain = one(*shards[0])
    for cut in shards[1:]:
        gain = gain * one(*cut)
    return gain


def centred(own_key, dims, width, bound, cuts=(), held_as=jnp.bfloat16):
    values = width * jax.random.normal(own_key, dims, jnp.float32)
    if cuts:
        values = values * steps_of(own_key, dims, cuts, -0.22, 0.18)
    return jnp.clip(values, -bound, bound).astype(held_as)


def setup_inputs(seed: int = 0) -> dict:
    key_list = jax.random.split(jax.random.key(seed), 9)
    return {
        "features": centred(key_list[0], (NODES, FEAT), 1.0, 6.0, ((0, 128),)),
        "tile_index": draw_tile_index(jax.random.fold_in(key_list[8], 71), 0),
        "tile_counts": draw_tile_counts(jax.random.fold_in(key_list[8], 71), 0),
        "w_self": centred(key_list[3], (FEAT, HID), FEAT ** -0.5, 0.5),
        "w_neigh": centred(key_list[4], (FEAT, HID), 0.25, 2.5),
        "bias": centred(key_list[5], (HID,), 0.5, 3.0, (), jnp.float32),
        "pos_pairs": set_ends(jax.random.randint(key_list[6], (BLOCKS * PAIRS, 2), 0, ROWS), jax.random.fold_in(key_list[6], 1), 0, ROWS - 1).astype(jnp.int32),
        "neg_pairs": set_ends(jax.random.randint(key_list[7], (BLOCKS * PAIRS, 2), 0, ROWS), jax.random.fold_in(key_list[7], 1), 0, ROWS - 1).astype(jnp.int32),
    }


norm_eps = 1e-05
contract_rows = (((0,), (0,)), ((), ()))
contract_cols = (((1,), (1,)), ((), ()))

def tile_items(index_block, count_block):
    step_of = index_block[:, 0, :].reshape(-1)
    dst_of = index_block[:, 1, :].reshape(-1)
    src_of = index_block[:, 2, :].reshape(-1)
    rep_of = jnp.repeat(jnp.arange(REPS, dtype=jnp.int32), TILES)
    tile_stack = count_block.reshape(REPS * TILES, TILE, TILE)
    return (step_of, dst_of, src_of, rep_of, tile_stack)

def source_start(block_id, step_id, rep_id, src_row):
    source = (block_id - rep_id - REPS * step_id) % BLOCKS
    return (source * ROWS + src_row * TILE).astype(jnp.int32)

def aggregate_block(block_id, index_block, count_block, features):

    def add_tile(partial_value, item_tuple):
        totals, degree = partial_value
        step_id, dst_row, src_row, rep_id, tile_block = item_tuple
        weight = jnp.where(step_id < STEPS, tile_block, 0).astype(jnp.bfloat16)
        src_start = source_start(block_id, step_id, rep_id, src_row)
        src_rows = lax.dynamic_slice_in_dim(features, src_start, TILE, 0)
        product = jnp.dot(weight, src_rows, preferred_element_type=jnp.float32)
        dst_start = (dst_row * TILE).astype(jnp.int32)
        totals = lax.dynamic_update_slice_in_dim(totals, lax.dynamic_slice_in_dim(totals, dst_start, TILE, 0) + product, dst_start, 0)
        row_sums = lax.optimization_barrier(jnp.sum(weight.astype(jnp.float32), axis=1))
        degree = lax.dynamic_update_slice_in_dim(degree, lax.dynamic_slice_in_dim(degree, dst_start, TILE, 0) + row_sums, dst_start, 0)
        return ((totals, degree), None)
    initial = (jnp.zeros((ROWS, FEAT), jnp.float32), jnp.zeros((ROWS,), jnp.float32))
    result, _ = lax.scan(add_tile, initial, tile_items(index_block, count_block))
    return result

def pair_gradient(hidden, pos_pairs, neg_pairs, base):
    all_pairs = jnp.concatenate([pos_pairs, neg_pairs], axis=0) + jnp.concatenate([base, base], axis=0)[:, None]
    left_rows = hidden[all_pairs[:, 0]]
    right_rows = hidden[all_pairs[:, 1]]
    score_scale = 1.0 / math.sqrt(HID)
    scores = lax.optimization_barrier(jnp.sum(left_rows * right_rows, axis=1)) * score_scale
    count_pos = pos_pairs.shape[0]
    coefficient = jnp.concatenate([-jax.nn.sigmoid(-scores[:count_pos]), jax.nn.sigmoid(scores[count_pos:])], axis=0) * score_scale
    d_hidden = jnp.zeros_like(hidden).at[all_pairs[:, 0]].add(coefficient[:, None] * right_rows)
    return d_hidden.at[all_pairs[:, 1]].add(coefficient[:, None] * left_rows)

def reference(features, tile_index, tile_counts, w_self, w_neigh, bias, pos_pairs, neg_pairs):
    block_ids = jnp.arange(BLOCKS, dtype=jnp.int32)

    def aggregate_entry(mapped):
        return aggregate_block(mapped[0], mapped[1], mapped[2], features)
    totals, degree = lax.map(aggregate_entry, (block_ids, tile_index, tile_counts))
    totals = totals.reshape(NODES, FEAT)
    degree = degree.reshape(NODES)
    divisor = jnp.maximum(degree, 1.0)
    neighbour_mean = (totals / divisor[:, None]).astype(jnp.bfloat16)
    preact = jnp.dot(features, w_self, preferred_element_type=jnp.float32) + jnp.dot(neighbour_mean, w_neigh, preferred_element_type=jnp.float32) + bias
    inverse = lax.rsqrt(lax.optimization_barrier(jnp.mean(preact * preact, axis=1, keepdims=True)) + norm_eps)
    hidden = preact * inverse
    embeddings = hidden.astype(jnp.bfloat16)
    base = jnp.arange(BLOCKS * PAIRS, dtype=jnp.int32) // PAIRS * ROWS
    d_hidden = pair_gradient(hidden, pos_pairs, neg_pairs, base)
    d_preact = inverse * (d_hidden - hidden * lax.optimization_barrier(jnp.mean(d_hidden * hidden, axis=1, keepdims=True)))
    grad_low = d_preact.astype(jnp.bfloat16)
    d_w_self = lax.dot_general(features, grad_low, contract_rows, preferred_element_type=jnp.float32)
    d_w_neigh = lax.dot_general(neighbour_mean, grad_low, contract_rows, preferred_element_type=jnp.float32)
    d_bias = lax.optimization_barrier(jnp.sum(d_preact, axis=0))
    d_mean = (lax.dot_general(grad_low, w_neigh, contract_cols, preferred_element_type=jnp.float32) / divisor[:, None]).astype(jnp.bfloat16)
    d_self = lax.dot_general(grad_low, w_self, contract_cols, preferred_element_type=jnp.float32)

    def spread_block(d_neigh, mapped):
        block_id, index_block, count_block = mapped

        def add_tile(inner, item_tuple):
            step_id, dst_row, src_row, rep_id, tile_block = item_tuple
            weight = jnp.where(step_id < STEPS, tile_block, 0).astype(jnp.bfloat16)
            dst_start = (block_id * ROWS + dst_row * TILE).astype(jnp.int32)
            grad_rows = lax.dynamic_slice_in_dim(d_mean, dst_start, TILE, 0)
            product = lax.dot_general(weight, grad_rows, contract_rows, preferred_element_type=jnp.float32)
            src_start = source_start(block_id, step_id, rep_id, src_row)
            inner = lax.dynamic_update_slice_in_dim(inner, lax.dynamic_slice_in_dim(inner, src_start, TILE, 0) + product, src_start, 0)
            return (inner, None)
        d_neigh, _ = lax.scan(add_tile, d_neigh, tile_items(index_block, count_block))
        return (d_neigh, None)
    d_neigh, _ = lax.scan(spread_block, jnp.zeros((NODES, FEAT), jnp.float32), (block_ids, tile_index, tile_counts))
    d_features = d_self + d_neigh
    return (embeddings, d_features, d_w_self, d_w_neigh, d_bias)
```

```python
import math

import jax
import jax.numpy as jnp
from jax import lax
from jax.experimental import pallas as pl
from jax.experimental.pallas import tpu as pltpu
from jax.sharding import PartitionSpec as P

STEPS = 8
TILE = 128
ROWS = 1024
FEAT = 128
HID = 256
TILES = 64
BLOCKS = 128
REPS = 2
GROUP = 8
WROWS = 192
norm_eps = 1e-05
VMEM_LIMIT = 56 * 1024 * 1024

vmem = pl.BlockSpec(memory_space=pltpu.VMEM)
smem = pl.BlockSpec(memory_space=pltpu.SMEM)
anywhere = pl.BlockSpec(memory_space=pl.ANY)


def params():
    return pltpu.CompilerParams(vmem_limit_bytes=VMEM_LIMIT)


def cost(flops, bytes_accessed):
    return pl.CostEstimate(flops=flops, bytes_accessed=bytes_accessed, transcendentals=0)


def shifted(value, source_of):
    route = []
    for block in range(BLOCKS):
        for rep in range(REPS):
            source = source_of(block, rep)
            if source is not None:
                route.append(((source[0] % BLOCKS) * REPS + source[1], block * REPS + rep))
    return lax.ppermute(value, ("blk", "rep"), route)


def tiles_kernel(index_ref, counts_ref, tile_ref, turned_ref, degree_ref, sums):
    group = pl.program_id(0)

    @pl.when(group == 0)
    def _():
        sums[...] = jnp.zeros_like(sums)

    ones = jnp.ones((8, TILE), jnp.bfloat16)
    for k in range(GROUP):
        slot = group * GROUP + k
        used = index_ref[0, slot] < STEPS
        counts = jnp.where(used, counts_ref[k], 0).astype(jnp.float32)
        turned = counts.T.astype(jnp.bfloat16)
        tile_ref[k] = counts.astype(jnp.bfloat16)
        turned_ref[k] = turned
        row = index_ref[1, slot]
        sums[row] += jnp.dot(ones, turned, preferred_element_type=jnp.float32)

    @pl.when(group == pl.num_programs(0) - 1)
    def _():
        degree_ref[...] = sums[:, 0, :]


def prepare_tiles(index, counts):
    spec = pl.BlockSpec((GROUP, TILE, TILE), lambda g: (g, 0, 0))
    shape = jax.ShapeDtypeStruct((TILES, TILE, TILE), jnp.bfloat16)
    return pl.pallas_call(
        tiles_kernel,
        grid=(TILES // GROUP,),
        in_specs=[smem, spec],
        out_specs=[spec, spec, pl.BlockSpec((8, TILE), lambda g: (0, 0))],
        out_shape=[shape, shape, jax.ShapeDtypeStruct((8, TILE), jnp.float32)],
        scratch_shapes=[pltpu.VMEM((8, 8, TILE), jnp.float32)],
        compiler_params=params(),
        cost_estimate=cost(10**9, 8 * 2**20),
        name="prepare_tiles",
    )(index, counts)


def pairs_kernel(pos_ref, neg_ref, pos_turned, neg_turned, joined_ref, left, right):
    for sign, (pairs, turned) in enumerate(((pos_ref, pos_turned), (neg_ref, neg_turned))):
        lanes = lax.broadcasted_iota(jnp.int32, (128, ROWS), 1)

        def fill(i, carry, pairs=pairs):
            at = pl.ds(pl.multiple_of(i * 128, 128), 128)
            left[at, :] = (pairs[at, 0:1] == lanes).astype(jnp.float32).astype(jnp.bfloat16)
            right[at, :] = (pairs[at, 1:2] == lanes).astype(jnp.float32).astype(jnp.bfloat16)
            return carry

        lax.fori_loop(0, ROWS // 128, fill, 0)

        def count(i, carry, sign=sign, turned=turned):
            at = pl.ds(pl.multiple_of(i * 128, 128), 128)
            rows = lax.broadcasted_iota(jnp.int32, (128, ROWS), 0) + i * 128
            from_left = (turned[0:1, :] == rows).astype(jnp.float32).astype(jnp.bfloat16)
            from_right = (turned[1:2, :] == rows).astype(jnp.float32).astype(jnp.bfloat16)
            joined_ref[sign, at, :] = jnp.dot(
                from_left, right[...], preferred_element_type=jnp.float32
            ) + jnp.dot(from_right, left[...], preferred_element_type=jnp.float32)
            return carry

        lax.fori_loop(0, ROWS // 128, count, 0)


def join_pairs(pos_pairs, neg_pairs):
    return pl.pallas_call(
        pairs_kernel,
        in_specs=[vmem] * 4,
        out_specs=vmem,
        out_shape=jax.ShapeDtypeStruct((2, ROWS, ROWS), jnp.float32),
        scratch_shapes=[pltpu.VMEM((ROWS, ROWS), jnp.bfloat16)] * 2,
        compiler_params=params(),
        cost_estimate=cost(8 * 10**9, 8 * 2**20),
        name="join_pairs",
    )(pos_pairs, neg_pairs, pos_pairs.T, neg_pairs.T)


def gather_kernel(count, index_ref, tile_ref, *refs):
    sources, (out_ref, held, total, sem) = refs[:count], refs[count:]
    span = STEPS * ROWS // count
    copies = [
        pltpu.make_async_copy(source, held.at[pl.ds(k * span, span)], sem.at[k])
        for k, source in enumerate(sources)
    ]
    for copy in copies:
        copy.start()
    total[...] = jnp.zeros_like(total)
    for copy in copies:
        copy.wait()

    def some(j, carry):
        for u in range(4):
            slot = j * 4 + u
            step = jnp.minimum(index_ref[0, slot], STEPS - 1)
            source = pl.multiple_of(step * ROWS + index_ref[2, slot] * TILE, TILE)
            target = pl.multiple_of(index_ref[1, slot] * TILE, TILE)
            total[pl.ds(target, TILE), :] += jnp.dot(
                tile_ref[slot], held[pl.ds(source, TILE), :], preferred_element_type=jnp.float32
            )
        return carry

    lax.fori_loop(0, TILES // 4, some, 0)
    out_ref[...] = total[...].astype(jnp.bfloat16)


def gather_tiles(index, tiles, sources):
    return pl.pallas_call(
        lambda *refs: gather_kernel(len(sources), *refs),
        in_specs=[smem, vmem] + [anywhere] * len(sources),
        out_specs=vmem,
        out_shape=jax.ShapeDtypeStruct((ROWS, FEAT), jnp.bfloat16),
        scratch_shapes=[
            pltpu.VMEM((STEPS * ROWS, FEAT), jnp.bfloat16),
            pltpu.VMEM((ROWS, FEAT), jnp.float32),
            pltpu.SemaphoreType.DMA((len(sources),)),
        ],
        compiler_params=params(),
        cost_estimate=cost(10**9, 4 * 2**20),
        name="gather_tiles",
    )(index, tiles, *sources)


def layer_kernel(
    rep_ref, mine_ref, other_ref, deg_mine, deg_other, feat_ref, w_self, w_neigh, bias, joined,
    emb_ref, d_self_ref, d_mean_ref, d_weight_ref,
    counts, hidden, scaled, mean, inverse, grad, bias_sum, sem,
):
    copy = pltpu.make_async_copy(joined, counts, sem)
    copy.start()
    factor = -math.log2(math.e) / math.sqrt(HID)
    nt = (((1,), (1,)), ((), ()))
    tn = (((0,), (0,)), ((), ()))

    def divisor_of(i):
        row = deg_mine[pl.ds(i, 1), :] + deg_other[pl.ds(i, 1), :]
        return jnp.broadcast_to(jnp.maximum(row, 1.0), (TILE, TILE)).T

    for i in range(ROWS // TILE):
        at = pl.ds(i * TILE, TILE)
        total = mine_ref[at, :].astype(jnp.float32) + other_ref[at, :].astype(jnp.float32)
        low = (total / divisor_of(i)).astype(jnp.bfloat16)
        mean[at, :] = low
        preact = (
            jnp.dot(feat_ref[at, :], w_self[...], preferred_element_type=jnp.float32)
            + jnp.dot(low, w_neigh[...], preferred_element_type=jnp.float32)
            + bias[...]
        )
        inv = lax.rsqrt(jnp.mean(preact * preact, axis=1, keepdims=True) + norm_eps)
        hid = preact * inv
        hidden[at, :] = hid
        inverse[at, :] = inv
        emb_ref[at, :] = hid.astype(jnp.bfloat16)
        scaled[at, :] = (hid * factor).astype(jnp.bfloat16)

    copy.wait()
    bias_sum[...] = jnp.zeros_like(bias_sum)
    diagonal = lax.broadcasted_iota(jnp.int32, (TILE, TILE), 0) == lax.broadcasted_iota(
        jnp.int32, (TILE, TILE), 1
    )
    for i in range(ROWS // TILE):
        at = pl.ds(i * TILE, TILE)
        power = lax.dot_general(scaled[at, :], emb_ref[...], nt, preferred_element_type=jnp.float32)
        grown = jnp.exp2(power)
        coef = (counts[1, at, :] - counts[0, at, :] * grown) * pl.reciprocal(
            1.0 + grown, approx=True
        )
        own = jnp.where(diagonal, coef[:, i * TILE : (i + 1) * TILE], 0.0)
        weight = jnp.sum(own, axis=1, keepdims=True)
        parts = []
        if i > 0:
            parts.append(coef[:, : i * TILE])
        parts.append(coef[:, i * TILE : (i + 1) * TILE] - own)
        if i < ROWS // TILE - 1:
            parts.append(coef[:, (i + 1) * TILE :])
        off = jnp.concatenate(parts, axis=1).astype(jnp.bfloat16)
        hid = hidden[at, :]
        d_hidden = (
            jnp.dot(off, emb_ref[...], preferred_element_type=jnp.float32) + weight * hid
        ) * (1.0 / math.sqrt(HID))
        d_preact = inverse[at, :] * (
            d_hidden - hid * jnp.mean(d_hidden * hid, axis=1, keepdims=True)
        )
        bias_sum[...] += jnp.sum(d_preact.reshape(TILE // 8, 8, HID), axis=0)
        low = d_preact.astype(jnp.bfloat16)
        grad[at, :] = low
        d_self_ref[at, :] = lax.dot_general(low, w_self[...], nt, preferred_element_type=jnp.float32)
        d_mean_ref[at, :] = (
            lax.dot_general(low, w_neigh[...], nt, preferred_element_type=jnp.float32)
            / divisor_of(i)
        ).astype(jnp.bfloat16)
    chosen = jnp.where(rep_ref[0] == 0, feat_ref[...].astype(jnp.float32), mean[...].astype(jnp.float32))
    d_weight_ref[0:FEAT, :] = lax.dot_general(
        chosen.astype(jnp.bfloat16), grad[...], tn, preferred_element_type=jnp.float32
    )
    d_weight_ref[FEAT : FEAT + 8, :] = jnp.broadcast_to(
        jnp.sum(bias_sum[...], axis=0, keepdims=True), (8, HID)
    )
    d_weight_ref[FEAT + 8 :, :] = jnp.zeros((WROWS - FEAT - 8, HID), jnp.float32)


def layer(rep, mine, other, deg_mine, deg_other, features, w_self, w_neigh, bias, joined):
    shapes = [
        jax.ShapeDtypeStruct((ROWS, HID), jnp.bfloat16),
        jax.ShapeDtypeStruct((ROWS, FEAT), jnp.float32),
        jax.ShapeDtypeStruct((ROWS, FEAT), jnp.bfloat16),
        jax.ShapeDtypeStruct((WROWS, HID), jnp.float32),
    ]
    return pl.pallas_call(
        layer_kernel,
        in_specs=[smem] + [vmem] * 8 + [anywhere],
        out_specs=[vmem] * 4,
        out_shape=shapes,
        scratch_shapes=[
            pltpu.VMEM((2, ROWS, ROWS), jnp.float32),
            pltpu.VMEM((ROWS, HID), jnp.float32),
            pltpu.VMEM((ROWS, HID), jnp.bfloat16),
            pltpu.VMEM((ROWS, FEAT), jnp.bfloat16),
            pltpu.VMEM((ROWS, 1), jnp.float32),
            pltpu.VMEM((ROWS, HID), jnp.bfloat16),
            pltpu.VMEM((8, HID), jnp.float32),
            pltpu.SemaphoreType.DMA,
        ],
        compiler_params=params(),
        cost_estimate=cost(2 * 10**9, 12 * 2**20),
        name="layer",
    )(rep, mine, other, deg_mine, deg_other, features, w_self, w_neigh, bias, joined)


def spread_kernel(count, index_ref, turned_ref, grad_ref, *refs):
    outs, (total,) = refs[:count], refs[count:]
    total[...] = jnp.zeros_like(total)

    def some(j, carry):
        for u in range(4):
            slot = j * 4 + u
            step = jnp.minimum(index_ref[0, slot], STEPS - 1)
            target = pl.multiple_of(step * ROWS + index_ref[2, slot] * TILE, TILE)
            source = pl.multiple_of(index_ref[1, slot] * TILE, TILE)
            total[pl.ds(target, TILE), :] += jnp.dot(
                turned_ref[slot], grad_ref[pl.ds(source, TILE), :], preferred_element_type=jnp.float32
            )
        return carry

    lax.fori_loop(0, TILES // 4, some, 0)
    span = STEPS * ROWS // count
    for k, out in enumerate(outs):
        out[...] = total[pl.ds(k * span, span), :].astype(jnp.bfloat16)


def spread_tiles(index, turned, d_mean, count):
    shape = jax.ShapeDtypeStruct((STEPS * ROWS // count, FEAT), jnp.bfloat16)
    return pl.pallas_call(
        lambda *refs: spread_kernel(count, *refs),
        in_specs=[smem, vmem, vmem],
        out_specs=[vmem] * count,
        out_shape=[shape] * count,
        scratch_shapes=[pltpu.VMEM((STEPS * ROWS, FEAT), jnp.float32)],
        compiler_params=params(),
        cost_estimate=cost(10**9, 4 * 2**20),
        name="spread_tiles",
    )(index, turned, d_mean)


def flipped(value, mask):
    return shifted(value, lambda block, rep: (block ^ mask, rep))


def sum_weights(value, block):
    core, x = block & 1, block >> 5
    half, quarter = WROWS // 2, WROWS // 8
    mine = lax.dynamic_slice_in_dim(value, core * half, half, 0)
    given = lax.dynamic_slice_in_dim(value, (1 - core) * half, half, 0)
    mine = mine + flipped(given, 1)
    pieces = [lax.dynamic_slice_in_dim(mine, (x ^ k) * quarter, quarter, 0) for k in range(4)]
    arrived = [flipped(pieces[k], k << 5) for k in range(1, 4)]
    own = (pieces[0] + arrived[0]) + (arrived[1] + arrived[2])
    for shift in (3, 1):
        arrived = [flipped(own, k << shift) for k in range(1, 4)]
        own = (own + arrived[0]) + (arrived[1] + arrived[2])
    arrived = [flipped(own, k << 5) for k in range(1, 4)]
    whole = jnp.zeros((half, HID), jnp.float32)
    for k, piece in enumerate([own] + arrived):
        whole = lax.dynamic_update_slice_in_dim(whole, piece, (x ^ k) * quarter, 0)
    other = flipped(whole, 1)
    return jnp.concatenate(
        [jnp.where(core == 0, whole, other), jnp.where(core == 0, other, whole)], axis=0
    )


def body(features, tile_index, tile_counts, w_self, w_neigh, bias, pos_pairs, neg_pairs):
    block, rep = lax.axis_index("blk"), lax.axis_index("rep")
    index, counts = tile_index[0, 0], tile_counts[0, 0]

    sources = [
        shifted(features, lambda b, r, s=s: (b - r - 2 * s, r)) for s in range(STEPS)
    ]
    tiles, turned, degree = prepare_tiles(index, counts)
    joined = join_pairs(pos_pairs, neg_pairs)
    degree_other = shifted(degree, lambda b, r: (b, 1 - r))
    mine = gather_tiles(index, tiles, sources)
    other = shifted(mine, lambda b, r: (b, 1 - r))
    embeddings, d_self, d_mean, d_weight = layer(
        rep.reshape(1).astype(jnp.int32), mine, other, degree, degree_other,
        features, w_self, w_neigh, bias.reshape(1, HID), joined,
    )
    spread = spread_tiles(index, turned, d_mean, STEPS)
    landed = [
        shifted(spread[s], lambda b, r, s=s: (b + r + 2 * s, r)) for s in range(STEPS)
    ]
    partial = sum(piece.astype(jnp.float32) for piece in landed).astype(jnp.bfloat16)
    partial_other = shifted(partial, lambda b, r: (b, 1 - r))
    d_features = d_self + (partial.astype(jnp.float32) + partial_other.astype(jnp.float32))

    d_weight = sum_weights(d_weight, block)
    d_here = d_weight[:FEAT]
    d_there = shifted(d_here, lambda b, r: (b, 1 - r))
    d_w_self = jnp.where(rep == 0, d_here, d_there)
    d_w_neigh = jnp.where(rep == 0, d_there, d_here)
    return (embeddings, d_features, d_w_self, d_w_neigh, d_weight[FEAT])


def solution(mesh):
    return jax.shard_map(
        body,
        mesh=mesh,
        in_specs=(
            P("blk", None),
            P("blk", "rep", None, None),
            P("blk", "rep", None, None, None),
            P(),
            P(),
            P(),
            P("blk", None),
            P("blk", None),
        ),
        out_specs=(P("blk", None), P("blk", None), P(), P(), P()),
        check_vma=False,
    )
```

```python
import math

import jax
import jax.numpy as jnp
from jax import lax
from jax.experimental import pallas as pl
from jax.experimental.pallas import tpu as pltpu
from jax.sharding import PartitionSpec as P

STEPS = 8
TILE = 128
ROWS = 1024
FEAT = 128
HID = 256
TILES = 64
BLOCKS = 128
REPS = 2
GROUP = 8
HALF = ROWS // 2
SPAN = 2 * BLOCKS // REPS
SLOTS = 2 * STEPS + 3
WROWS = 144
norm_eps = 1e-05
VMEM_LIMIT = 56 * 1024 * 1024

vmem = pl.BlockSpec(memory_space=pltpu.VMEM)
smem = pl.BlockSpec(memory_space=pltpu.SMEM)
anywhere = pl.BlockSpec(memory_space=pl.ANY)


def params():
    return pltpu.CompilerParams(vmem_limit_bytes=VMEM_LIMIT)


def cost(flops, bytes_accessed):
    return pl.CostEstimate(flops=flops, bytes_accessed=bytes_accessed, transcendentals=0)


def shifted(value, source_of):
    route = []
    for block in range(BLOCKS):
        for rep in range(REPS):
            source = source_of(block, rep)
            if source is not None:
                route.append(((source[0] % BLOCKS) * REPS + source[1], block * REPS + rep))
    return lax.ppermute(value, ("blk", "rep"), route)


def spot(block, rep):
    return (block & 1) ^ rep, (block & ~1) + rep


def device(stream, q):
    q %= SPAN
    return (q & ~1) + (stream ^ (q & 1)), q & 1


def owner(stream, q):
    q %= SPAN
    return (q & ~1) + stream, q & 1


def along(value, distance):
    def source_of(block, rep):
        stream, q = spot(block, rep)
        return device(stream, q + distance)

    return shifted(value, source_of)


def owned(value, distance):
    def source_of(block, rep):
        stream, q = spot(block, rep)
        return owner(stream, q + distance)

    return shifted(value, source_of)


def is_late(block, rep):
    return rep == 1 and block & 1 == 0


def tied(values, *others):
    flat = lax.optimization_barrier(tuple(values) + tuple(others))
    return flat[: len(values)]


def tiles_kernel(first, index_ref, before_ref, counts_ref, tile_ref, turned_ref, degree_ref, sums):
    group = pl.program_id(0)

    @pl.when(group == 0)
    def _():
        sums[...] = jnp.zeros_like(sums)

    ones = jnp.ones((8, TILE), jnp.bfloat16)
    for k in range(GROUP):
        slot = first + group * GROUP + k
        used = index_ref[0, slot] < STEPS
        counts = jnp.where(used, counts_ref[k], 0).astype(jnp.float32)
        turned = counts.T.astype(jnp.bfloat16)
        tile_ref[k] = counts.astype(jnp.bfloat16)
        turned_ref[k] = turned
        row = index_ref[1, slot]
        sums[row] += jnp.dot(ones, turned, preferred_element_type=jnp.float32)

    @pl.when(group == pl.num_programs(0) - 1)
    def _():
        degree_ref[...] = before_ref[...] + sums[:, 0, :]


def prepare_tiles(index, before, counts, part, parts):
    share = TILES // parts
    spec = pl.BlockSpec((GROUP, TILE, TILE), lambda g: (g, 0, 0))
    shape = jax.ShapeDtypeStruct((share, TILE, TILE), jnp.bfloat16)
    whole = pl.BlockSpec((8, TILE), lambda g: (0, 0))
    return pl.pallas_call(
        lambda *refs: tiles_kernel(part * share, *refs),
        grid=(share // GROUP,),
        in_specs=[
            smem,
            whole,
            pl.BlockSpec((GROUP, TILE, TILE), lambda g: (g + part * share // GROUP, 0, 0)),
        ],
        out_specs=[spec, spec, whole],
        out_shape=[shape, shape, jax.ShapeDtypeStruct((8, TILE), jnp.float32)],
        scratch_shapes=[pltpu.VMEM((8, 8, TILE), jnp.float32)],
        compiler_params=params(),
        cost_estimate=cost(10**9, 8 * 2**20),
        name="prepare_tiles",
    )(index, before, counts)


def pairs_kernel(part, pairs, turned, joined_ref, left, right):
    lanes = lax.broadcasted_iota(jnp.int32, (128, ROWS), 1)

    def fill(i, carry):
        at = pl.ds(pl.multiple_of(i * 128, 128), 128)
        left[at, :] = (pairs[at, 0:1] == lanes).astype(jnp.float32).astype(jnp.bfloat16)
        right[at, :] = (pairs[at, 1:2] == lanes).astype(jnp.float32).astype(jnp.bfloat16)
        return carry

    lax.fori_loop(0, ROWS // 128, fill, 0)

    def count(i, carry):
        at = pl.ds(pl.multiple_of(i * 128, 128), 128)
        rows = lax.broadcasted_iota(jnp.int32, (128, ROWS), 0) + (i * 128 + part * HALF)
        from_left = (turned[0:1, :] == rows).astype(jnp.float32).astype(jnp.bfloat16)
        from_right = (turned[1:2, :] == rows).astype(jnp.float32).astype(jnp.bfloat16)
        joined_ref[at, :] = jnp.dot(
            from_left, right[...], preferred_element_type=jnp.float32
        ) + jnp.dot(from_right, left[...], preferred_element_type=jnp.float32)
        return carry

    lax.fori_loop(0, HALF // 128, count, 0)


def join_pairs(pairs, turned, part):
    return pl.pallas_call(
        lambda *refs: pairs_kernel(part, *refs),
        in_specs=[vmem] * 2,
        out_specs=vmem,
        out_shape=jax.ShapeDtypeStruct((HALF, ROWS), jnp.float32),
        scratch_shapes=[pltpu.VMEM((ROWS, ROWS), jnp.bfloat16)] * 2,
        compiler_params=params(),
        cost_estimate=cost(2 * 10**9, 4 * 2**20),
        name="join_pairs",
    )(pairs, turned)


def held_row(base, index_ref, slot):
    step = jnp.minimum(index_ref[0, slot], STEPS - 1)
    row = index_ref[2, slot]
    late = jnp.where(row >= TILES // 16, 2 * HALF, 0)
    return pl.multiple_of((2 * step + base + 1) * HALF + row * TILE - late, TILE)


def gather_kernel(info_ref, index_ref, tile_a, tile_b, features, far, *refs):
    payloads, (out_ref, held, total, sem) = refs[:STEPS], refs[STEPS:]
    pieces = [(features, HALF, 0), (far, HALF, 17), (far, 0, 18)]
    for j, payload in enumerate(payloads):
        pieces += [(payload, 0, j + 1), (payload, HALF, j + 9)]
    copies = [
        pltpu.make_async_copy(ref.at[pl.ds(at, HALF)], held.at[pl.ds(slot * HALF, HALF)], sem.at[k])
        for k, (ref, at, slot) in enumerate(pieces)
    ]
    for copy in copies:
        copy.start()
    total[...] = jnp.zeros_like(total)
    for copy in copies:
        copy.wait()
    base = info_ref[1]
    for part, tiles in enumerate((tile_a, tile_b)):

        def some(j, carry, part=part, tiles=tiles):
            for u in range(4):
                slot = j * 4 + u
                whole = slot + part * (TILES // 2)
                source = held_row(base, index_ref, whole)
                target = pl.multiple_of(index_ref[1, whole] * TILE, TILE)
                total[pl.ds(target, TILE), :] += jnp.dot(
                    tiles[slot], held[pl.ds(source, TILE), :], preferred_element_type=jnp.float32
                )
            return carry

        lax.fori_loop(0, TILES // 8, some, 0)
    out_ref[...] = total[...].astype(jnp.bfloat16)


def gather_tiles(info, index, tiles, features, far, payloads):
    return pl.pallas_call(
        gather_kernel,
        in_specs=[smem, smem, vmem, vmem] + [anywhere] * (2 + STEPS),
        out_specs=vmem,
        out_shape=jax.ShapeDtypeStruct((ROWS, FEAT), jnp.bfloat16),
        scratch_shapes=[
            pltpu.VMEM((SLOTS * HALF, FEAT), jnp.bfloat16),
            pltpu.VMEM((ROWS, FEAT), jnp.float32),
            pltpu.SemaphoreType.DMA((SLOTS,)),
        ],
        compiler_params=params(),
        cost_estimate=cost(10**9, 4 * 2**20),
        name="gather_tiles",
    )(info, index, *tiles, features, far, *payloads)


def layer_kernel(
    info_ref, mine_ref, other_ref, deg_mine, deg_other, feat_ref, w_self, w_neigh, bias,
    joined_a, joined_b, joined_c, joined_d,
    emb_ref, d_self_ref, d_mean_ref, d_weight_ref,
    counts, hidden, scaled, mean, inverse, grad, bias_sum, sem,
):
    copies = [
        pltpu.make_async_copy(ref, counts.at[k // 2, pl.ds(k % 2 * HALF, HALF)], sem.at[k])
        for k, ref in enumerate((joined_a, joined_b, joined_c, joined_d))
    ]
    for copy in copies:
        copy.start()
    factor = -math.log2(math.e) / math.sqrt(HID)
    nt = (((1,), (1,)), ((), ()))
    tn = (((0,), (0,)), ((), ()))

    def divisor_of(i):
        row = deg_mine[pl.ds(i, 1), :] + deg_other[pl.ds(i, 1), :]
        return jnp.broadcast_to(jnp.maximum(row, 1.0), (TILE, TILE)).T

    for i in range(ROWS // TILE):
        at = pl.ds(i * TILE, TILE)
        total = mine_ref[at, :].astype(jnp.float32) + other_ref[at, :].astype(jnp.float32)
        low = (total / divisor_of(i)).astype(jnp.bfloat16)
        mean[at, :] = low
        preact = (
            jnp.dot(feat_ref[at, :], w_self[...], preferred_element_type=jnp.float32)
            + jnp.dot(low, w_neigh[...], preferred_element_type=jnp.float32)
            + bias[...]
        )
        inv = lax.rsqrt(jnp.mean(preact * preact, axis=1, keepdims=True) + norm_eps)
        hid = preact * inv
        hidden[at, :] = hid
        inverse[at, :] = inv
        emb_ref[at, :] = hid.astype(jnp.bfloat16)
        scaled[at, :] = (hid * factor).astype(jnp.bfloat16)

    for copy in copies:
        copy.wait()
    bias_sum[...] = jnp.zeros_like(bias_sum)
    diagonal = lax.broadcasted_iota(jnp.int32, (TILE, TILE), 0) == lax.broadcasted_iota(
        jnp.int32, (TILE, TILE), 1
    )
    for i in range(ROWS // TILE):
        at = pl.ds(i * TILE, TILE)
        power = lax.dot_general(scaled[at, :], emb_ref[...], nt, preferred_element_type=jnp.float32)
        grown = jnp.exp2(power)
        coef = (counts[1, at, :] - counts[0, at, :] * grown) * pl.reciprocal(
            1.0 + grown, approx=True
        )
        own = jnp.where(diagonal, coef[:, i * TILE : (i + 1) * TILE], 0.0)
        weight = jnp.sum(own, axis=1, keepdims=True)
        parts = []
        if i > 0:
            parts.append(coef[:, : i * TILE])
        parts.append(coef[:, i * TILE : (i + 1) * TILE] - own)
        if i < ROWS // TILE - 1:
            parts.append(coef[:, (i + 1) * TILE :])
        off = jnp.concatenate(parts, axis=1).astype(jnp.bfloat16)
        hid = hidden[at, :]
        d_hidden = (
            jnp.dot(off, emb_ref[...], preferred_element_type=jnp.float32) + weight * hid
        ) * (1.0 / math.sqrt(HID))
        d_preact = inverse[at, :] * (
            d_hidden - hid * jnp.mean(d_hidden * hid, axis=1, keepdims=True)
        )
        bias_sum[...] += jnp.sum(d_preact.reshape(TILE // 8, 8, HID), axis=0)
        low = d_preact.astype(jnp.bfloat16)
        grad[at, :] = low
        d_self_ref[at, :] = lax.dot_general(low, w_self[...], nt, preferred_element_type=jnp.float32)
        d_mean_ref[at, :] = (
            lax.dot_general(low, w_neigh[...], nt, preferred_element_type=jnp.float32)
            / divisor_of(i)
        ).astype(jnp.bfloat16)
    chosen = jnp.where(info_ref[0] == 0, feat_ref[...].astype(jnp.float32), mean[...].astype(jnp.float32))
    d_weight_ref[0:FEAT, :] = lax.dot_general(
        chosen.astype(jnp.bfloat16), grad[...], tn, preferred_element_type=jnp.float32
    )
    d_weight_ref[FEAT : FEAT + 8, :] = jnp.broadcast_to(
        jnp.sum(bias_sum[...], axis=0, keepdims=True), (8, HID)
    )
    d_weight_ref[FEAT + 8 :, :] = jnp.zeros((WROWS - FEAT - 8, HID), jnp.float32)


def layer(info, mine, other, deg_mine, deg_other, features, w_self, w_neigh, bias, joined):
    shapes = [
        jax.ShapeDtypeStruct((ROWS, HID), jnp.bfloat16),
        jax.ShapeDtypeStruct((ROWS, FEAT), jnp.float32),
        jax.ShapeDtypeStruct((ROWS, FEAT), jnp.bfloat16),
        jax.ShapeDtypeStruct((WROWS, HID), jnp.float32),
    ]
    return pl.pallas_call(
        layer_kernel,
        in_specs=[smem] + [vmem] * 8 + [anywhere] * 4,
        out_specs=[vmem] * 4,
        out_shape=shapes,
        scratch_shapes=[
            pltpu.VMEM((2, ROWS, ROWS), jnp.float32),
            pltpu.VMEM((ROWS, HID), jnp.float32),
            pltpu.VMEM((ROWS, HID), jnp.bfloat16),
            pltpu.VMEM((ROWS, FEAT), jnp.bfloat16),
            pltpu.VMEM((ROWS, 1), jnp.float32),
            pltpu.VMEM((ROWS, HID), jnp.bfloat16),
            pltpu.VMEM((8, HID), jnp.float32),
            pltpu.SemaphoreType.DMA((4,)),
        ],
        compiler_params=params(),
        cost_estimate=cost(2 * 10**9, 12 * 2**20),
        name="layer",
    )(info, mine, other, deg_mine, deg_other, features, w_self, w_neigh, bias, *joined)


def spread_kernel(info_ref, index_ref, turned_a, turned_b, grad_ref, *refs):
    outs, (own_ref, side_ref, far_ref, total) = refs[: STEPS - 1], refs[STEPS - 1 :]
    total[...] = jnp.zeros_like(total)
    base = info_ref[1]
    for part, tiles in enumerate((turned_a, turned_b)):

        def some(j, carry, part=part, tiles=tiles):
            for u in range(4):
                slot = j * 4 + u
                whole = slot + part * (TILES // 2)
                target = held_row(base, index_ref, whole)
                source = pl.multiple_of(index_ref[1, whole] * TILE, TILE)
                total[pl.ds(target, TILE), :] += jnp.dot(
                    tiles[slot], grad_ref[pl.ds(source, TILE), :], preferred_element_type=jnp.float32
                )
            return carry

        lax.fori_loop(0, TILES // 8, some, 0)
    for k, out in enumerate(outs):
        out[:HALF, :] = total[pl.ds((k + 2) * HALF, HALF), :].astype(jnp.bfloat16)
        out[HALF:, :] = total[pl.ds((k + 10) * HALF, HALF), :].astype(jnp.bfloat16)
    own_ref[:HALF, :] = total[HALF : 2 * HALF, :]
    own_ref[HALF:, :] = total[9 * HALF : 10 * HALF, :]
    side = pl.multiple_of(jnp.where(info_ref[0] == 0, 0, 18 * HALF), HALF)
    side_ref[...] = total[pl.ds(side, HALF), :].astype(jnp.bfloat16)
    far_ref[...] = total[17 * HALF : 18 * HALF, :].astype(jnp.bfloat16)


def spread_tiles(info, index, turned, d_mean):
    half = jax.ShapeDtypeStruct((HALF, FEAT), jnp.bfloat16)
    shapes = [jax.ShapeDtypeStruct((ROWS, FEAT), jnp.bfloat16)] * (STEPS - 1)
    shapes += [jax.ShapeDtypeStruct((ROWS, FEAT), jnp.float32), half, half]
    return pl.pallas_call(
        spread_kernel,
        in_specs=[smem, smem, vmem, vmem, vmem],
        out_specs=[vmem] * len(shapes),
        out_shape=shapes,
        scratch_shapes=[pltpu.VMEM((SLOTS * HALF, FEAT), jnp.float32)],
        compiler_params=params(),
        cost_estimate=cost(10**9, 4 * 2**20),
        name="spread_tiles",
    )(info, index, *turned, d_mean)


def flipped(value, mask):
    return shifted(value, lambda block, rep: (block ^ mask, rep))


def added(left, right):
    return (left.astype(jnp.float32) + right.astype(jnp.float32)).astype(jnp.bfloat16)


def body(features, tile_index, tile_counts, w_self, w_neigh, bias, pos_pairs, neg_pairs):
    block, rep = lax.axis_index("blk"), lax.axis_index("rep")
    core = block & 1
    index, counts = tile_index[0, 0], tile_counts[0, 0]
    base = jnp.where(rep == 0, 0, jnp.where(core == 1, 1, 3))
    info = jnp.stack([rep, base]).astype(jnp.int32)
    half = features.shape[0] // 2

    given = lax.dynamic_slice_in_dim(features, rep * half, half, 0)
    here, before = owned(given, 0), owned(given, -8)
    first = jnp.concatenate([here, before], axis=0)
    pay = {0: first, 1: along(first, -1), 7: along(first, -7)}
    tiles_a, turned_a, degree = prepare_tiles(index, jnp.zeros((8, TILE), jnp.float32), counts, 0, 2)
    far = shifted(
        features, lambda b, r: ((b & ~1) - 15, 1) if is_late(b, r) else None
    )
    pos_turned, neg_turned = pos_pairs.T, neg_pairs.T
    joined = [join_pairs(pos_pairs, pos_turned, 0)]
    pay[1], pay[7], degree = tied((pay[1], pay[7], degree), joined[0])
    pay[2], pay[6] = along(pay[1], -1), along(pay[7], 1)
    tiles_b, turned_b, degree = prepare_tiles(index, degree, counts, 1, 2)
    (pairs,) = tied((pos_pairs,), pay[1])
    joined.append(join_pairs(pairs, pos_turned, 1))
    pay[2], pay[6], degree = tied((pay[2], pay[6], degree), joined[1])
    pay[3], pay[5] = along(pay[2], -1), along(pay[6], 1)
    degree_other = shifted(degree, lambda b, r: (b, 1 - r))
    (pairs,) = tied((neg_pairs,), pay[2])
    joined.append(join_pairs(pairs, neg_turned, 0))
    pay[3], pay[5] = tied((pay[3], pay[5]), joined[2])
    pay[4] = along(pay[3], -1)
    payloads = [pay[j] for j in range(STEPS)]
    mine = gather_tiles(info, index, (tiles_a, tiles_b), features, far, payloads)
    other = shifted(mine, lambda b, r: (b, 1 - r))
    (pairs,) = tied((neg_pairs,), pay[3])
    joined.append(join_pairs(pairs, neg_turned, 1))

    embeddings, d_self, d_mean, d_weight = layer(
        info, mine, other, degree, degree_other,
        features, w_self, w_neigh, bias.reshape(1, HID), joined,
    )
    *spread, own, side, late = spread_tiles(info, index, (turned_a, turned_b), d_mean)
    part = dict(enumerate(spread, 1))

    up, down = along(part[4], 1), along(part[5], -1)
    (d_weight,) = tied((d_weight,), own)
    rows = d_weight.shape[0] // 2
    kept = lax.dynamic_slice_in_dim(d_weight, core * rows, rows, 0)
    sent = lax.dynamic_slice_in_dim(d_weight, (1 - core) * rows, rows, 0)
    summed = kept + flipped(sent, 1)
    side = shifted(
        side,
        lambda b, r: device(spot(b, r)[0], spot(b, r)[1] - 1)
        if r == 1
        else (device(1, spot(b, r)[1] + 17) if b & 1 else None),
    )
    late = shifted(late, lambda b, r: device(1, spot(b, r)[1] + 16) if is_late(b, r) else None)
    up, down = added(up, part[3]), added(down, part[6])
    up, down = along(up, 1), along(down, -1)
    summed = summed + flipped(summed, 32)
    up, down = added(up, part[2]), added(down, part[7])
    (summed,) = tied((summed,), up)
    up, down = along(up, 1), along(down, 7)
    summed = summed + flipped(summed, 64)
    up = added(up, part[1])
    (summed,) = tied((summed,), up)
    up = along(up, 1)
    summed = summed + flipped(summed, 8)
    own = own + (up.astype(jnp.float32) + down.astype(jnp.float32))
    back = own[half:].astype(jnp.bfloat16)
    (summed,) = tied((summed,), back)
    back = along(back, 8)
    summed = summed + flipped(summed, 16)
    landed = (
        (own[:half] + back.astype(jnp.float32)) + (side.astype(jnp.float32) + late.astype(jnp.float32))
    ).astype(jnp.bfloat16)
    crossed = shifted(landed, lambda b, r: (b, 0) if r else (b ^ 1, 1))
    swapped = shifted(landed, lambda b, r: (b ^ r, r))
    (summed,) = tied((summed,), landed)
    summed = summed + flipped(summed, 2)
    summed = summed + flipped(summed, 4)
    lower = jnp.where(rep == 0, swapped, crossed)
    upper = jnp.where(rep == 0, crossed, swapped)
    d_features = d_self + jnp.concatenate([lower, upper], axis=0).astype(jnp.float32)

    traded = flipped(summed, 1)
    d_here = jnp.concatenate(
        [jnp.where(core == 0, summed, traded), jnp.where(core == 0, traded, summed)], axis=0
    )
    d_there = shifted(d_here[:FEAT], lambda b, r: (b, 1 - r))
    d_w_self = jnp.where(rep == 0, d_here[:FEAT], d_there)
    d_w_neigh = jnp.where(rep == 0, d_there, d_here[:FEAT])
    return (embeddings, d_features, d_w_self, d_w_neigh, d_here[FEAT])


def solution(mesh):
    return jax.shard_map(
        body,
        mesh=mesh,
        in_specs=(
            P("blk", None),
            P("blk", "rep", None, None),
            P("blk", "rep", None, None, None),
            P(),
            P(),
            P(),
            P("blk", None),
            P("blk", None),
        ),
        out_specs=(P("blk", None), P("blk", None), P(), P(), P()),
        check_vma=False,
    )
```

```python
import math

import jax
import jax.numpy as jnp
from jax import lax
from jax.experimental import pallas as pl
from jax.experimental.pallas import tpu as pltpu
from jax.sharding import PartitionSpec as P

STEPS = 8
TILE = 128
ROWS = 1024
FEAT = 128
HID = 256
TILES = 64
BLOCKS = 128
REPS = 2
GROUP = 8
HALF = ROWS // 2
SPAN = 2 * BLOCKS // REPS
SLOTS = 2 * STEPS + 3
WROWS = 144
PANEL = 256
norm_eps = 1e-05
VMEM_LIMIT = 56 * 1024 * 1024
across = (((1,), (1,)), ((), ()))
down = (((0,), (0,)), ((), ()))

vmem = pl.BlockSpec(memory_space=pltpu.VMEM)
smem = pl.BlockSpec(memory_space=pltpu.SMEM)
anywhere = pl.BlockSpec(memory_space=pl.ANY)


def params():
    return pltpu.CompilerParams(vmem_limit_bytes=VMEM_LIMIT)


def cost(flops, bytes_accessed):
    return pl.CostEstimate(flops=flops, bytes_accessed=bytes_accessed, transcendentals=0)


def shifted(value, source_of):
    route = []
    for block in range(BLOCKS):
        for rep in range(REPS):
            source = source_of(block, rep)
            if source is not None:
                route.append(((source[0] % BLOCKS) * REPS + source[1], block * REPS + rep))
    return lax.ppermute(value, ("blk", "rep"), route)


def spot(block, rep):
    return (block & 1) ^ rep, (block & ~1) + rep


def device(stream, q):
    q %= SPAN
    return (q & ~1) + (stream ^ (q & 1)), q & 1


def owner(stream, q):
    q %= SPAN
    return (q & ~1) + stream, q & 1


def along(value, distance):
    def source_of(block, rep):
        stream, q = spot(block, rep)
        return device(stream, q + distance)

    return shifted(value, source_of)


def owned(value, distance):
    def source_of(block, rep):
        stream, q = spot(block, rep)
        return owner(stream, q + distance)

    return shifted(value, source_of)


def is_late(block, rep):
    return rep == 1 and block & 1 == 0


def tied(values, *others):
    flat = lax.optimization_barrier(tuple(values) + tuple(others))
    return flat[: len(values)]


def tiles_kernel(first, index_ref, before_ref, counts_ref, tile_ref, turned_ref, degree_ref, sums):
    group = pl.program_id(0)

    @pl.when(group == 0)
    def _():
        sums[...] = jnp.zeros_like(sums)

    ones = jnp.ones((8, TILE), jnp.bfloat16)
    for k in range(GROUP):
        slot = first + group * GROUP + k
        used = index_ref[0, slot] < STEPS
        counts = jnp.where(used, counts_ref[k], 0).astype(jnp.float32)
        turned = counts.T.astype(jnp.bfloat16)
        tile_ref[k] = counts.astype(jnp.bfloat16)
        turned_ref[k] = turned
        row = index_ref[1, slot]
        sums[row] += jnp.dot(ones, turned, preferred_element_type=jnp.float32)

    @pl.when(group == pl.num_programs(0) - 1)
    def _():
        degree_ref[...] = before_ref[...] + sums[:, 0, :]


def prepare_tiles(index, before, counts, part, parts):
    share = TILES // parts
    spec = pl.BlockSpec((GROUP, TILE, TILE), lambda g: (g, 0, 0))
    shape = jax.ShapeDtypeStruct((share, TILE, TILE), jnp.bfloat16)
    whole = pl.BlockSpec((8, TILE), lambda g: (0, 0))
    return pl.pallas_call(
        lambda *refs: tiles_kernel(part * share, *refs),
        grid=(share // GROUP,),
        in_specs=[
            smem,
            whole,
            pl.BlockSpec((GROUP, TILE, TILE), lambda g: (g + part * share // GROUP, 0, 0)),
        ],
        out_specs=[spec, spec, whole],
        out_shape=[shape, shape, jax.ShapeDtypeStruct((8, TILE), jnp.float32)],
        scratch_shapes=[pltpu.VMEM((8, 8, TILE), jnp.float32)],
        compiler_params=params(),
        cost_estimate=cost(10**9, 8 * 2**20),
        name="prepare_tiles",
    )(index, before, counts)


def pairs_kernel(turned, joined_ref, left, right):
    def fill(i, carry):
        at = pl.ds(pl.multiple_of(i * TILE, TILE), TILE)
        rows = lax.broadcasted_iota(jnp.int32, (TILE, ROWS), 0) + i * TILE
        left[at, :] = (turned[0:1, :] == rows).astype(jnp.float32).astype(left.dtype)
        right[at, :] = (turned[1:2, :] == rows).astype(jnp.float32).astype(right.dtype)
        return carry

    lax.fori_loop(0, ROWS // TILE, fill, 0)
    for i in range(ROWS // PANEL):
        at = pl.ds(i * PANEL, PANEL)
        joined_ref[at, :] = lax.dot_general(
            left[at, :], right[...], across, preferred_element_type=jnp.float32
        )
    for i in range(ROWS // TILE):
        for j in range(i, ROWS // TILE):
            over = (pl.ds(i * TILE, TILE), pl.ds(j * TILE, TILE))
            under = (pl.ds(j * TILE, TILE), pl.ds(i * TILE, TILE))
            both = joined_ref[over] + joined_ref[under].T
            joined_ref[over] = both
            if i != j:
                joined_ref[under] = both.T


def join_pairs(turned):
    return pl.pallas_call(
        pairs_kernel,
        in_specs=[vmem],
        out_specs=vmem,
        out_shape=jax.ShapeDtypeStruct((ROWS, ROWS), jnp.float32),
        scratch_shapes=[pltpu.VMEM((ROWS, ROWS), jnp.float8_e4m3fn)] * 2,
        compiler_params=params(),
        cost_estimate=cost(3 * 10**9, 4 * 2**20),
        name="join_pairs",
    )(turned)


def held_row(base, index_ref, slot):
    step = jnp.minimum(index_ref[0, slot], STEPS - 1)
    row = index_ref[2, slot]
    late = jnp.where(row >= TILES // 16, 2 * HALF, 0)
    return pl.multiple_of((2 * step + base + 1) * HALF + row * TILE - late, TILE)


def gather_kernel(info_ref, index_ref, tile_a, tile_b, features, far, *refs):
    payloads, (out_ref, held, total, sem) = refs[:STEPS], refs[STEPS:]
    pieces = [(features, HALF, 0), (far, HALF, 17), (far, 0, 18)]
    for j, payload in enumerate(payloads):
        pieces += [(payload, 0, j + 1), (payload, HALF, j + 9)]
    copies = [
        pltpu.make_async_copy(ref.at[pl.ds(at, HALF)], held.at[pl.ds(slot * HALF, HALF)], sem.at[k])
        for k, (ref, at, slot) in enumerate(pieces)
    ]
    for copy in copies:
        copy.start()
    total[...] = jnp.zeros_like(total)
    for copy in copies:
        copy.wait()
    base = info_ref[1]
    for slot in range(TILES):
        tile = (tile_a if slot < TILES // 2 else tile_b)[slot % (TILES // 2)]
        source = held_row(base, index_ref, slot)
        target = pl.multiple_of(index_ref[1, slot] * TILE, TILE)
        total[pl.ds(target, TILE), :] += jnp.dot(
            tile, held[pl.ds(source, TILE), :], preferred_element_type=jnp.float32
        )
    out_ref[...] = total[...].astype(jnp.bfloat16)


def gather_tiles(info, index, tiles, features, far, payloads):
    return pl.pallas_call(
        gather_kernel,
        in_specs=[smem, smem, vmem, vmem] + [anywhere] * (2 + STEPS),
        out_specs=vmem,
        out_shape=jax.ShapeDtypeStruct((ROWS, FEAT), jnp.bfloat16),
        scratch_shapes=[
            pltpu.VMEM((SLOTS * HALF, FEAT), jnp.bfloat16),
            pltpu.VMEM((ROWS, FEAT), jnp.float32),
            pltpu.SemaphoreType.DMA((SLOTS,)),
        ],
        compiler_params=params(),
        cost_estimate=cost(10**9, 4 * 2**20),
        name="gather_tiles",
    )(info, index, *tiles, features, far, *payloads)


def layer_kernel(
    info_ref, mine_ref, other_ref, deg_mine, deg_other, feat_ref, w_self, w_neigh, bias,
    joined_pos, joined_neg,
    emb_ref, d_self_ref, d_mean_ref, d_weight_ref,
    counts, hidden, scaled, mean, inverse, grad, bias_sum, sem,
):
    copies = [
        pltpu.make_async_copy(ref, counts.at[k], sem.at[k])
        for k, ref in enumerate((joined_pos, joined_neg))
    ]
    for copy in copies:
        copy.start()
    factor = -math.log2(math.e) / math.sqrt(HID)

    def divisor_of(i):
        rows = []
        for k in range(i * PANEL // TILE, (i + 1) * PANEL // TILE):
            row = deg_mine[pl.ds(k, 1), :] + deg_other[pl.ds(k, 1), :]
            rows.append(jnp.broadcast_to(jnp.maximum(row, 1.0), (TILE, TILE)).T)
        return jnp.concatenate(rows, axis=0)

    for i in range(ROWS // PANEL):
        at = pl.ds(i * PANEL, PANEL)
        total = mine_ref[at, :].astype(jnp.float32) + other_ref[at, :].astype(jnp.float32)
        low = (total / divisor_of(i)).astype(jnp.bfloat16)
        mean[at, :] = low
        preact = (
            jnp.dot(feat_ref[at, :], w_self[...], preferred_element_type=jnp.float32)
            + jnp.dot(low, w_neigh[...], preferred_element_type=jnp.float32)
            + bias[...]
        )
        inv = lax.rsqrt(jnp.mean(preact * preact, axis=1, keepdims=True) + norm_eps)
        hid = preact * inv
        hidden[at, :] = hid
        inverse[at, :] = inv
        emb_ref[at, :] = hid.astype(jnp.bfloat16)
        scaled[at, :] = (hid * factor).astype(jnp.bfloat16)

    for copy in copies:
        copy.wait()
    bias_sum[...] = jnp.zeros_like(bias_sum)
    diagonal = lax.broadcasted_iota(jnp.int32, (PANEL, PANEL), 0) == lax.broadcasted_iota(
        jnp.int32, (PANEL, PANEL), 1
    )
    for i in range(ROWS // PANEL):
        at = pl.ds(i * PANEL, PANEL)
        d_hidden = jnp.zeros((PANEL, HID), jnp.float32)
        for j in range(ROWS // PANEL):
            to = pl.ds(j * PANEL, PANEL)
            power = lax.dot_general(
                scaled[at, :], emb_ref[to, :], across, preferred_element_type=jnp.float32
            )
            grown = jnp.exp2(power)
            coef = (counts[1, at, to] - counts[0, at, to] * grown) * pl.reciprocal(
                1.0 + grown, approx=True
            )
            if i == j:
                own = jnp.where(diagonal, coef, 0.0)
                coef = coef - own
                d_hidden += jnp.sum(own, axis=1, keepdims=True) * hidden[at, :]
            d_hidden += jnp.dot(
                coef.astype(jnp.bfloat16), emb_ref[to, :], preferred_element_type=jnp.float32
            )
        d_hidden *= 1.0 / math.sqrt(HID)
        hid = hidden[at, :]
        d_preact = inverse[at, :] * (
            d_hidden - hid * jnp.mean(d_hidden * hid, axis=1, keepdims=True)
        )
        bias_sum[...] += jnp.sum(d_preact.reshape(PANEL // 8, 8, HID), axis=0)
        low = d_preact.astype(jnp.bfloat16)
        grad[at, :] = low
        d_self_ref[at, :] = lax.dot_general(
            low, w_self[...], across, preferred_element_type=jnp.float32
        )
        d_mean_ref[at, :] = (
            lax.dot_general(low, w_neigh[...], across, preferred_element_type=jnp.float32)
            / divisor_of(i)
        ).astype(jnp.bfloat16)
    chosen = jnp.where(
        info_ref[0] == 0, feat_ref[...].astype(jnp.float32), mean[...].astype(jnp.float32)
    )
    d_weight_ref[0:FEAT, :] = lax.dot_general(
        chosen.astype(jnp.bfloat16), grad[...], down, preferred_element_type=jnp.float32
    )
    d_weight_ref[FEAT : FEAT + 8, :] = jnp.broadcast_to(
        jnp.sum(bias_sum[...], axis=0, keepdims=True), (8, HID)
    )
    d_weight_ref[FEAT + 8 :, :] = jnp.zeros((WROWS - FEAT - 8, HID), jnp.float32)


def layer(info, mine, other, deg_mine, deg_other, features, w_self, w_neigh, bias, joined):
    shapes = [
        jax.ShapeDtypeStruct((ROWS, HID), jnp.bfloat16),
        jax.ShapeDtypeStruct((ROWS, FEAT), jnp.float32),
        jax.ShapeDtypeStruct((ROWS, FEAT), jnp.bfloat16),
        jax.ShapeDtypeStruct((WROWS, HID), jnp.float32),
    ]
    return pl.pallas_call(
        layer_kernel,
        in_specs=[smem] + [vmem] * 8 + [anywhere] * 2,
        out_specs=[vmem] * 4,
        out_shape=shapes,
        scratch_shapes=[
            pltpu.VMEM((2, ROWS, ROWS), jnp.float32),
            pltpu.VMEM((ROWS, HID), jnp.float32),
            pltpu.VMEM((ROWS, HID), jnp.bfloat16),
            pltpu.VMEM((ROWS, FEAT), jnp.bfloat16),
            pltpu.VMEM((ROWS, 1), jnp.float32),
            pltpu.VMEM((ROWS, HID), jnp.bfloat16),
            pltpu.VMEM((8, HID), jnp.float32),
            pltpu.SemaphoreType.DMA((2,)),
        ],
        compiler_params=params(),
        cost_estimate=cost(2 * 10**9, 12 * 2**20),
        name="layer",
    )(info, mine, other, deg_mine, deg_other, features, w_self, w_neigh, bias, *joined)


def spread_kernel(info_ref, index_ref, turned_a, turned_b, grad_ref, *refs):
    outs, (own_ref, side_ref, far_ref, total) = refs[: STEPS - 1], refs[STEPS - 1 :]
    total[...] = jnp.zeros_like(total)
    base = info_ref[1]
    for slot in range(TILES):
        tile = (turned_a if slot < TILES // 2 else turned_b)[slot % (TILES // 2)]
        target = held_row(base, index_ref, slot)
        source = pl.multiple_of(index_ref[1, slot] * TILE, TILE)
        total[pl.ds(target, TILE), :] += jnp.dot(
            tile, grad_ref[pl.ds(source, TILE), :], preferred_element_type=jnp.float32
        )
    for k, out in enumerate(outs):
        out[:HALF, :] = total[pl.ds((k + 2) * HALF, HALF), :].astype(jnp.bfloat16)
        out[HALF:, :] = total[pl.ds((k + 10) * HALF, HALF), :].astype(jnp.bfloat16)
    own_ref[:HALF, :] = total[HALF : 2 * HALF, :]
    own_ref[HALF:, :] = total[9 * HALF : 10 * HALF, :]
    side = pl.multiple_of(jnp.where(info_ref[0] == 0, 0, 18 * HALF), HALF)
    side_ref[...] = total[pl.ds(side, HALF), :].astype(jnp.bfloat16)
    far_ref[...] = total[17 * HALF : 18 * HALF, :].astype(jnp.bfloat16)


def spread_tiles(info, index, turned, d_mean):
    half = jax.ShapeDtypeStruct((HALF, FEAT), jnp.bfloat16)
    shapes = [jax.ShapeDtypeStruct((ROWS, FEAT), jnp.bfloat16)] * (STEPS - 1)
    shapes += [jax.ShapeDtypeStruct((ROWS, FEAT), jnp.float32), half, half]
    return pl.pallas_call(
        spread_kernel,
        in_specs=[smem, smem, vmem, vmem, vmem],
        out_specs=[vmem] * len(shapes),
        out_shape=shapes,
        scratch_shapes=[pltpu.VMEM((SLOTS * HALF, FEAT), jnp.float32)],
        compiler_params=params(),
        cost_estimate=cost(10**9, 4 * 2**20),
        name="spread_tiles",
    )(info, index, *turned, d_mean)


def flipped(value, mask):
    return shifted(value, lambda block, rep: (block ^ mask, rep))


def added(left, right):
    return (left.astype(jnp.float32) + right.astype(jnp.float32)).astype(jnp.bfloat16)


def body(features, tile_index, tile_counts, w_self, w_neigh, bias, pos_pairs, neg_pairs):
    block, rep = lax.axis_index("blk"), lax.axis_index("rep")
    core = block & 1
    index, counts = tile_index[0, 0], tile_counts[0, 0]
    base = jnp.where(rep == 0, 0, jnp.where(core == 1, 1, 3))
    info = jnp.stack([rep, base]).astype(jnp.int32)
    half = features.shape[0] // 2

    pos_turned, neg_turned = pos_pairs.T, neg_pairs.T
    given = lax.dynamic_slice_in_dim(features, rep * half, half, 0)
    here, before = owned(given, 0), owned(given, -8)
    tiles_a, turned_a, degree = prepare_tiles(index, jnp.zeros((8, TILE), jnp.float32), counts, 0, 2)
    before, degree = tied((before, degree), turned_a)
    first = jnp.concatenate([here, before], axis=0)
    pay = {0: first, 1: along(first, -1), 7: along(first, -7)}
    tiles_b, turned_b, degree = prepare_tiles(index, degree, counts, 1, 2)
    pay[1], pay[7], degree = tied((pay[1], pay[7], degree), turned_b)
    pay[2], pay[6] = along(pay[1], -1), along(pay[7], 1)
    (pos_turned,) = tied((pos_turned,), pay[1])
    joined_pos = join_pairs(pos_turned)
    pay[2], pay[6] = tied((pay[2], pay[6]), joined_pos)
    pay[3], pay[5] = along(pay[2], -1), along(pay[6], 1)
    (neg_turned,) = tied((neg_turned,), pay[2])
    joined_neg = join_pairs(neg_turned)
    pay[3], pay[5] = tied((pay[3], pay[5]), joined_neg)
    pay[4] = along(pay[3], -1)
    spare, degree = tied((features, degree), pay[3])
    degree_other = shifted(degree, lambda b, r: (b, 1 - r))
    far = shifted(spare, lambda b, r: ((b & ~1) - 15, 1) if is_late(b, r) else None)
    payloads = [pay[j] for j in range(STEPS)]
    mine = gather_tiles(info, index, (tiles_a, tiles_b), features, far, payloads)
    other = shifted(mine, lambda b, r: (b, 1 - r))

    embeddings, d_self, d_mean, d_weight = layer(
        info, mine, other, degree, degree_other,
        features, w_self, w_neigh, bias.reshape(1, HID), (joined_pos, joined_neg),
    )

    rows = d_weight.shape[0] // 2
    kept = lax.dynamic_slice_in_dim(d_weight, core * rows, rows, 0)
    sent = lax.dynamic_slice_in_dim(d_weight, (1 - core) * rows, rows, 0)
    sent = flipped(sent, 1)
    *spread, own, side, late = spread_tiles(info, index, (turned_a, turned_b), d_mean)
    part = dict(enumerate(spread, 1))

    up, down = along(part[4], 1), along(part[5], -1)
    kept, sent = tied((kept, sent), own)
    summed = kept + sent
    given = flipped(summed, 32)
    up, down = tied((up, down), summed)
    up, down = added(up, part[3]), added(down, part[6])

    given, side = tied((given, side), up)
    up, down = along(up, 1), along(down, -1)
    summed = summed + given
    given = flipped(summed, 64)
    side = shifted(
        side,
        lambda b, r: device(spot(b, r)[0], spot(b, r)[1] - 1)
        if r == 1
        else (device(1, spot(b, r)[1] + 17) if b & 1 else None),
    )
    up, down = tied((up, down), summed)
    up, down = added(up, part[2]), added(down, part[7])

    given, late = tied((given, late), up)
    up, down = along(up, 1), along(down, 7)
    summed = summed + given
    given = flipped(summed, 8)
    late = shifted(late, lambda b, r: device(1, spot(b, r)[1] + 16) if is_late(b, r) else None)
    up, down = tied((up, down), summed)
    up = added(up, part[1])

    given, side = tied((given, side), up)
    up = along(up, 1)
    summed = summed + given
    given = flipped(summed, 16)
    own = own + down.astype(jnp.float32)
    up, own = tied((up, own), summed)
    own = own + up.astype(jnp.float32)
    back = own[half:].astype(jnp.bfloat16)

    (given,) = tied((given,), back)
    back = along(back, 8)
    summed = summed + given
    given = [flipped(summed, k << 1) for k in range(1, 4)]
    (back,) = tied((back,), summed)
    landed = (
        (own[:half] + back.astype(jnp.float32)) + (side.astype(jnp.float32) + late.astype(jnp.float32))
    ).astype(jnp.bfloat16)

    given = tied(given, landed)
    crossed = shifted(landed, lambda b, r: (b, 0) if r else (b ^ 1, 1))
    swapped = shifted(landed, lambda b, r: (b ^ r, r))
    summed = (summed + given[0]) + (given[1] + given[2])
    traded = flipped(summed, 1)
    there = shifted(summed, lambda b, r: (b, 1 - r))
    aside = shifted(summed, lambda b, r: (b ^ 1, 1 - r))
    crossed, swapped = tied((crossed, swapped), summed)
    lower = jnp.where(rep == 0, swapped, crossed)
    upper = jnp.where(rep == 0, crossed, swapped)
    d_features = d_self + jnp.concatenate([lower, upper], axis=0).astype(jnp.float32)

    def whole(mine, others):
        return jnp.concatenate(
            [jnp.where(core == 0, mine, others), jnp.where(core == 0, others, mine)], axis=0
        )

    d_here, d_there = whole(summed, traded), whole(there, aside)
    d_w_self = jnp.where(rep == 0, d_here, d_there)[:FEAT]
    d_w_neigh = jnp.where(rep == 0, d_there, d_here)[:FEAT]
    return (embeddings, d_features, d_w_self, d_w_neigh, d_here[FEAT])


def solution(mesh):
    return jax.shard_map(
        body,
        mesh=mesh,
        in_specs=(
            P("blk", None),
            P("blk", "rep", None, None),
            P("blk", "rep", None, None, None),
            P(),
            P(),
            P(),
            P("blk", None),
            P("blk", None),
        ),
        out_specs=(P("blk", None), P("blk", None), P(), P(), P()),
        check_vma=False,
    )
```

```python
import math

import jax
import jax.numpy as jnp
from jax import lax
from jax.experimental import pallas as pl
from jax.experimental.pallas import tpu as pltpu
from jax.sharding import PartitionSpec as P

STEPS = 8
TILE = 128
ROWS = 1024
FEAT = 128
HID = 256
TILES = 64
BLOCKS = 128
REPS = 2
GROUP = 8
NEAR = STEPS // 2
WROWS = 144
PANEL = 256
norm_eps = 1e-05
VMEM_LIMIT = 56 * 1024 * 1024
across = (((1,), (1,)), ((), ()))
down = (((0,), (0,)), ((), ()))

vmem = pl.BlockSpec(memory_space=pltpu.VMEM)
smem = pl.BlockSpec(memory_space=pltpu.SMEM)
anywhere = pl.BlockSpec(memory_space=pl.ANY)


def params():
    return pltpu.CompilerParams(vmem_limit_bytes=VMEM_LIMIT)


def cost(flops, bytes_accessed):
    return pl.CostEstimate(flops=flops, bytes_accessed=bytes_accessed, transcendentals=0)


def shifted(value, source_of):
    route = []
    for block in range(BLOCKS):
        for rep in range(REPS):
            source = source_of(block, rep)
            if source is not None:
                route.append(((source[0] % BLOCKS) * REPS + source[1], block * REPS + rep))
    return lax.ppermute(value, ("blk", "rep"), route)


def from_step(value, step):
    return shifted(value, lambda block, rep: (block - rep - 2 * step, rep))


def to_step(value, step):
    return shifted(value, lambda block, rep: (block + rep + 2 * step, rep))


def from_before(value):
    return shifted(value, lambda block, rep: (block - STEPS, rep))


def to_before(value):
    return shifted(value, lambda block, rep: (block + STEPS, rep))


def tied(values, *others):
    flat = lax.optimization_barrier(tuple(values) + tuple(others))
    return flat[: len(values)]


def tiles_kernel(first, index_ref, before_ref, counts_ref, tile_ref, turned_ref, degree_ref, sums):
    group = pl.program_id(0)

    @pl.when(group == 0)
    def _():
        sums[...] = jnp.zeros_like(sums)

    ones = jnp.ones((8, TILE), jnp.bfloat16)
    for k in range(GROUP):
        slot = first + group * GROUP + k
        used = index_ref[0, slot] < STEPS
        counts = jnp.where(used, counts_ref[k], 0).astype(jnp.float32)
        turned = counts.T.astype(jnp.bfloat16)
        tile_ref[k] = counts.astype(jnp.bfloat16)
        turned_ref[k] = turned
        row = index_ref[1, slot]
        sums[row] += jnp.dot(ones, turned, preferred_element_type=jnp.float32)

    @pl.when(group == pl.num_programs(0) - 1)
    def _():
        degree_ref[...] = before_ref[...] + sums[:, 0, :]


def prepare_tiles(index, before, counts, part, parts):
    share = TILES // parts
    spec = pl.BlockSpec((GROUP, TILE, TILE), lambda g: (g, 0, 0))
    shape = jax.ShapeDtypeStruct((share, TILE, TILE), jnp.bfloat16)
    whole = pl.BlockSpec((8, TILE), lambda g: (0, 0))
    return pl.pallas_call(
        lambda *refs: tiles_kernel(part * share, *refs),
        grid=(share // GROUP,),
        in_specs=[
            smem,
            whole,
            pl.BlockSpec((GROUP, TILE, TILE), lambda g: (g + part * share // GROUP, 0, 0)),
        ],
        out_specs=[spec, spec, whole],
        out_shape=[shape, shape, jax.ShapeDtypeStruct((8, TILE), jnp.float32)],
        scratch_shapes=[pltpu.VMEM((8, 8, TILE), jnp.float32)],
        compiler_params=params(),
        cost_estimate=cost(10**9, 8 * 2**20),
        name="prepare_tiles",
    )(index, before, counts)


def pairs_kernel(turned, joined_ref, left, right):
    def fill(i, carry):
        at = pl.ds(pl.multiple_of(i * TILE, TILE), TILE)
        rows = lax.broadcasted_iota(jnp.int32, (TILE, ROWS), 0) + i * TILE
        left[at, :] = (turned[0:1, :] == rows).astype(jnp.float32).astype(left.dtype)
        right[at, :] = (turned[1:2, :] == rows).astype(jnp.float32).astype(right.dtype)
        return carry

    lax.fori_loop(0, ROWS // TILE, fill, 0)
    for i in range(ROWS // PANEL):
        at = pl.ds(i * PANEL, PANEL)
        joined_ref[at, :] = lax.dot_general(
            left[at, :], right[...], across, preferred_element_type=jnp.float32
        )
    for i in range(ROWS // TILE):
        for j in range(i, ROWS // TILE):
            over = (pl.ds(i * TILE, TILE), pl.ds(j * TILE, TILE))
            under = (pl.ds(j * TILE, TILE), pl.ds(i * TILE, TILE))
            both = joined_ref[over] + joined_ref[under].T
            joined_ref[over] = both
            if i != j:
                joined_ref[under] = both.T


def join_pairs(turned):
    return pl.pallas_call(
        pairs_kernel,
        in_specs=[vmem],
        out_specs=vmem,
        out_shape=jax.ShapeDtypeStruct((ROWS, ROWS), jnp.float32),
        scratch_shapes=[pltpu.VMEM((ROWS, ROWS), jnp.float8_e4m3fn)] * 2,
        compiler_params=params(),
        cost_estimate=cost(3 * 10**9, 4 * 2**20),
        name="join_pairs",
    )(turned)


def held_row(index_ref, slot):
    step = jnp.minimum(index_ref[0, slot], STEPS - 1)
    return pl.multiple_of(step * ROWS + index_ref[2, slot] * TILE, TILE)


def gather_kernel(index_ref, tile_a, tile_b, *refs):
    blocks, (out_ref, held, total, sem) = refs[:STEPS], refs[STEPS:]
    copies = [
        pltpu.make_async_copy(block, held.at[pl.ds(k * ROWS, ROWS)], sem.at[k])
        for k, block in enumerate(blocks)
    ]
    for copy in copies:
        copy.start()
    total[...] = jnp.zeros_like(total)
    for copy in copies:
        copy.wait()
    for slot in range(TILES):
        tile = (tile_a if slot < TILES // 2 else tile_b)[slot % (TILES // 2)]
        source = held_row(index_ref, slot)
        target = pl.multiple_of(index_ref[1, slot] * TILE, TILE)
        total[pl.ds(target, TILE), :] += jnp.dot(
            tile, held[pl.ds(source, TILE), :], preferred_element_type=jnp.float32
        )
    out_ref[...] = total[...].astype(jnp.bfloat16)


def gather_tiles(index, tiles, blocks):
    return pl.pallas_call(
        gather_kernel,
        in_specs=[smem, vmem, vmem] + [anywhere] * STEPS,
        out_specs=vmem,
        out_shape=jax.ShapeDtypeStruct((ROWS, FEAT), jnp.bfloat16),
        scratch_shapes=[
            pltpu.VMEM((STEPS * ROWS, FEAT), jnp.bfloat16),
            pltpu.VMEM((ROWS, FEAT), jnp.float32),
            pltpu.SemaphoreType.DMA((STEPS,)),
        ],
        compiler_params=params(),
        cost_estimate=cost(10**9, 4 * 2**20),
        name="gather_tiles",
    )(index, *tiles, *blocks)


def layer_kernel(
    info_ref, mine_ref, other_ref, deg_mine, deg_other, feat_ref, w_self, w_neigh, bias,
    joined_pos, joined_neg,
    emb_ref, d_self_ref, d_mean_ref, d_weight_ref,
    counts, hidden, scaled, mean, inverse, grad, bias_sum, sem,
):
    copies = [
        pltpu.make_async_copy(ref, counts.at[k], sem.at[k])
        for k, ref in enumerate((joined_pos, joined_neg))
    ]
    for copy in copies:
        copy.start()
    factor = -math.log2(math.e) / math.sqrt(HID)

    def divisor_of(i):
        rows = []
        for k in range(i * PANEL // TILE, (i + 1) * PANEL // TILE):
            row = deg_mine[pl.ds(k, 1), :] + deg_other[pl.ds(k, 1), :]
            rows.append(jnp.broadcast_to(jnp.maximum(row, 1.0), (TILE, TILE)).T)
        return jnp.concatenate(rows, axis=0)

    for i in range(ROWS // PANEL):
        at = pl.ds(i * PANEL, PANEL)
        total = mine_ref[at, :].astype(jnp.float32) + other_ref[at, :].astype(jnp.float32)
        low = (total / divisor_of(i)).astype(jnp.bfloat16)
        mean[at, :] = low
        preact = (
            jnp.dot(feat_ref[at, :], w_self[...], preferred_element_type=jnp.float32)
            + jnp.dot(low, w_neigh[...], preferred_element_type=jnp.float32)
            + bias[...]
        )
        inv = lax.rsqrt(jnp.mean(preact * preact, axis=1, keepdims=True) + norm_eps)
        hid = preact * inv
        hidden[at, :] = hid
        inverse[at, :] = inv
        emb_ref[at, :] = hid.astype(jnp.bfloat16)
        scaled[at, :] = (hid * factor).astype(jnp.bfloat16)

    for copy in copies:
        copy.wait()
    bias_sum[...] = jnp.zeros_like(bias_sum)
    diagonal = lax.broadcasted_iota(jnp.int32, (PANEL, PANEL), 0) == lax.broadcasted_iota(
        jnp.int32, (PANEL, PANEL), 1
    )
    for i in range(ROWS // PANEL):
        at = pl.ds(i * PANEL, PANEL)
        d_hidden = jnp.zeros((PANEL, HID), jnp.float32)
        for j in range(ROWS // PANEL):
            to = pl.ds(j * PANEL, PANEL)
            power = lax.dot_general(
                scaled[at, :], emb_ref[to, :], across, preferred_element_type=jnp.float32
            )
            grown = jnp.exp2(power)
            coef = (counts[1, at, to] - counts[0, at, to] * grown) * pl.reciprocal(
                1.0 + grown, approx=True
            )
            if i == j:
                own = jnp.where(diagonal, coef, 0.0)
                coef = coef - own
                d_hidden += jnp.sum(own, axis=1, keepdims=True) * hidden[at, :]
            d_hidden += jnp.dot(
                coef.astype(jnp.bfloat16), emb_ref[to, :], preferred_element_type=jnp.float32
            )
        d_hidden *= 1.0 / math.sqrt(HID)
        hid = hidden[at, :]
        d_preact = inverse[at, :] * (
            d_hidden - hid * jnp.mean(d_hidden * hid, axis=1, keepdims=True)
        )
        bias_sum[...] += jnp.sum(d_preact.reshape(PANEL // 8, 8, HID), axis=0)
        low = d_preact.astype(jnp.bfloat16)
        grad[at, :] = low
        d_self_ref[at, :] = lax.dot_general(
            low, w_self[...], across, preferred_element_type=jnp.float32
        )
        d_mean_ref[at, :] = (
            lax.dot_general(low, w_neigh[...], across, preferred_element_type=jnp.float32)
            / divisor_of(i)
        ).astype(jnp.bfloat16)
    chosen = jnp.where(
        info_ref[0] == 0, feat_ref[...].astype(jnp.float32), mean[...].astype(jnp.float32)
    )
    d_weight_ref[0:FEAT, :] = lax.dot_general(
        chosen.astype(jnp.bfloat16), grad[...], down, preferred_element_type=jnp.float32
    )
    d_weight_ref[FEAT : FEAT + 8, :] = jnp.broadcast_to(
        jnp.sum(bias_sum[...], axis=0, keepdims=True), (8, HID)
    )
    d_weight_ref[FEAT + 8 :, :] = jnp.zeros((WROWS - FEAT - 8, HID), jnp.float32)


def layer(info, mine, other, deg_mine, deg_other, features, w_self, w_neigh, bias, joined):
    shapes = [
        jax.ShapeDtypeStruct((ROWS, HID), jnp.bfloat16),
        jax.ShapeDtypeStruct((ROWS, FEAT), jnp.float32),
        jax.ShapeDtypeStruct((ROWS, FEAT), jnp.bfloat16),
        jax.ShapeDtypeStruct((WROWS, HID), jnp.float32),
    ]
    return pl.pallas_call(
        layer_kernel,
        in_specs=[smem] + [vmem] * 8 + [anywhere] * 2,
        out_specs=[vmem] * 4,
        out_shape=shapes,
        scratch_shapes=[
            pltpu.VMEM((2, ROWS, ROWS), jnp.float32),
            pltpu.VMEM((ROWS, HID), jnp.float32),
            pltpu.VMEM((ROWS, HID), jnp.bfloat16),
            pltpu.VMEM((ROWS, FEAT), jnp.bfloat16),
            pltpu.VMEM((ROWS, 1), jnp.float32),
            pltpu.VMEM((ROWS, HID), jnp.bfloat16),
            pltpu.VMEM((8, HID), jnp.float32),
            pltpu.SemaphoreType.DMA((2,)),
        ],
        compiler_params=params(),
        cost_estimate=cost(2 * 10**9, 12 * 2**20),
        name="layer",
    )(info, mine, other, deg_mine, deg_other, features, w_self, w_neigh, bias, *joined)


def spread_kernel(index_ref, turned_a, turned_b, grad_ref, *refs):
    outs, (total,) = refs[:STEPS], refs[STEPS:]
    total[...] = jnp.zeros_like(total)
    for slot in range(TILES):
        tile = (turned_a if slot < TILES // 2 else turned_b)[slot % (TILES // 2)]
        target = held_row(index_ref, slot)
        source = pl.multiple_of(index_ref[1, slot] * TILE, TILE)
        total[pl.ds(target, TILE), :] += jnp.dot(
            tile, grad_ref[pl.ds(source, TILE), :], preferred_element_type=jnp.float32
        )
    for k, out in enumerate(outs):
        out[...] = total[k * ROWS : (k + 1) * ROWS, :].astype(jnp.bfloat16)


def spread_tiles(index, turned, d_mean):
    return pl.pallas_call(
        spread_kernel,
        in_specs=[smem, vmem, vmem, vmem],
        out_specs=[vmem] * STEPS,
        out_shape=[jax.ShapeDtypeStruct((ROWS, FEAT), jnp.bfloat16)] * STEPS,
        scratch_shapes=[pltpu.VMEM((STEPS * ROWS, FEAT), jnp.float32)],
        compiler_params=params(),
        cost_estimate=cost(10**9, 4 * 2**20),
        name="spread_tiles",
    )(index, *turned, d_mean)


def flipped(value, mask):
    return shifted(value, lambda block, rep: (block ^ mask, rep))


def added(left, right):
    return (left.astype(jnp.float32) + right.astype(jnp.float32)).astype(jnp.bfloat16)


def body(features, tile_index, tile_counts, w_self, w_neigh, bias, pos_pairs, neg_pairs):
    block, rep = lax.axis_index("blk"), lax.axis_index("rep")
    core = block & 1
    index, counts = tile_index[0, 0], tile_counts[0, 0]
    info = rep.reshape(1).astype(jnp.int32)
    pos_turned, neg_turned = pos_pairs.T, neg_pairs.T

    held = {s: from_step(features, s) for s in (4, 1, 3, 2, 0)}
    tiles_a, turned_a, degree = prepare_tiles(index, jnp.zeros((8, TILE), jnp.float32), counts, 0, 2)
    tiles_b, turned_b, degree = prepare_tiles(index, degree, counts, 1, 2)
    held[1], degree = tied((held[1], degree), turned_b)
    held[5] = from_before(held[1])
    degree_other = shifted(degree, lambda b, r: (b, 1 - r))
    (pos_turned,) = tied((pos_turned,), held[1])
    joined_pos = join_pairs(pos_turned)
    (held[3],) = tied((held[3],), joined_pos)
    held[7] = from_before(held[3])
    (neg_turned,) = tied((neg_turned,), held[3], held[5], degree_other)
    joined_neg = join_pairs(neg_turned)
    (held[2],) = tied((held[2],), joined_neg)
    held[6] = from_before(held[2])
    mine = gather_tiles(index, (tiles_a, tiles_b), [held[s] for s in range(STEPS)])
    other = shifted(mine, lambda b, r: (b, 1 - r))

    embeddings, d_self, d_mean, d_weight = layer(
        info, mine, other, degree, degree_other,
        features, w_self, w_neigh, bias.reshape(1, HID), (joined_pos, joined_neg),
    )

    rows = d_weight.shape[0] // 2
    kept = lax.dynamic_slice_in_dim(d_weight, core * rows, rows, 0)
    given = lax.dynamic_slice_in_dim(d_weight, (1 - core) * rows, rows, 0)
    given = flipped(given, 1)
    spread = spread_tiles(index, (turned_a, turned_b), d_mean)
    order = (2, 1, 3, 0)
    back = {s: to_before(spread[s + NEAR]) for s in order}
    kept, given = tied((kept, given), spread[0])
    summed = kept + given
    near = {2: added(spread[2], back[2])}
    landed = {2: to_step(near[2], 2)}
    (summed,) = tied((summed,), near[2])
    given = [flipped(summed, k << 5) for k in range(1, 4)]
    summed = (summed + given[0]) + (given[1] + given[2])
    after = near[2]
    for s in (1, 3, 0):
        if s == 0:
            after = landed[2]
        (back[s],) = tied((back[s],), after)
        after = near[s] = added(spread[s], back[s])
        landed[s] = to_step(near[s], s)
    summed, landed[2] = tied((summed, landed[2]), near[0])
    (summed,) = tied((summed,), landed[2])
    given = [flipped(summed, k << 3) for k in range(1, 4)]
    summed = (summed + given[0]) + (given[1] + given[2])
    arrived = tied([landed[s] for s in range(NEAR)], summed)
    arrived = [value.astype(jnp.float32) for value in arrived]
    partial = ((arrived[0] + arrived[1]) + (arrived[2] + arrived[3])).astype(jnp.bfloat16)
    partial_other = shifted(partial, lambda b, r: (b, 1 - r))
    (summed,) = tied((summed,), partial)
    given = [flipped(summed, k << 1) for k in range(1, 4)]
    summed = (summed + given[0]) + (given[1] + given[2])
    traded = flipped(summed, 1)
    there = shifted(summed, lambda b, r: (b, 1 - r))
    aside = shifted(summed, lambda b, r: (b ^ 1, 1 - r))
    d_features = d_self + (partial.astype(jnp.float32) + partial_other.astype(jnp.float32))

    def whole(mine, others):
        return jnp.concatenate(
            [jnp.where(core == 0, mine, others), jnp.where(core == 0, others, mine)], axis=0
        )

    d_here, d_there = whole(summed, traded), whole(there, aside)
    d_w_self = jnp.where(rep == 0, d_here, d_there)[:FEAT]
    d_w_neigh = jnp.where(rep == 0, d_there, d_here)[:FEAT]
    return (embeddings, d_features, d_w_self, d_w_neigh, d_here[FEAT])


def solution(mesh):
    return jax.shard_map(
        body,
        mesh=mesh,
        in_specs=(
            P("blk", None),
            P("blk", "rep", None, None),
            P("blk", "rep", None, None, None),
            P(),
            P(),
            P(),
            P("blk", None),
            P("blk", None),
        ),
        out_specs=(P("blk", None), P("blk", None), P(), P(), P()),
        check_vma=False,
    )
```

```python
import math

import jax
import jax.numpy as jnp
from jax import lax
from jax.experimental import pallas as pl
from jax.experimental.pallas import tpu as pltpu
from jax.sharding import PartitionSpec as P

STEPS = 8
TILE = 128
ROWS = 1024
FEAT = 128
HID = 256
TILES = 64
BLOCKS = 128
REPS = 2
GROUP = 8
NEAR = STEPS // 2
WROWS = 144
PANEL = 256
norm_eps = 1e-05
VMEM_LIMIT = 56 * 1024 * 1024
across = (((1,), (1,)), ((), ()))
down = (((0,), (0,)), ((), ()))

vmem = pl.BlockSpec(memory_space=pltpu.VMEM)
smem = pl.BlockSpec(memory_space=pltpu.SMEM)
anywhere = pl.BlockSpec(memory_space=pl.ANY)


def params():
    return pltpu.CompilerParams(vmem_limit_bytes=VMEM_LIMIT)


def cost(flops, bytes_accessed):
    return pl.CostEstimate(flops=flops, bytes_accessed=bytes_accessed, transcendentals=0)


def shifted(value, source_of):
    route = []
    for block in range(BLOCKS):
        for rep in range(REPS):
            source = source_of(block, rep)
            if source is not None:
                route.append(((source[0] % BLOCKS) * REPS + source[1], block * REPS + rep))
    return lax.ppermute(value, ("blk", "rep"), route)


def from_step(value, step):
    return shifted(value, lambda block, rep: (block - rep - 2 * step, rep))


def to_step(value, step):
    return shifted(value, lambda block, rep: (block + rep + 2 * step, rep))


def from_before(value):
    return shifted(value, lambda block, rep: (block - STEPS, rep))


def to_before(value):
    return shifted(value, lambda block, rep: (block + STEPS, rep))


def tied(values, *others):
    flat = lax.optimization_barrier(tuple(values) + tuple(others))
    return flat[: len(values)]


def tiles_kernel(first, index_ref, before_ref, counts_ref, tile_ref, turned_ref, degree_ref, sums):
    group = pl.program_id(0)

    @pl.when(group == 0)
    def _():
        sums[...] = jnp.zeros_like(sums)

    ones = jnp.ones((8, TILE), jnp.bfloat16)
    for k in range(GROUP):
        slot = first + group * GROUP + k
        used = index_ref[0, slot] < STEPS
        counts = jnp.where(used, counts_ref[k], 0).astype(jnp.float32)
        turned = counts.T.astype(jnp.bfloat16)
        tile_ref[k] = counts.astype(jnp.bfloat16)
        turned_ref[k] = turned
        row = index_ref[1, slot]
        sums[row] += jnp.dot(ones, turned, preferred_element_type=jnp.float32)

    @pl.when(group == pl.num_programs(0) - 1)
    def _():
        degree_ref[...] = before_ref[...] + sums[:, 0, :]


def prepare_tiles(index, before, counts, part, parts):
    share = TILES // parts
    spec = pl.BlockSpec((GROUP, TILE, TILE), lambda g: (g, 0, 0))
    shape = jax.ShapeDtypeStruct((share, TILE, TILE), jnp.bfloat16)
    whole = pl.BlockSpec((8, TILE), lambda g: (0, 0))
    return pl.pallas_call(
        lambda *refs: tiles_kernel(part * share, *refs),
        grid=(share // GROUP,),
        in_specs=[
            smem,
            whole,
            pl.BlockSpec((GROUP, TILE, TILE), lambda g: (g + part * share // GROUP, 0, 0)),
        ],
        out_specs=[spec, spec, whole],
        out_shape=[shape, shape, jax.ShapeDtypeStruct((8, TILE), jnp.float32)],
        scratch_shapes=[pltpu.VMEM((8, 8, TILE), jnp.float32)],
        compiler_params=params(),
        cost_estimate=cost(10**9, 8 * 2**20),
        name="prepare_tiles",
    )(index, before, counts)


def pairs_kernel(turned, joined_ref, left, right):
    def fill(i, carry):
        at = pl.ds(pl.multiple_of(i * TILE, TILE), TILE)
        rows = lax.broadcasted_iota(jnp.int32, (TILE, ROWS), 0) + i * TILE
        left[at, :] = (turned[0:1, :] == rows).astype(jnp.float32).astype(left.dtype)
        right[at, :] = (turned[1:2, :] == rows).astype(jnp.float32).astype(right.dtype)
        return carry

    lax.fori_loop(0, ROWS // TILE, fill, 0)
    for i in range(ROWS // PANEL):
        at = pl.ds(i * PANEL, PANEL)
        joined_ref[at, :] = lax.dot_general(
            left[at, :], right[...], across, preferred_element_type=jnp.float32
        )
    for i in range(ROWS // TILE):
        for j in range(i, ROWS // TILE):
            over = (pl.ds(i * TILE, TILE), pl.ds(j * TILE, TILE))
            under = (pl.ds(j * TILE, TILE), pl.ds(i * TILE, TILE))
            both = joined_ref[over] + joined_ref[under].T
            joined_ref[over] = both
            if i != j:
                joined_ref[under] = both.T


def join_pairs(turned):
    return pl.pallas_call(
        pairs_kernel,
        in_specs=[vmem],
        out_specs=vmem,
        out_shape=jax.ShapeDtypeStruct((ROWS, ROWS), jnp.float32),
        scratch_shapes=[pltpu.VMEM((ROWS, ROWS), jnp.float8_e4m3fn)] * 2,
        compiler_params=params(),
        cost_estimate=cost(3 * 10**9, 4 * 2**20),
        name="join_pairs",
    )(turned)


def held_row(index_ref, slot):
    step = jnp.minimum(index_ref[0, slot], STEPS - 1)
    return pl.multiple_of(step * ROWS + index_ref[2, slot] * TILE, TILE)


def gather_kernel(index_ref, tile_a, tile_b, *refs):
    blocks, (out_ref, held, total, sem) = refs[:STEPS], refs[STEPS:]
    copies = [
        pltpu.make_async_copy(block, held.at[pl.ds(k * ROWS, ROWS)], sem.at[k])
        for k, block in enumerate(blocks)
    ]
    for copy in copies:
        copy.start()
    total[...] = jnp.zeros_like(total)
    for copy in copies:
        copy.wait()
    for slot in range(TILES):
        tile = (tile_a if slot < TILES // 2 else tile_b)[slot % (TILES // 2)]
        source = held_row(index_ref, slot)
        target = pl.multiple_of(index_ref[1, slot] * TILE, TILE)
        total[pl.ds(target, TILE), :] += jnp.dot(
            tile, held[pl.ds(source, TILE), :], preferred_element_type=jnp.float32
        )
    out_ref[...] = total[...].astype(jnp.bfloat16)


def gather_tiles(index, tiles, blocks):
    return pl.pallas_call(
        gather_kernel,
        in_specs=[smem, vmem, vmem] + [anywhere] * STEPS,
        out_specs=vmem,
        out_shape=jax.ShapeDtypeStruct((ROWS, FEAT), jnp.bfloat16),
        scratch_shapes=[
            pltpu.VMEM((STEPS * ROWS, FEAT), jnp.bfloat16),
            pltpu.VMEM((ROWS, FEAT), jnp.float32),
            pltpu.SemaphoreType.DMA((STEPS,)),
        ],
        compiler_params=params(),
        cost_estimate=cost(10**9, 4 * 2**20),
        name="gather_tiles",
    )(index, *tiles, *blocks)


def layer_kernel(
    info_ref, mine_ref, other_ref, deg_mine, deg_other, feat_ref, w_self, w_neigh, bias,
    joined_pos, joined_neg,
    emb_ref, d_self_ref, d_mean_ref, d_weight_ref,
    counts, hidden, scaled, mean, inverse, grad, bias_sum, sem,
):
    copies = [
        pltpu.make_async_copy(ref, counts.at[k], sem.at[k])
        for k, ref in enumerate((joined_pos, joined_neg))
    ]
    for copy in copies:
        copy.start()
    factor = -math.log2(math.e) / math.sqrt(HID)

    def divisor_of(i):
        rows = []
        for k in range(i * PANEL // TILE, (i + 1) * PANEL // TILE):
            row = deg_mine[pl.ds(k, 1), :] + deg_other[pl.ds(k, 1), :]
            rows.append(jnp.broadcast_to(jnp.maximum(row, 1.0), (TILE, TILE)).T)
        return jnp.concatenate(rows, axis=0)

    for i in range(ROWS // PANEL):
        at = pl.ds(i * PANEL, PANEL)
        total = mine_ref[at, :].astype(jnp.float32) + other_ref[at, :].astype(jnp.float32)
        low = (total / divisor_of(i)).astype(jnp.bfloat16)
        mean[at, :] = low
        preact = (
            jnp.dot(feat_ref[at, :], w_self[...], preferred_element_type=jnp.float32)
            + jnp.dot(low, w_neigh[...], preferred_element_type=jnp.float32)
            + bias[...]
        )
        inv = lax.rsqrt(jnp.mean(preact * preact, axis=1, keepdims=True) + norm_eps)
        hid = preact * inv
        hidden[at, :] = hid
        inverse[at, :] = inv
        emb_ref[at, :] = hid.astype(jnp.bfloat16)
        scaled[at, :] = (hid * factor).astype(jnp.bfloat16)

    for copy in copies:
        copy.wait()
    bias_sum[...] = jnp.zeros_like(bias_sum)
    diagonal = lax.broadcasted_iota(jnp.int32, (PANEL, PANEL), 0) == lax.broadcasted_iota(
        jnp.int32, (PANEL, PANEL), 1
    )
    for i in range(ROWS // PANEL):
        at = pl.ds(i * PANEL, PANEL)
        d_hidden = jnp.zeros((PANEL, HID), jnp.float32)
        for j in range(ROWS // PANEL):
            to = pl.ds(j * PANEL, PANEL)
            power = lax.dot_general(
                scaled[at, :], emb_ref[to, :], across, preferred_element_type=jnp.float32
            )
            grown = jnp.exp2(power)
            coef = (counts[1, at, to] - counts[0, at, to] * grown) * pl.reciprocal(
                1.0 + grown, approx=True
            )
            if i == j:
                own = jnp.where(diagonal, coef, 0.0)
                coef = coef - own
                d_hidden += jnp.sum(own, axis=1, keepdims=True) * hidden[at, :]
            d_hidden += jnp.dot(
                coef.astype(jnp.bfloat16), emb_ref[to, :], preferred_element_type=jnp.float32
            )
        d_hidden *= 1.0 / math.sqrt(HID)
        hid = hidden[at, :]
        d_preact = inverse[at, :] * (
            d_hidden - hid * jnp.mean(d_hidden * hid, axis=1, keepdims=True)
        )
        bias_sum[...] += jnp.sum(d_preact.reshape(PANEL // 8, 8, HID), axis=0)
        low = d_preact.astype(jnp.bfloat16)
        grad[at, :] = low
        d_self_ref[at, :] = lax.dot_general(
            low, w_self[...], across, preferred_element_type=jnp.float32
        )
        d_mean_ref[at, :] = (
            lax.dot_general(low, w_neigh[...], across, preferred_element_type=jnp.float32)
            / divisor_of(i)
        ).astype(jnp.bfloat16)
    chosen = jnp.where(
        info_ref[0] == 0, feat_ref[...].astype(jnp.float32), mean[...].astype(jnp.float32)
    )
    d_weight_ref[0:FEAT, :] = lax.dot_general(
        chosen.astype(jnp.bfloat16), grad[...], down, preferred_element_type=jnp.float32
    )
    d_weight_ref[FEAT : FEAT + 8, :] = jnp.broadcast_to(
        jnp.sum(bias_sum[...], axis=0, keepdims=True), (8, HID)
    )
    d_weight_ref[FEAT + 8 :, :] = jnp.zeros((WROWS - FEAT - 8, HID), jnp.float32)


def layer(info, mine, other, deg_mine, deg_other, features, w_self, w_neigh, bias, joined):
    shapes = [
        jax.ShapeDtypeStruct((ROWS, HID), jnp.bfloat16),
        jax.ShapeDtypeStruct((ROWS, FEAT), jnp.float32),
        jax.ShapeDtypeStruct((ROWS, FEAT), jnp.bfloat16),
        jax.ShapeDtypeStruct((WROWS, HID), jnp.float32),
    ]
    return pl.pallas_call(
        layer_kernel,
        in_specs=[smem] + [vmem] * 8 + [anywhere] * 2,
        out_specs=[vmem] * 4,
        out_shape=shapes,
        scratch_shapes=[
            pltpu.VMEM((2, ROWS, ROWS), jnp.float32),
            pltpu.VMEM((ROWS, HID), jnp.float32),
            pltpu.VMEM((ROWS, HID), jnp.bfloat16),
            pltpu.VMEM((ROWS, FEAT), jnp.bfloat16),
            pltpu.VMEM((ROWS, 1), jnp.float32),
            pltpu.VMEM((ROWS, HID), jnp.bfloat16),
            pltpu.VMEM((8, HID), jnp.float32),
            pltpu.SemaphoreType.DMA((2,)),
        ],
        compiler_params=params(),
        cost_estimate=cost(2 * 10**9, 12 * 2**20),
        name="layer",
    )(info, mine, other, deg_mine, deg_other, features, w_self, w_neigh, bias, *joined)


def spread_kernel(index_ref, turned_a, turned_b, grad_ref, *refs):
    outs, (total,) = refs[:STEPS], refs[STEPS:]
    total[...] = jnp.zeros_like(total)
    for slot in range(TILES):
        tile = (turned_a if slot < TILES // 2 else turned_b)[slot % (TILES // 2)]
        target = held_row(index_ref, slot)
        source = pl.multiple_of(index_ref[1, slot] * TILE, TILE)
        total[pl.ds(target, TILE), :] += jnp.dot(
            tile, grad_ref[pl.ds(source, TILE), :], preferred_element_type=jnp.float32
        )
    for k, out in enumerate(outs):
        out[...] = total[k * ROWS : (k + 1) * ROWS, :].astype(jnp.bfloat16)


def spread_tiles(index, turned, d_mean):
    return pl.pallas_call(
        spread_kernel,
        in_specs=[smem, vmem, vmem, vmem],
        out_specs=[vmem] * STEPS,
        out_shape=[jax.ShapeDtypeStruct((ROWS, FEAT), jnp.bfloat16)] * STEPS,
        scratch_shapes=[pltpu.VMEM((STEPS * ROWS, FEAT), jnp.float32)],
        compiler_params=params(),
        cost_estimate=cost(10**9, 4 * 2**20),
        name="spread_tiles",
    )(index, *turned, d_mean)


def flipped(value, mask):
    return shifted(value, lambda block, rep: (block ^ mask, rep))


def added(left, right):
    return (left.astype(jnp.float32) + right.astype(jnp.float32)).astype(jnp.bfloat16)


def body(features, tile_index, tile_counts, w_self, w_neigh, bias, pos_pairs, neg_pairs):
    block, rep = lax.axis_index("blk"), lax.axis_index("rep")
    core = block & 1
    index, counts = tile_index[0, 0], tile_counts[0, 0]
    info = rep.reshape(1).astype(jnp.int32)
    pos_turned, neg_turned = pos_pairs.T, neg_pairs.T

    held = {s: from_step(features, s) for s in (4, 1, 3, 2, 0)}
    tiles_a, turned_a, degree = prepare_tiles(index, jnp.zeros((8, TILE), jnp.float32), counts, 0, 2)
    tiles_b, turned_b, degree = prepare_tiles(index, degree, counts, 1, 2)
    held[1], degree = tied((held[1], degree), turned_b)
    held[5] = from_before(held[1])
    (pos_turned,) = tied((pos_turned,), held[1])
    joined_pos = join_pairs(pos_turned)
    held[3], degree = tied((held[3], degree), joined_pos, held[4])
    held[7] = from_before(held[3])
    (held[2],) = tied((held[2],), held[5], held[3])
    held[6] = from_before(held[2])
    degree_other = shifted(degree, lambda b, r: (b, 1 - r))
    mine = gather_tiles(index, (tiles_a, tiles_b), [held[s] for s in range(STEPS)])
    other = shifted(mine, lambda b, r: (b, 1 - r))
    (neg_turned,) = tied((neg_turned,), mine)
    joined_neg = join_pairs(neg_turned)

    embeddings, d_self, d_mean, d_weight = layer(
        info, mine, other, degree, degree_other,
        features, w_self, w_neigh, bias.reshape(1, HID), (joined_pos, joined_neg),
    )

    rows = d_weight.shape[0] // 2
    kept = lax.dynamic_slice_in_dim(d_weight, core * rows, rows, 0)
    given = lax.dynamic_slice_in_dim(d_weight, (1 - core) * rows, rows, 0)
    given = flipped(given, 1)
    spread = spread_tiles(index, (turned_a, turned_b), d_mean)
    order = (2, 1, 3, 0)
    back = {s: to_before(spread[s + NEAR]) for s in order}
    kept, given = tied((kept, given), spread[0])
    summed = kept + given
    near = {2: added(spread[2], back[2])}
    landed = {2: to_step(near[2], 2)}
    (summed,) = tied((summed,), near[2])
    given = [flipped(summed, k << 5) for k in range(1, 4)]
    summed = (summed + given[0]) + (given[1] + given[2])
    for s, after in ((1, near[2]), (3, summed)):
        (back[s],) = tied((back[s],), after)
        near[s] = added(spread[s], back[s])
        landed[s] = to_step(near[s], s)
    (summed,) = tied((summed,), near[1])
    given = [flipped(summed, k << 3) for k in range(1, 4)]
    summed = (summed + given[0]) + (given[1] + given[2])
    (back[0],) = tied((back[0],), near[3], landed[2], summed)
    near[0] = added(spread[0], back[0])
    landed[0] = to_step(near[0], 0)
    (summed,) = tied((summed,), near[0])
    given = [flipped(summed, k << 1) for k in range(1, 4)]
    summed = (summed + given[0]) + (given[1] + given[2])
    arrived = tied([landed[s] for s in range(NEAR)], summed)
    arrived = [value.astype(jnp.float32) for value in arrived]
    partial = ((arrived[0] + arrived[1]) + (arrived[2] + arrived[3])).astype(jnp.bfloat16)
    partial_other = shifted(partial, lambda b, r: (b, 1 - r))
    (summed,) = tied((summed,), partial)
    traded = flipped(summed, 1)
    there = shifted(summed, lambda b, r: (b, 1 - r))
    aside = shifted(summed, lambda b, r: (b ^ 1, 1 - r))
    d_features = d_self + (partial.astype(jnp.float32) + partial_other.astype(jnp.float32))

    def whole(mine, others):
        return jnp.concatenate(
            [jnp.where(core == 0, mine, others), jnp.where(core == 0, others, mine)], axis=0
        )

    d_here, d_there = whole(summed, traded), whole(there, aside)
    d_w_self = jnp.where(rep == 0, d_here, d_there)[:FEAT]
    d_w_neigh = jnp.where(rep == 0, d_there, d_here)[:FEAT]
    return (embeddings, d_features, d_w_self, d_w_neigh, d_here[FEAT])


def solution(mesh):
    return jax.shard_map(
        body,
        mesh=mesh,
        in_specs=(
            P("blk", None),
            P("blk", "rep", None, None),
            P("blk", "rep", None, None, None),
            P(),
            P(),
            P(),
            P("blk", None),
            P("blk", None),
        ),
        out_specs=(P("blk", None), P("blk", None), P(), P(), P()),
        check_vma=False,
    )
```

```python
import math

import jax
import jax.numpy as jnp
from jax import lax
from jax.experimental import pallas as pl
from jax.experimental.pallas import tpu as pltpu
from jax.sharding import PartitionSpec as P

STEPS = 8
TILE = 128
ROWS = 1024
FEAT = 128
HID = 256
TILES = 64
BLOCKS = 128
REPS = 2
GROUP = 8
NEAR = STEPS // 2
WROWS = 144
PANEL = 256
norm_eps = 1e-05
VMEM_LIMIT = 56 * 1024 * 1024
across = (((1,), (1,)), ((), ()))
down = (((0,), (0,)), ((), ()))

vmem = pl.BlockSpec(memory_space=pltpu.VMEM)
smem = pl.BlockSpec(memory_space=pltpu.SMEM)
anywhere = pl.BlockSpec(memory_space=pl.ANY)


def params():
    return pltpu.CompilerParams(vmem_limit_bytes=VMEM_LIMIT)


def cost(flops, bytes_accessed):
    return pl.CostEstimate(flops=flops, bytes_accessed=bytes_accessed, transcendentals=0)


def shifted(value, source_of):
    route = []
    for block in range(BLOCKS):
        for rep in range(REPS):
            source = source_of(block, rep)
            if source is not None:
                route.append(((source[0] % BLOCKS) * REPS + source[1], block * REPS + rep))
    return lax.ppermute(value, ("blk", "rep"), route)


def from_step(value, step):
    return shifted(value, lambda block, rep: (block - rep - 2 * step, rep))


def to_step(value, step):
    return shifted(value, lambda block, rep: (block + rep + 2 * step, rep))


def from_before(value):
    return shifted(value, lambda block, rep: (block - STEPS, rep))


def to_before(value):
    return shifted(value, lambda block, rep: (block + STEPS, rep))


def tied(values, *others):
    flat = lax.optimization_barrier(tuple(values) + tuple(others))
    return flat[: len(values)]


def tiles_kernel(first, index_ref, before_ref, counts_ref, tile_ref, turned_ref, degree_ref, sums):
    group = pl.program_id(0)

    @pl.when(group == 0)
    def _():
        sums[...] = jnp.zeros_like(sums)

    ones = jnp.ones((8, TILE), jnp.bfloat16)
    for k in range(GROUP):
        slot = first + group * GROUP + k
        used = index_ref[0, slot] < STEPS
        counts = jnp.where(used, counts_ref[k], 0).astype(jnp.float32)
        turned = counts.T.astype(jnp.bfloat16)
        tile_ref[k] = counts.astype(jnp.bfloat16)
        turned_ref[k] = turned
        row = index_ref[1, slot]
        sums[row] += jnp.dot(ones, turned, preferred_element_type=jnp.float32)

    @pl.when(group == pl.num_programs(0) - 1)
    def _():
        degree_ref[...] = before_ref[...] + sums[:, 0, :]


def prepare_tiles(index, before, counts, part, parts):
    share = TILES // parts
    spec = pl.BlockSpec((GROUP, TILE, TILE), lambda g: (g, 0, 0))
    shape = jax.ShapeDtypeStruct((share, TILE, TILE), jnp.bfloat16)
    whole = pl.BlockSpec((8, TILE), lambda g: (0, 0))
    return pl.pallas_call(
        lambda *refs: tiles_kernel(part * share, *refs),
        grid=(share // GROUP,),
        in_specs=[
            smem,
            whole,
            pl.BlockSpec((GROUP, TILE, TILE), lambda g: (g + part * share // GROUP, 0, 0)),
        ],
        out_specs=[spec, spec, whole],
        out_shape=[shape, shape, jax.ShapeDtypeStruct((8, TILE), jnp.float32)],
        scratch_shapes=[pltpu.VMEM((8, 8, TILE), jnp.float32)],
        compiler_params=params(),
        cost_estimate=cost(10**9, 8 * 2**20),
        name="prepare_tiles",
    )(index, before, counts)


def pairs_kernel(turned, joined_ref, left, right):
    def fill(i, carry):
        at = pl.ds(pl.multiple_of(i * TILE, TILE), TILE)
        rows = lax.broadcasted_iota(jnp.int32, (TILE, ROWS), 0) + i * TILE
        left[at, :] = (turned[0:1, :] == rows).astype(jnp.float32).astype(left.dtype)
        right[at, :] = (turned[1:2, :] == rows).astype(jnp.float32).astype(right.dtype)
        return carry

    lax.fori_loop(0, ROWS // TILE, fill, 0)
    for i in range(ROWS // PANEL):
        at = pl.ds(i * PANEL, PANEL)
        joined_ref[at, :] = lax.dot_general(
            left[at, :], right[...], across, preferred_element_type=jnp.float32
        )
    for i in range(ROWS // TILE):
        for j in range(i, ROWS // TILE):
            over = (pl.ds(i * TILE, TILE), pl.ds(j * TILE, TILE))
            under = (pl.ds(j * TILE, TILE), pl.ds(i * TILE, TILE))
            both = joined_ref[over] + joined_ref[under].T
            joined_ref[over] = both
            if i != j:
                joined_ref[under] = both.T


def join_pairs(turned):
    return pl.pallas_call(
        pairs_kernel,
        in_specs=[vmem],
        out_specs=vmem,
        out_shape=jax.ShapeDtypeStruct((ROWS, ROWS), jnp.float32),
        scratch_shapes=[pltpu.VMEM((ROWS, ROWS), jnp.float8_e4m3fn)] * 2,
        compiler_params=params(),
        cost_estimate=cost(3 * 10**9, 4 * 2**20),
        name="join_pairs",
    )(turned)


def held_row(index_ref, slot):
    step = jnp.minimum(index_ref[0, slot], STEPS - 1)
    return pl.multiple_of(step * ROWS + index_ref[2, slot] * TILE, TILE)


def gather_kernel(index_ref, tile_a, tile_b, *refs):
    blocks, (out_ref, held, total, sem) = refs[:STEPS], refs[STEPS:]
    copies = [
        pltpu.make_async_copy(block, held.at[pl.ds(k * ROWS, ROWS)], sem.at[k])
        for k, block in enumerate(blocks)
    ]
    for copy in copies:
        copy.start()
    total[...] = jnp.zeros_like(total)
    for copy in copies:
        copy.wait()
    for slot in range(TILES):
        tile = (tile_a if slot < TILES // 2 else tile_b)[slot % (TILES // 2)]
        source = held_row(index_ref, slot)
        target = pl.multiple_of(index_ref[1, slot] * TILE, TILE)
        total[pl.ds(target, TILE), :] += jnp.dot(
            tile, held[pl.ds(source, TILE), :], preferred_element_type=jnp.float32
        )
    out_ref[...] = total[...].astype(jnp.bfloat16)


def gather_tiles(index, tiles, blocks):
    return pl.pallas_call(
        gather_kernel,
        in_specs=[smem, vmem, vmem] + [anywhere] * STEPS,
        out_specs=vmem,
        out_shape=jax.ShapeDtypeStruct((ROWS, FEAT), jnp.bfloat16),
        scratch_shapes=[
            pltpu.VMEM((STEPS * ROWS, FEAT), jnp.bfloat16),
            pltpu.VMEM((ROWS, FEAT), jnp.float32),
            pltpu.SemaphoreType.DMA((STEPS,)),
        ],
        compiler_params=params(),
        cost_estimate=cost(10**9, 4 * 2**20),
        name="gather_tiles",
    )(index, *tiles, *blocks)


def layer_kernel(
    info_ref, mine_ref, other_ref, deg_mine, deg_other, feat_ref, w_self, w_neigh, bias,
    joined_pos, joined_neg,
    emb_ref, d_self_ref, d_mean_ref, d_weight_ref,
    counts, hidden, scaled, mean, inverse, grad, bias_sum, sem,
):
    copies = [
        pltpu.make_async_copy(ref, counts.at[k], sem.at[k])
        for k, ref in enumerate((joined_pos, joined_neg))
    ]
    for copy in copies:
        copy.start()
    factor = -math.log2(math.e) / math.sqrt(HID)

    def divisor_of(i):
        rows = []
        for k in range(i * PANEL // TILE, (i + 1) * PANEL // TILE):
            row = deg_mine[pl.ds(k, 1), :] + deg_other[pl.ds(k, 1), :]
            rows.append(jnp.broadcast_to(jnp.maximum(row, 1.0), (TILE, TILE)).T)
        return jnp.concatenate(rows, axis=0)

    for i in range(ROWS // PANEL):
        at = pl.ds(i * PANEL, PANEL)
        total = mine_ref[at, :].astype(jnp.float32) + other_ref[at, :].astype(jnp.float32)
        low = (total / divisor_of(i)).astype(jnp.bfloat16)
        mean[at, :] = low
        preact = (
            jnp.dot(feat_ref[at, :], w_self[...], preferred_element_type=jnp.float32)
            + jnp.dot(low, w_neigh[...], preferred_element_type=jnp.float32)
            + bias[...]
        )
        inv = lax.rsqrt(jnp.mean(preact * preact, axis=1, keepdims=True) + norm_eps)
        hid = preact * inv
        hidden[at, :] = hid
        inverse[at, :] = inv
        emb_ref[at, :] = hid.astype(jnp.bfloat16)
        scaled[at, :] = (hid * factor).astype(jnp.bfloat16)

    for copy in copies:
        copy.wait()
    bias_sum[...] = jnp.zeros_like(bias_sum)
    diagonal = lax.broadcasted_iota(jnp.int32, (PANEL, PANEL), 0) == lax.broadcasted_iota(
        jnp.int32, (PANEL, PANEL), 1
    )
    for i in range(ROWS // PANEL):
        at = pl.ds(i * PANEL, PANEL)
        d_hidden = jnp.zeros((PANEL, HID), jnp.float32)
        for j in range(ROWS // PANEL):
            to = pl.ds(j * PANEL, PANEL)
            power = lax.dot_general(
                scaled[at, :], emb_ref[to, :], across, preferred_element_type=jnp.float32
            )
            grown = jnp.exp2(power)
            coef = (counts[1, at, to] - counts[0, at, to] * grown) * pl.reciprocal(
                1.0 + grown, approx=True
            )
            if i == j:
                own = jnp.where(diagonal, coef, 0.0)
                coef = coef - own
                d_hidden += jnp.sum(own, axis=1, keepdims=True) * hidden[at, :]
            d_hidden += jnp.dot(
                coef.astype(jnp.bfloat16), emb_ref[to, :], preferred_element_type=jnp.float32
            )
        d_hidden *= 1.0 / math.sqrt(HID)
        hid = hidden[at, :]
        d_preact = inverse[at, :] * (
            d_hidden - hid * jnp.mean(d_hidden * hid, axis=1, keepdims=True)
        )
        bias_sum[...] += jnp.sum(d_preact.reshape(PANEL // 8, 8, HID), axis=0)
        low = d_preact.astype(jnp.bfloat16)
        grad[at, :] = low
        d_self_ref[at, :] = lax.dot_general(
            low, w_self[...], across, preferred_element_type=jnp.float32
        )
        d_mean_ref[at, :] = (
            lax.dot_general(low, w_neigh[...], across, preferred_element_type=jnp.float32)
            / divisor_of(i)
        ).astype(jnp.bfloat16)
    chosen = jnp.where(
        info_ref[0] == 0, feat_ref[...].astype(jnp.float32), mean[...].astype(jnp.float32)
    )
    d_weight_ref[0:FEAT, :] = lax.dot_general(
        chosen.astype(jnp.bfloat16), grad[...], down, preferred_element_type=jnp.float32
    )
    d_weight_ref[FEAT : FEAT + 8, :] = jnp.broadcast_to(
        jnp.sum(bias_sum[...], axis=0, keepdims=True), (8, HID)
    )
    d_weight_ref[FEAT + 8 :, :] = jnp.zeros((WROWS - FEAT - 8, HID), jnp.float32)


def layer(info, mine, other, deg_mine, deg_other, features, w_self, w_neigh, bias, joined):
    shapes = [
        jax.ShapeDtypeStruct((ROWS, HID), jnp.bfloat16),
        jax.ShapeDtypeStruct((ROWS, FEAT), jnp.float32),
        jax.ShapeDtypeStruct((ROWS, FEAT), jnp.bfloat16),
        jax.ShapeDtypeStruct((WROWS, HID), jnp.float32),
    ]
    return pl.pallas_call(
        layer_kernel,
        in_specs=[smem] + [vmem] * 8 + [anywhere] * 2,
        out_specs=[vmem] * 4,
        out_shape=shapes,
        scratch_shapes=[
            pltpu.VMEM((2, ROWS, ROWS), jnp.float32),
            pltpu.VMEM((ROWS, HID), jnp.float32),
            pltpu.VMEM((ROWS, HID), jnp.bfloat16),
            pltpu.VMEM((ROWS, FEAT), jnp.bfloat16),
            pltpu.VMEM((ROWS, 1), jnp.float32),
            pltpu.VMEM((ROWS, HID), jnp.bfloat16),
            pltpu.VMEM((8, HID), jnp.float32),
            pltpu.SemaphoreType.DMA((2,)),
        ],
        compiler_params=params(),
        cost_estimate=cost(2 * 10**9, 12 * 2**20),
        name="layer",
    )(info, mine, other, deg_mine, deg_other, features, w_self, w_neigh, bias, *joined)


def spread_kernel(index_ref, turned_a, turned_b, grad_ref, *refs):
    outs, (total,) = refs[:STEPS], refs[STEPS:]
    total[...] = jnp.zeros_like(total)
    for slot in range(TILES):
        tile = (turned_a if slot < TILES // 2 else turned_b)[slot % (TILES // 2)]
        target = held_row(index_ref, slot)
        source = pl.multiple_of(index_ref[1, slot] * TILE, TILE)
        total[pl.ds(target, TILE), :] += jnp.dot(
            tile, grad_ref[pl.ds(source, TILE), :], preferred_element_type=jnp.float32
        )
    for k, out in enumerate(outs):
        out[...] = total[k * ROWS : (k + 1) * ROWS, :].astype(jnp.bfloat16)


def spread_tiles(index, turned, d_mean):
    return pl.pallas_call(
        spread_kernel,
        in_specs=[smem, vmem, vmem, vmem],
        out_specs=[vmem] * STEPS,
        out_shape=[jax.ShapeDtypeStruct((ROWS, FEAT), jnp.bfloat16)] * STEPS,
        scratch_shapes=[pltpu.VMEM((STEPS * ROWS, FEAT), jnp.float32)],
        compiler_params=params(),
        cost_estimate=cost(10**9, 4 * 2**20),
        name="spread_tiles",
    )(index, *turned, d_mean)


def flipped(value, mask):
    return shifted(value, lambda block, rep: (block ^ mask, rep))


def added(left, right):
    return (left.astype(jnp.float32) + right.astype(jnp.float32)).astype(jnp.bfloat16)


def body(features, tile_index, tile_counts, w_self, w_neigh, bias, pos_pairs, neg_pairs):
    block, rep = lax.axis_index("blk"), lax.axis_index("rep")
    core = block & 1
    index, counts = tile_index[0, 0], tile_counts[0, 0]
    info = rep.reshape(1).astype(jnp.int32)
    pos_turned, neg_turned = pos_pairs.T, neg_pairs.T

    held = {s: from_step(features, s) for s in (4, 1, 3, 2, 0)}
    tiles_a, turned_a, degree = prepare_tiles(index, jnp.zeros((8, TILE), jnp.float32), counts, 0, 2)
    tiles_b, turned_b, degree = prepare_tiles(index, degree, counts, 1, 2)
    held[1], degree = tied((held[1], degree), turned_b)
    held[5] = from_before(held[1])
    (pos_turned,) = tied((pos_turned,), held[1])
    joined_pos = join_pairs(pos_turned)
    held[3], degree = tied((held[3], degree), joined_pos, held[4])
    held[7] = from_before(held[3])
    (held[2],) = tied((held[2],), held[5], held[3])
    held[6] = from_before(held[2])
    degree_other = shifted(degree, lambda b, r: (b, 1 - r))
    mine = gather_tiles(index, (tiles_a, tiles_b), [held[s] for s in range(STEPS)])
    other = shifted(mine, lambda b, r: (b, 1 - r))
    (neg_turned,) = tied((neg_turned,), mine)
    joined_neg = join_pairs(neg_turned)

    embeddings, d_self, d_mean, d_weight = layer(
        info, mine, other, degree, degree_other,
        features, w_self, w_neigh, bias.reshape(1, HID), (joined_pos, joined_neg),
    )

    rows = d_weight.shape[0] // 2
    kept = lax.dynamic_slice_in_dim(d_weight, core * rows, rows, 0)
    given = lax.dynamic_slice_in_dim(d_weight, (1 - core) * rows, rows, 0)
    given = flipped(given, 1)
    spread = spread_tiles(index, (turned_a, turned_b), d_mean)
    back = {s: to_before(spread[s + NEAR]) for s in (2, 1, 3)}
    kept, given = tied((kept, given), spread[0])
    summed = kept + given
    landed = {s: to_step(spread[s], s) for s in (0, 4)}
    (first,) = tied((back[2],), summed)
    first = added(spread[2], first)
    landed[2] = to_step(first, 2)
    later = tied([back[1], back[3]], landed[0], landed[4], landed[2])
    near = [added(spread[1], later[0]), added(spread[3], later[1])]
    landed[1], landed[3] = to_step(near[0], 1), to_step(near[1], 3)

    def over_blocks(_, value):
        for shift in (5, 3, 1):
            given = [flipped(value, k << shift) for k in range(1, 4)]
            value = (value + given[0]) + (given[1] + given[2])
        return value

    (summed,) = tied((summed,), *near)
    summed = lax.fori_loop(0, 1 + jnp.minimum(rep, 0), over_blocks, summed)
    landed[1], landed[3] = tied((landed[1], landed[3]), summed)
    arrived = [landed[s].astype(jnp.float32) for s in (0, 4, 2, 1, 3)]
    partial = ((arrived[0] + arrived[1]) + arrived[2] + (arrived[3] + arrived[4]))
    partial = partial.astype(jnp.bfloat16)
    partial_other = shifted(partial, lambda b, r: (b, 1 - r))
    (summed,) = tied((summed,), partial)
    traded = flipped(summed, 1)
    there = shifted(summed, lambda b, r: (b, 1 - r))
    aside = shifted(summed, lambda b, r: (b ^ 1, 1 - r))
    d_features = d_self + (partial.astype(jnp.float32) + partial_other.astype(jnp.float32))

    def whole(mine, others):
        return jnp.concatenate(
            [jnp.where(core == 0, mine, others), jnp.where(core == 0, others, mine)], axis=0
        )

    d_here, d_there = whole(summed, traded), whole(there, aside)
    d_w_self = jnp.where(rep == 0, d_here, d_there)[:FEAT]
    d_w_neigh = jnp.where(rep == 0, d_there, d_here)[:FEAT]
    return (embeddings, d_features, d_w_self, d_w_neigh, d_here[FEAT])


def solution(mesh):
    return jax.shard_map(
        body,
        mesh=mesh,
        in_specs=(
            P("blk", None),
            P("blk", "rep", None, None),
            P("blk", "rep", None, None, None),
            P(),
            P(),
            P(),
            P("blk", None),
            P("blk", None),
        ),
        out_specs=(P("blk", None), P("blk", None), P(), P(), P()),
        check_vma=False,
    )
```

```python
import math

import jax
import jax.numpy as jnp
from jax import lax
from jax.experimental import pallas as pl
from jax.experimental.pallas import tpu as pltpu
from jax.sharding import PartitionSpec as P

STEPS = 8
TILE = 128
ROWS = 1024
FEAT = 128
HID = 256
TILES = 64
BLOCKS = 128
REPS = 2
GROUP = 8
NEAR = STEPS // 2
WROWS = 144
PANEL = 256
norm_eps = 1e-05
VMEM_LIMIT = 56 * 1024 * 1024
across = (((1,), (1,)), ((), ()))
down = (((0,), (0,)), ((), ()))

vmem = pl.BlockSpec(memory_space=pltpu.VMEM)
smem = pl.BlockSpec(memory_space=pltpu.SMEM)
anywhere = pl.BlockSpec(memory_space=pl.ANY)


def params():
    return pltpu.CompilerParams(vmem_limit_bytes=VMEM_LIMIT)


def cost(flops, bytes_accessed):
    return pl.CostEstimate(flops=flops, bytes_accessed=bytes_accessed, transcendentals=0)


def shifted(value, source_of):
    route = []
    for block in range(BLOCKS):
        for rep in range(REPS):
            source = source_of(block, rep)
            if source is not None:
                route.append(((source[0] % BLOCKS) * REPS + source[1], block * REPS + rep))
    return lax.ppermute(value, ("blk", "rep"), route)


def from_step(value, step):
    return shifted(value, lambda block, rep: (block - rep - 2 * step, rep))


def to_step(value, step):
    return shifted(value, lambda block, rep: (block + rep + 2 * step, rep))


def from_before(value):
    return shifted(value, lambda block, rep: (block - STEPS, rep))


def to_before(value):
    return shifted(value, lambda block, rep: (block + STEPS, rep))


def tied(values, *others):
    flat = lax.optimization_barrier(tuple(values) + tuple(others))
    return flat[: len(values)]


def tiles_kernel(first, index_ref, before_ref, counts_ref, tile_ref, turned_ref, degree_ref, sums):
    group = pl.program_id(0)

    @pl.when(group == 0)
    def _():
        sums[...] = jnp.zeros_like(sums)

    ones = jnp.ones((8, TILE), jnp.bfloat16)
    for k in range(GROUP):
        slot = first + group * GROUP + k
        used = index_ref[0, slot] < STEPS
        counts = jnp.where(used, counts_ref[k], 0).astype(jnp.float32)
        turned = counts.T.astype(jnp.bfloat16)
        tile_ref[k] = counts.astype(jnp.bfloat16)
        turned_ref[k] = turned
        row = index_ref[1, slot]
        sums[row] += jnp.dot(ones, turned, preferred_element_type=jnp.float32)

    @pl.when(group == pl.num_programs(0) - 1)
    def _():
        degree_ref[...] = before_ref[...] + sums[:, 0, :]


def prepare_tiles(index, before, counts, part, parts):
    share = TILES // parts
    spec = pl.BlockSpec((GROUP, TILE, TILE), lambda g: (g, 0, 0))
    shape = jax.ShapeDtypeStruct((share, TILE, TILE), jnp.bfloat16)
    whole = pl.BlockSpec((8, TILE), lambda g: (0, 0))
    return pl.pallas_call(
        lambda *refs: tiles_kernel(part * share, *refs),
        grid=(share // GROUP,),
        in_specs=[
            smem,
            whole,
            pl.BlockSpec((GROUP, TILE, TILE), lambda g: (g + part * share // GROUP, 0, 0)),
        ],
        out_specs=[spec, spec, whole],
        out_shape=[shape, shape, jax.ShapeDtypeStruct((8, TILE), jnp.float32)],
        scratch_shapes=[pltpu.VMEM((8, 8, TILE), jnp.float32)],
        compiler_params=params(),
        cost_estimate=cost(10**9, 8 * 2**20),
        name="prepare_tiles",
    )(index, before, counts)


def pairs_kernel(turned, joined_ref, left, right):
    def fill(i, carry):
        at = pl.ds(pl.multiple_of(i * TILE, TILE), TILE)
        rows = lax.broadcasted_iota(jnp.int32, (TILE, ROWS), 0) + i * TILE
        left[at, :] = (turned[0:1, :] == rows).astype(jnp.float32).astype(left.dtype)
        right[at, :] = (turned[1:2, :] == rows).astype(jnp.float32).astype(right.dtype)
        return carry

    lax.fori_loop(0, ROWS // TILE, fill, 0)
    for i in range(ROWS // PANEL):
        at = pl.ds(i * PANEL, PANEL)
        joined_ref[at, :] = lax.dot_general(
            left[at, :], right[...], across, preferred_element_type=jnp.float32
        )
    for i in range(ROWS // TILE):
        for j in range(i, ROWS // TILE):
            over = (pl.ds(i * TILE, TILE), pl.ds(j * TILE, TILE))
            under = (pl.ds(j * TILE, TILE), pl.ds(i * TILE, TILE))
            both = joined_ref[over] + joined_ref[under].T
            joined_ref[over] = both
            if i != j:
                joined_ref[under] = both.T


def join_pairs(turned):
    return pl.pallas_call(
        pairs_kernel,
        in_specs=[vmem],
        out_specs=vmem,
        out_shape=jax.ShapeDtypeStruct((ROWS, ROWS), jnp.float32),
        scratch_shapes=[pltpu.VMEM((ROWS, ROWS), jnp.float8_e4m3fn)] * 2,
        compiler_params=params(),
        cost_estimate=cost(3 * 10**9, 4 * 2**20),
        name="join_pairs",
    )(turned)


def held_row(index_ref, slot):
    step = jnp.minimum(index_ref[0, slot], STEPS - 1)
    return pl.multiple_of(step * ROWS + index_ref[2, slot] * TILE, TILE)


def gather_kernel(index_ref, tile_a, tile_b, *refs):
    blocks, (out_ref, held, total, sem) = refs[:STEPS], refs[STEPS:]
    copies = [
        pltpu.make_async_copy(block, held.at[pl.ds(k * ROWS, ROWS)], sem.at[k])
        for k, block in enumerate(blocks)
    ]
    for copy in copies:
        copy.start()
    total[...] = jnp.zeros_like(total)
    for copy in copies:
        copy.wait()
    for slot in range(TILES):
        tile = (tile_a if slot < TILES // 2 else tile_b)[slot % (TILES // 2)]
        source = held_row(index_ref, slot)
        target = pl.multiple_of(index_ref[1, slot] * TILE, TILE)
        total[pl.ds(target, TILE), :] += jnp.dot(
            tile, held[pl.ds(source, TILE), :], preferred_element_type=jnp.float32
        )
    out_ref[...] = total[...].astype(jnp.bfloat16)


def gather_tiles(index, tiles, blocks):
    return pl.pallas_call(
        gather_kernel,
        in_specs=[smem, vmem, vmem] + [anywhere] * STEPS,
        out_specs=vmem,
        out_shape=jax.ShapeDtypeStruct((ROWS, FEAT), jnp.bfloat16),
        scratch_shapes=[
            pltpu.VMEM((STEPS * ROWS, FEAT), jnp.bfloat16),
            pltpu.VMEM((ROWS, FEAT), jnp.float32),
            pltpu.SemaphoreType.DMA((STEPS,)),
        ],
        compiler_params=params(),
        cost_estimate=cost(10**9, 4 * 2**20),
        name="gather_tiles",
    )(index, *tiles, *blocks)


def layer_kernel(
    info_ref, mine_ref, other_ref, deg_mine, deg_other, feat_ref, w_self, w_neigh, bias,
    joined_pos, joined_neg,
    emb_ref, d_self_ref, d_mean_ref, d_weight_ref,
    counts, hidden, scaled, mean, inverse, grad, bias_sum, sem,
):
    copies = [
        pltpu.make_async_copy(ref, counts.at[k], sem.at[k])
        for k, ref in enumerate((joined_pos, joined_neg))
    ]
    for copy in copies:
        copy.start()
    factor = -math.log2(math.e) / math.sqrt(HID)

    def divisor_of(i):
        rows = []
        for k in range(i * PANEL // TILE, (i + 1) * PANEL // TILE):
            row = deg_mine[pl.ds(k, 1), :] + deg_other[pl.ds(k, 1), :]
            rows.append(jnp.broadcast_to(jnp.maximum(row, 1.0), (TILE, TILE)).T)
        return jnp.concatenate(rows, axis=0)

    for i in range(ROWS // PANEL):
        at = pl.ds(i * PANEL, PANEL)
        total = mine_ref[at, :].astype(jnp.float32) + other_ref[at, :].astype(jnp.float32)
        low = (total / divisor_of(i)).astype(jnp.bfloat16)
        mean[at, :] = low
        preact = (
            jnp.dot(feat_ref[at, :], w_self[...], preferred_element_type=jnp.float32)
            + jnp.dot(low, w_neigh[...], preferred_element_type=jnp.float32)
            + bias[...]
        )
        inv = lax.rsqrt(jnp.mean(preact * preact, axis=1, keepdims=True) + norm_eps)
        hid = preact * inv
        hidden[at, :] = hid
        inverse[at, :] = inv
        emb_ref[at, :] = hid.astype(jnp.bfloat16)
        scaled[at, :] = (hid * factor).astype(jnp.bfloat16)

    for copy in copies:
        copy.wait()
    bias_sum[...] = jnp.zeros_like(bias_sum)
    diagonal = lax.broadcasted_iota(jnp.int32, (PANEL, PANEL), 0) == lax.broadcasted_iota(
        jnp.int32, (PANEL, PANEL), 1
    )
    for i in range(ROWS // PANEL):
        at = pl.ds(i * PANEL, PANEL)
        d_hidden = jnp.zeros((PANEL, HID), jnp.float32)
        for j in range(ROWS // PANEL):
            to = pl.ds(j * PANEL, PANEL)
            power = lax.dot_general(
                scaled[at, :], emb_ref[to, :], across, preferred_element_type=jnp.float32
            )
            grown = jnp.exp2(power)
            coef = (counts[1, at, to] - counts[0, at, to] * grown) * pl.reciprocal(
                1.0 + grown, approx=True
            )
            if i == j:
                own = jnp.where(diagonal, coef, 0.0)
                coef = coef - own
                d_hidden += jnp.sum(own, axis=1, keepdims=True) * hidden[at, :]
            d_hidden += jnp.dot(
                coef.astype(jnp.bfloat16), emb_ref[to, :], preferred_element_type=jnp.float32
            )
        d_hidden *= 1.0 / math.sqrt(HID)
        hid = hidden[at, :]
        d_preact = inverse[at, :] * (
            d_hidden - hid * jnp.mean(d_hidden * hid, axis=1, keepdims=True)
        )
        bias_sum[...] += jnp.sum(d_preact.reshape(PANEL // 8, 8, HID), axis=0)
        low = d_preact.astype(jnp.bfloat16)
        grad[at, :] = low
        d_self_ref[at, :] = lax.dot_general(
            low, w_self[...], across, preferred_element_type=jnp.float32
        )
        d_mean_ref[at, :] = (
            lax.dot_general(low, w_neigh[...], across, preferred_element_type=jnp.float32)
            / divisor_of(i)
        ).astype(jnp.bfloat16)
    chosen = jnp.where(
        info_ref[0] == 0, feat_ref[...].astype(jnp.float32), mean[...].astype(jnp.float32)
    )
    d_weight_ref[0:FEAT, :] = lax.dot_general(
        chosen.astype(jnp.bfloat16), grad[...], down, preferred_element_type=jnp.float32
    )
    d_weight_ref[FEAT : FEAT + 8, :] = jnp.broadcast_to(
        jnp.sum(bias_sum[...], axis=0, keepdims=True), (8, HID)
    )
    d_weight_ref[FEAT + 8 :, :] = jnp.zeros((WROWS - FEAT - 8, HID), jnp.float32)


def layer(info, mine, other, deg_mine, deg_other, features, w_self, w_neigh, bias, joined):
    shapes = [
        jax.ShapeDtypeStruct((ROWS, HID), jnp.bfloat16),
        jax.ShapeDtypeStruct((ROWS, FEAT), jnp.float32),
        jax.ShapeDtypeStruct((ROWS, FEAT), jnp.bfloat16),
        jax.ShapeDtypeStruct((WROWS, HID), jnp.float32),
    ]
    return pl.pallas_call(
        layer_kernel,
        in_specs=[smem] + [vmem] * 8 + [anywhere] * 2,
        out_specs=[vmem] * 4,
        out_shape=shapes,
        scratch_shapes=[
            pltpu.VMEM((2, ROWS, ROWS), jnp.float32),
            pltpu.VMEM((ROWS, HID), jnp.float32),
            pltpu.VMEM((ROWS, HID), jnp.bfloat16),
            pltpu.VMEM((ROWS, FEAT), jnp.bfloat16),
            pltpu.VMEM((ROWS, 1), jnp.float32),
            pltpu.VMEM((ROWS, HID), jnp.bfloat16),
            pltpu.VMEM((8, HID), jnp.float32),
            pltpu.SemaphoreType.DMA((2,)),
        ],
        compiler_params=params(),
        cost_estimate=cost(2 * 10**9, 12 * 2**20),
        name="layer",
    )(info, mine, other, deg_mine, deg_other, features, w_self, w_neigh, bias, *joined)


def spread_kernel(index_ref, turned_a, turned_b, grad_ref, *refs):
    outs, (total,) = refs[:STEPS], refs[STEPS:]
    total[...] = jnp.zeros_like(total)
    for slot in range(TILES):
        tile = (turned_a if slot < TILES // 2 else turned_b)[slot % (TILES // 2)]
        target = held_row(index_ref, slot)
        source = pl.multiple_of(index_ref[1, slot] * TILE, TILE)
        total[pl.ds(target, TILE), :] += jnp.dot(
            tile, grad_ref[pl.ds(source, TILE), :], preferred_element_type=jnp.float32
        )
    for k, out in enumerate(outs):
        out[...] = total[k * ROWS : (k + 1) * ROWS, :].astype(jnp.bfloat16)


def spread_tiles(index, turned, d_mean):
    return pl.pallas_call(
        spread_kernel,
        in_specs=[smem, vmem, vmem, vmem],
        out_specs=[vmem] * STEPS,
        out_shape=[jax.ShapeDtypeStruct((ROWS, FEAT), jnp.bfloat16)] * STEPS,
        scratch_shapes=[pltpu.VMEM((STEPS * ROWS, FEAT), jnp.float32)],
        compiler_params=params(),
        cost_estimate=cost(10**9, 4 * 2**20),
        name="spread_tiles",
    )(index, *turned, d_mean)


def flipped(value, mask):
    return shifted(value, lambda block, rep: (block ^ mask, rep))


def added(left, right):
    return (left.astype(jnp.float32) + right.astype(jnp.float32)).astype(jnp.bfloat16)


def body(features, tile_index, tile_counts, w_self, w_neigh, bias, pos_pairs, neg_pairs):
    block, rep = lax.axis_index("blk"), lax.axis_index("rep")
    core = block & 1
    index, counts = tile_index[0, 0], tile_counts[0, 0]
    info = rep.reshape(1).astype(jnp.int32)
    pos_turned, neg_turned = pos_pairs.T, neg_pairs.T

    held = {s: from_step(features, s) for s in (4, 1, 3, 2, 0)}
    tiles_a, turned_a, degree = prepare_tiles(index, jnp.zeros((8, TILE), jnp.float32), counts, 0, 2)
    tiles_b, turned_b, degree = prepare_tiles(index, degree, counts, 1, 2)
    held[1], degree = tied((held[1], degree), turned_b)
    held[5] = from_before(held[1])
    (pos_turned,) = tied((pos_turned,), held[1])
    joined_pos = join_pairs(pos_turned)
    held[3], degree = tied((held[3], degree), joined_pos, held[4])
    held[7] = from_before(held[3])
    (held[2],) = tied((held[2],), held[5], held[3])
    held[6] = from_before(held[2])
    degree_other = shifted(degree, lambda b, r: (b, 1 - r))
    mine = gather_tiles(index, (tiles_a, tiles_b), [held[s] for s in range(STEPS)])
    other = shifted(mine, lambda b, r: (b, 1 - r))
    (neg_turned,) = tied((neg_turned,), mine)
    joined_neg = join_pairs(neg_turned)

    embeddings, d_self, d_mean, d_weight = layer(
        info, mine, other, degree, degree_other,
        features, w_self, w_neigh, bias.reshape(1, HID), (joined_pos, joined_neg),
    )

    rows = d_weight.shape[0] // 2
    kept = lax.dynamic_slice_in_dim(d_weight, core * rows, rows, 0)
    given = lax.dynamic_slice_in_dim(d_weight, (1 - core) * rows, rows, 0)
    given = flipped(given, 1)
    spread = spread_tiles(index, (turned_a, turned_b), d_mean)
    order = (2, 1, 3, 0)
    back = {s: to_before(spread[s + NEAR]) for s in order}
    kept, given = tied((kept, given), spread[0])
    once = 1 + jnp.minimum(rep, 0)

    def summed_over(value, *shifts):
        def one_pass(_, value):
            for shift in shifts:
                value = value + flipped(value, 1 << shift)
            return value

        return lax.fori_loop(0, once, one_pass, value)

    summed = summed_over(kept + given, 5, 6)
    (first,) = tied((back[2],), summed)
    first = added(spread[2], first)
    landed = {2: to_step(first, 2)}
    (summed,) = tied((summed,), first)
    summed = summed_over(summed, 3, 4)
    later = tied([back[s] for s in order[1:]], landed[2], summed)
    near = {s: added(spread[s], value) for s, value in zip(order[1:], later)}
    landed.update({s: to_step(near[s], s) for s in order[1:]})
    (summed,) = tied((summed,), *near.values())

    def last_pass(_, state):
        value = state[0][:rows]
        for shift in (1, 2):
            value = value + flipped(value, 1 << shift)
        traded = flipped(value, 1)
        value = jnp.concatenate(
            [jnp.where(core == 0, value, traded), jnp.where(core == 0, traded, value)], axis=0
        )
        return value, shifted(value[:FEAT], lambda b, r: (b, 1 - r))

    both = jnp.concatenate([summed, summed], axis=0)

    d_here, d_there = lax.fori_loop(0, once, last_pass, (both, both[:FEAT]))
    arrived = tied([landed[s] for s in range(NEAR)], d_there)
    arrived = [value.astype(jnp.float32) for value in arrived]
    partial = ((arrived[0] + arrived[1]) + (arrived[2] + arrived[3])).astype(jnp.bfloat16)
    partial_other = shifted(partial, lambda b, r: (b, 1 - r))
    d_features = d_self + (partial.astype(jnp.float32) + partial_other.astype(jnp.float32))
    d_w_self = jnp.where(rep == 0, d_here[:FEAT], d_there)
    d_w_neigh = jnp.where(rep == 0, d_there, d_here[:FEAT])
    return (embeddings, d_features, d_w_self, d_w_neigh, d_here[FEAT])


def solution(mesh):
    return jax.shard_map(
        body,
        mesh=mesh,
        in_specs=(
            P("blk", None),
            P("blk", "rep", None, None),
            P("blk", "rep", None, None, None),
            P(),
            P(),
            P(),
            P("blk", None),
            P("blk", None),
        ),
        out_specs=(P("blk", None), P("blk", None), P(), P(), P()),
        check_vma=False,
    )
```

```python
import math

import jax
import jax.numpy as jnp
from jax import lax
from jax.experimental import pallas as pl
from jax.experimental.pallas import tpu as pltpu
from jax.sharding import PartitionSpec as P

STEPS = 8
TILE = 128
ROWS = 1024
FEAT = 128
HID = 256
TILES = 64
BLOCKS = 128
REPS = 2
GROUP = 8
NEAR = STEPS // 2
WROWS = 144
PANEL = 256
norm_eps = 1e-05
VMEM_LIMIT = 56 * 1024 * 1024
across = (((1,), (1,)), ((), ()))
down = (((0,), (0,)), ((), ()))

vmem = pl.BlockSpec(memory_space=pltpu.VMEM)
smem = pl.BlockSpec(memory_space=pltpu.SMEM)
anywhere = pl.BlockSpec(memory_space=pl.ANY)


def params():
    return pltpu.CompilerParams(vmem_limit_bytes=VMEM_LIMIT)


def cost(flops, bytes_accessed):
    return pl.CostEstimate(flops=flops, bytes_accessed=bytes_accessed, transcendentals=0)


def shifted(value, source_of):
    route = []
    for block in range(BLOCKS):
        for rep in range(REPS):
            source = source_of(block, rep)
            if source is not None:
                route.append(((source[0] % BLOCKS) * REPS + source[1], block * REPS + rep))
    return lax.ppermute(value, ("blk", "rep"), route)


def from_step(value, step):
    return shifted(value, lambda block, rep: (block - rep - 2 * step, rep))


def to_step(value, step):
    return shifted(value, lambda block, rep: (block + rep + 2 * step, rep))


def from_before(value):
    return shifted(value, lambda block, rep: (block - STEPS, rep))


def to_before(value):
    return shifted(value, lambda block, rep: (block + STEPS, rep))


def tied(values, *others):
    flat = lax.optimization_barrier(tuple(values) + tuple(others))
    return flat[: len(values)]


def tiles_kernel(first, index_ref, before_ref, counts_ref, tile_ref, turned_ref, degree_ref, sums):
    group = pl.program_id(0)

    @pl.when(group == 0)
    def _():
        sums[...] = jnp.zeros_like(sums)

    ones = jnp.ones((8, TILE), jnp.bfloat16)
    for k in range(GROUP):
        slot = first + group * GROUP + k
        used = index_ref[0, slot] < STEPS
        counts = jnp.where(used, counts_ref[k], 0).astype(jnp.float32)
        turned = counts.T.astype(jnp.bfloat16)
        tile_ref[k] = counts.astype(jnp.bfloat16)
        turned_ref[k] = turned
        row = index_ref[1, slot]
        sums[row] += jnp.dot(ones, turned, preferred_element_type=jnp.float32)

    @pl.when(group == pl.num_programs(0) - 1)
    def _():
        degree_ref[...] = before_ref[...] + sums[:, 0, :]


def prepare_tiles(index, before, counts, part, parts):
    share = TILES // parts
    spec = pl.BlockSpec((GROUP, TILE, TILE), lambda g: (g, 0, 0))
    shape = jax.ShapeDtypeStruct((share, TILE, TILE), jnp.bfloat16)
    whole = pl.BlockSpec((8, TILE), lambda g: (0, 0))
    return pl.pallas_call(
        lambda *refs: tiles_kernel(part * share, *refs),
        grid=(share // GROUP,),
        in_specs=[
            smem,
            whole,
            pl.BlockSpec((GROUP, TILE, TILE), lambda g: (g + part * share // GROUP, 0, 0)),
        ],
        out_specs=[spec, spec, whole],
        out_shape=[shape, shape, jax.ShapeDtypeStruct((8, TILE), jnp.float32)],
        scratch_shapes=[pltpu.VMEM((8, 8, TILE), jnp.float32)],
        compiler_params=params(),
        cost_estimate=cost(10**9, 8 * 2**20),
        name="prepare_tiles",
    )(index, before, counts)


def pairs_kernel(turned, joined_ref, left, right):
    def fill(i, carry):
        at = pl.ds(pl.multiple_of(i * TILE, TILE), TILE)
        rows = lax.broadcasted_iota(jnp.int32, (TILE, ROWS), 0) + i * TILE
        left[at, :] = (turned[0:1, :] == rows).astype(jnp.float32).astype(left.dtype)
        right[at, :] = (turned[1:2, :] == rows).astype(jnp.float32).astype(right.dtype)
        return carry

    lax.fori_loop(0, ROWS // TILE, fill, 0)
    for i in range(ROWS // PANEL):
        at = pl.ds(i * PANEL, PANEL)
        joined_ref[at, :] = lax.dot_general(
            left[at, :], right[...], across, preferred_element_type=jnp.float32
        )
    for i in range(ROWS // TILE):
        for j in range(i, ROWS // TILE):
            over = (pl.ds(i * TILE, TILE), pl.ds(j * TILE, TILE))
            under = (pl.ds(j * TILE, TILE), pl.ds(i * TILE, TILE))
            both = joined_ref[over] + joined_ref[under].T
            joined_ref[over] = both
            if i != j:
                joined_ref[under] = both.T


def join_pairs(turned):
    return pl.pallas_call(
        pairs_kernel,
        in_specs=[vmem],
        out_specs=vmem,
        out_shape=jax.ShapeDtypeStruct((ROWS, ROWS), jnp.float32),
        scratch_shapes=[pltpu.VMEM((ROWS, ROWS), jnp.float8_e4m3fn)] * 2,
        compiler_params=params(),
        cost_estimate=cost(3 * 10**9, 4 * 2**20),
        name="join_pairs",
    )(turned)


def held_row(index_ref, slot):
    step = jnp.minimum(index_ref[0, slot], STEPS - 1)
    return pl.multiple_of(step * ROWS + index_ref[2, slot] * TILE, TILE)


def gather_kernel(index_ref, tile_a, tile_b, *refs):
    blocks, (out_ref, held, total, sem) = refs[:STEPS], refs[STEPS:]
    copies = [
        pltpu.make_async_copy(block, held.at[pl.ds(k * ROWS, ROWS)], sem.at[k])
        for k, block in enumerate(blocks)
    ]
    for copy in copies:
        copy.start()
    total[...] = jnp.zeros_like(total)
    for copy in copies:
        copy.wait()
    for slot in range(TILES):
        tile = (tile_a if slot < TILES // 2 else tile_b)[slot % (TILES // 2)]
        source = held_row(index_ref, slot)
        target = pl.multiple_of(index_ref[1, slot] * TILE, TILE)
        total[pl.ds(target, TILE), :] += jnp.dot(
            tile, held[pl.ds(source, TILE), :], preferred_element_type=jnp.float32
        )
    out_ref[...] = total[...].astype(jnp.bfloat16)


def gather_tiles(index, tiles, blocks):
    return pl.pallas_call(
        gather_kernel,
        in_specs=[smem, vmem, vmem] + [anywhere] * STEPS,
        out_specs=vmem,
        out_shape=jax.ShapeDtypeStruct((ROWS, FEAT), jnp.bfloat16),
        scratch_shapes=[
            pltpu.VMEM((STEPS * ROWS, FEAT), jnp.bfloat16),
            pltpu.VMEM((ROWS, FEAT), jnp.float32),
            pltpu.SemaphoreType.DMA((STEPS,)),
        ],
        compiler_params=params(),
        cost_estimate=cost(10**9, 4 * 2**20),
        name="gather_tiles",
    )(index, *tiles, *blocks)


def layer_kernel(
    info_ref, mine_ref, other_ref, deg_mine, deg_other, feat_ref, w_self, w_neigh, bias,
    joined_pos, joined_neg,
    emb_ref, d_self_ref, d_mean_ref, d_weight_ref,
    counts, hidden, scaled, mean, inverse, grad, bias_sum, sem,
):
    copies = [
        pltpu.make_async_copy(ref, counts.at[k], sem.at[k])
        for k, ref in enumerate((joined_pos, joined_neg))
    ]
    for copy in copies:
        copy.start()
    factor = -math.log2(math.e) / math.sqrt(HID)

    def divisor_of(i):
        rows = []
        for k in range(i * PANEL // TILE, (i + 1) * PANEL // TILE):
            row = deg_mine[pl.ds(k, 1), :] + deg_other[pl.ds(k, 1), :]
            rows.append(jnp.broadcast_to(jnp.maximum(row, 1.0), (TILE, TILE)).T)
        return jnp.concatenate(rows, axis=0)

    for i in range(ROWS // PANEL):
        at = pl.ds(i * PANEL, PANEL)
        total = mine_ref[at, :].astype(jnp.float32) + other_ref[at, :].astype(jnp.float32)
        low = (total / divisor_of(i)).astype(jnp.bfloat16)
        mean[at, :] = low
        preact = (
            jnp.dot(feat_ref[at, :], w_self[...], preferred_element_type=jnp.float32)
            + jnp.dot(low, w_neigh[...], preferred_element_type=jnp.float32)
            + bias[...]
        )
        inv = lax.rsqrt(jnp.mean(preact * preact, axis=1, keepdims=True) + norm_eps)
        hid = preact * inv
        hidden[at, :] = hid
        inverse[at, :] = inv
        emb_ref[at, :] = hid.astype(jnp.bfloat16)
        scaled[at, :] = (hid * factor).astype(jnp.bfloat16)

    for copy in copies:
        copy.wait()
    bias_sum[...] = jnp.zeros_like(bias_sum)
    diagonal = lax.broadcasted_iota(jnp.int32, (PANEL, PANEL), 0) == lax.broadcasted_iota(
        jnp.int32, (PANEL, PANEL), 1
    )
    for i in range(ROWS // PANEL):
        at = pl.ds(i * PANEL, PANEL)
        d_hidden = jnp.zeros((PANEL, HID), jnp.float32)
        for j in range(ROWS // PANEL):
            to = pl.ds(j * PANEL, PANEL)
            power = lax.dot_general(
                scaled[at, :], emb_ref[to, :], across, preferred_element_type=jnp.float32
            )
            grown = jnp.exp2(power)
            coef = (counts[1, at, to] - counts[0, at, to] * grown) * pl.reciprocal(
                1.0 + grown, approx=True
            )
            if i == j:
                own = jnp.where(diagonal, coef, 0.0)
                coef = coef - own
                d_hidden += jnp.sum(own, axis=1, keepdims=True) * hidden[at, :]
            d_hidden += jnp.dot(
                coef.astype(jnp.bfloat16), emb_ref[to, :], preferred_element_type=jnp.float32
            )
        d_hidden *= 1.0 / math.sqrt(HID)
        hid = hidden[at, :]
        d_preact = inverse[at, :] * (
            d_hidden - hid * jnp.mean(d_hidden * hid, axis=1, keepdims=True)
        )
        bias_sum[...] += jnp.sum(d_preact.reshape(PANEL // 8, 8, HID), axis=0)
        low = d_preact.astype(jnp.bfloat16)
        grad[at, :] = low
        d_self_ref[at, :] = lax.dot_general(
            low, w_self[...], across, preferred_element_type=jnp.float32
        )
        d_mean_ref[at, :] = (
            lax.dot_general(low, w_neigh[...], across, preferred_element_type=jnp.float32)
            / divisor_of(i)
        ).astype(jnp.bfloat16)
    chosen = jnp.where(
        info_ref[0] == 0, feat_ref[...].astype(jnp.float32), mean[...].astype(jnp.float32)
    )
    d_weight_ref[0:FEAT, :] = lax.dot_general(
        chosen.astype(jnp.bfloat16), grad[...], down, preferred_element_type=jnp.float32
    )
    d_weight_ref[FEAT : FEAT + 8, :] = jnp.broadcast_to(
        jnp.sum(bias_sum[...], axis=0, keepdims=True), (8, HID)
    )
    d_weight_ref[FEAT + 8 :, :] = jnp.zeros((WROWS - FEAT - 8, HID), jnp.float32)


def layer(info, mine, other, deg_mine, deg_other, features, w_self, w_neigh, bias, joined):
    shapes = [
        jax.ShapeDtypeStruct((ROWS, HID), jnp.bfloat16),
        jax.ShapeDtypeStruct((ROWS, FEAT), jnp.float32),
        jax.ShapeDtypeStruct((ROWS, FEAT), jnp.bfloat16),
        jax.ShapeDtypeStruct((WROWS, HID), jnp.float32),
    ]
    return pl.pallas_call(
        layer_kernel,
        in_specs=[smem] + [vmem] * 8 + [anywhere] * 2,
        out_specs=[vmem] * 4,
        out_shape=shapes,
        scratch_shapes=[
            pltpu.VMEM((2, ROWS, ROWS), jnp.float32),
            pltpu.VMEM((ROWS, HID), jnp.float32),
            pltpu.VMEM((ROWS, HID), jnp.bfloat16),
            pltpu.VMEM((ROWS, FEAT), jnp.bfloat16),
            pltpu.VMEM((ROWS, 1), jnp.float32),
            pltpu.VMEM((ROWS, HID), jnp.bfloat16),
            pltpu.VMEM((8, HID), jnp.float32),
            pltpu.SemaphoreType.DMA((2,)),
        ],
        compiler_params=params(),
        cost_estimate=cost(2 * 10**9, 12 * 2**20),
        name="layer",
    )(info, mine, other, deg_mine, deg_other, features, w_self, w_neigh, bias, *joined)


def spread_kernel(index_ref, turned_a, turned_b, grad_ref, *refs):
    outs, (total,) = refs[:STEPS], refs[STEPS:]
    total[...] = jnp.zeros_like(total)
    for slot in range(TILES):
        tile = (turned_a if slot < TILES // 2 else turned_b)[slot % (TILES // 2)]
        target = held_row(index_ref, slot)
        source = pl.multiple_of(index_ref[1, slot] * TILE, TILE)
        total[pl.ds(target, TILE), :] += jnp.dot(
            tile, grad_ref[pl.ds(source, TILE), :], preferred_element_type=jnp.float32
        )
    for k, out in enumerate(outs):
        out[...] = total[k * ROWS : (k + 1) * ROWS, :].astype(jnp.bfloat16)


def spread_tiles(index, turned, d_mean):
    return pl.pallas_call(
        spread_kernel,
        in_specs=[smem, vmem, vmem, vmem],
        out_specs=[vmem] * STEPS,
        out_shape=[jax.ShapeDtypeStruct((ROWS, FEAT), jnp.bfloat16)] * STEPS,
        scratch_shapes=[pltpu.VMEM((STEPS * ROWS, FEAT), jnp.float32)],
        compiler_params=params(),
        cost_estimate=cost(10**9, 4 * 2**20),
        name="spread_tiles",
    )(index, *turned, d_mean)


def flipped(value, mask):
    return shifted(value, lambda block, rep: (block ^ mask, rep))


def added(left, right):
    return (left.astype(jnp.float32) + right.astype(jnp.float32)).astype(jnp.bfloat16)


def body(features, tile_index, tile_counts, w_self, w_neigh, bias, pos_pairs, neg_pairs):
    block, rep = lax.axis_index("blk"), lax.axis_index("rep")
    core = block & 1
    index, counts = tile_index[0, 0], tile_counts[0, 0]
    info = rep.reshape(1).astype(jnp.int32)
    pos_turned, neg_turned = pos_pairs.T, neg_pairs.T

    held = {s: from_step(features, s) for s in (4, 1, 3, 2, 0)}
    tiles_a, turned_a, degree = prepare_tiles(index, jnp.zeros((8, TILE), jnp.float32), counts, 0, 2)
    tiles_b, turned_b, degree = prepare_tiles(index, degree, counts, 1, 2)
    held[1], degree = tied((held[1], degree), turned_b)
    held[5] = from_before(held[1])
    (pos_turned,) = tied((pos_turned,), held[1])
    joined_pos = join_pairs(pos_turned)
    held[3], degree = tied((held[3], degree), joined_pos, held[4])
    held[7] = from_before(held[3])
    (held[2],) = tied((held[2],), held[5], held[3])
    held[6] = from_before(held[2])
    degree_other = shifted(degree, lambda b, r: (b, 1 - r))
    mine = gather_tiles(index, (tiles_a, tiles_b), [held[s] for s in range(STEPS)])
    other = shifted(mine, lambda b, r: (b, 1 - r))
    (neg_turned,) = tied((neg_turned,), mine)
    joined_neg = join_pairs(neg_turned)

    embeddings, d_self, d_mean, d_weight = layer(
        info, mine, other, degree, degree_other,
        features, w_self, w_neigh, bias.reshape(1, HID), (joined_pos, joined_neg),
    )

    rows = d_weight.shape[0] // 2
    kept = lax.dynamic_slice_in_dim(d_weight, core * rows, rows, 0)
    given = lax.dynamic_slice_in_dim(d_weight, (1 - core) * rows, rows, 0)
    given = flipped(given, 1)
    spread = spread_tiles(index, (turned_a, turned_b), d_mean)
    order = (2, 1, 3)
    back = {s: to_before(spread[s + NEAR]) for s in order}
    landed = {NEAR: to_step(spread[NEAR], NEAR)}
    kept, given = tied((kept, given), spread[0])
    once = 1 + jnp.minimum(rep, 0)

    def summed_over(value, *shifts):
        def one_pass(_, value):
            for shift in shifts:
                value = value + flipped(value, 1 << shift)
            return value

        return lax.fori_loop(0, once, one_pass, value)

    summed = summed_over(kept + given, 5, 6, 1, 2)
    later = tied([back[s] for s in order], landed[NEAR], summed)
    near = {s: added(spread[s], value) for s, value in zip(order, later)}
    near[0] = spread[0]
    landed.update({s: to_step(value, s) for s, value in near.items()})
    (summed,) = tied((summed,), *near.values())

    def last_pass(_, value):
        value = value[:rows]
        for shift in (3, 4):
            value = value + flipped(value, 1 << shift)
        traded = flipped(value, 1)
        return jnp.concatenate(
            [jnp.where(core == 0, value, traded), jnp.where(core == 0, traded, value)], axis=0
        )

    d_here = lax.fori_loop(0, once, last_pass, jnp.concatenate([summed, summed], axis=0))
    arrived = tied([landed[s] for s in (0, 4, 2, 1, 3)], d_here)
    arrived = [value.astype(jnp.float32) for value in arrived]
    partial = (arrived[0] + arrived[1]) + arrived[2] + (arrived[3] + arrived[4])
    partial = partial.astype(jnp.bfloat16)
    partial_other = shifted(partial, lambda b, r: (b, 1 - r))
    (given,) = tied((d_here,), partial)
    d_there = shifted(given[:FEAT], lambda b, r: (b, 1 - r))
    d_features = d_self + (partial.astype(jnp.float32) + partial_other.astype(jnp.float32))
    d_w_self = jnp.where(rep == 0, d_here[:FEAT], d_there)
    d_w_neigh = jnp.where(rep == 0, d_there, d_here[:FEAT])
    return (embeddings, d_features, d_w_self, d_w_neigh, d_here[FEAT])


def solution(mesh):
    return jax.shard_map(
        body,
        mesh=mesh,
        in_specs=(
            P("blk", None),
            P("blk", "rep", None, None),
            P("blk", "rep", None, None, None),
            P(),
            P(),
            P(),
            P("blk", None),
            P("blk", None),
        ),
        out_specs=(P("blk", None), P("blk", None), P(), P(), P()),
        check_vma=False,
    )
```

```python
import math

import jax
import jax.numpy as jnp
from jax import lax
from jax.experimental import pallas as pl
from jax.experimental.pallas import tpu as pltpu
from jax.sharding import PartitionSpec as P

STEPS = 8
TILE = 128
ROWS = 1024
FEAT = 128
HID = 256
TILES = 64
BLOCKS = 128
REPS = 2
GROUP = 8
NEAR = STEPS // 2
WROWS = 144
PANEL = 256
norm_eps = 1e-05
VMEM_LIMIT = 56 * 1024 * 1024
across = (((1,), (1,)), ((), ()))
down = (((0,), (0,)), ((), ()))

vmem = pl.BlockSpec(memory_space=pltpu.VMEM)
smem = pl.BlockSpec(memory_space=pltpu.SMEM)
anywhere = pl.BlockSpec(memory_space=pl.ANY)


def params():
    return pltpu.CompilerParams(vmem_limit_bytes=VMEM_LIMIT)


def cost(flops, bytes_accessed):
    return pl.CostEstimate(flops=flops, bytes_accessed=bytes_accessed, transcendentals=0)


def shifted(value, source_of):
    route = []
    for block in range(BLOCKS):
        for rep in range(REPS):
            source = source_of(block, rep)
            if source is not None:
                route.append(((source[0] % BLOCKS) * REPS + source[1], block * REPS + rep))
    return lax.ppermute(value, ("blk", "rep"), route)


def from_step(value, step):
    return shifted(value, lambda block, rep: (block - rep - 2 * step, rep))


def to_step(value, step):
    return shifted(value, lambda block, rep: (block + rep + 2 * step, rep))


def from_before(value):
    return shifted(value, lambda block, rep: (block - STEPS, rep))


def to_before(value):
    return shifted(value, lambda block, rep: (block + STEPS, rep))


def tied(values, *others):
    flat = lax.optimization_barrier(tuple(values) + tuple(others))
    return flat[: len(values)]


def tiles_kernel(first, index_ref, before_ref, counts_ref, tile_ref, turned_ref, degree_ref, sums):
    group = pl.program_id(0)

    @pl.when(group == 0)
    def _():
        sums[...] = jnp.zeros_like(sums)

    ones = jnp.ones((8, TILE), jnp.bfloat16)
    for k in range(GROUP):
        slot = first + group * GROUP + k
        used = index_ref[0, slot] < STEPS
        counts = jnp.where(used, counts_ref[k], 0).astype(jnp.float32)
        turned = counts.T.astype(jnp.bfloat16)
        tile_ref[k] = counts.astype(jnp.bfloat16)
        turned_ref[k] = turned
        row = index_ref[1, slot]
        sums[row] += jnp.dot(ones, turned, preferred_element_type=jnp.float32)

    @pl.when(group == pl.num_programs(0) - 1)
    def _():
        degree_ref[...] = before_ref[...] + sums[:, 0, :]


def prepare_tiles(index, before, counts, part, parts):
    share = TILES // parts
    spec = pl.BlockSpec((GROUP, TILE, TILE), lambda g: (g, 0, 0))
    shape = jax.ShapeDtypeStruct((share, TILE, TILE), jnp.bfloat16)
    whole = pl.BlockSpec((8, TILE), lambda g: (0, 0))
    return pl.pallas_call(
        lambda *refs: tiles_kernel(part * share, *refs),
        grid=(share // GROUP,),
        in_specs=[
            smem,
            whole,
            pl.BlockSpec((GROUP, TILE, TILE), lambda g: (g + part * share // GROUP, 0, 0)),
        ],
        out_specs=[spec, spec, whole],
        out_shape=[shape, shape, jax.ShapeDtypeStruct((8, TILE), jnp.float32)],
        scratch_shapes=[pltpu.VMEM((8, 8, TILE), jnp.float32)],
        compiler_params=params(),
        cost_estimate=cost(10**9, 8 * 2**20),
        name="prepare_tiles",
    )(index, before, counts)


def pairs_kernel(turned, joined_ref, left, right):
    def fill(i, carry):
        at = pl.ds(pl.multiple_of(i * TILE, TILE), TILE)
        rows = lax.broadcasted_iota(jnp.int32, (TILE, ROWS), 0) + i * TILE
        left[at, :] = (turned[0:1, :] == rows).astype(jnp.float32).astype(left.dtype)
        right[at, :] = (turned[1:2, :] == rows).astype(jnp.float32).astype(right.dtype)
        return carry

    lax.fori_loop(0, ROWS // TILE, fill, 0)
    for i in range(ROWS // PANEL):
        at = pl.ds(i * PANEL, PANEL)
        joined_ref[at, :] = lax.dot_general(
            left[at, :], right[...], across, preferred_element_type=jnp.float32
        )
    for i in range(ROWS // TILE):
        for j in range(i, ROWS // TILE):
            over = (pl.ds(i * TILE, TILE), pl.ds(j * TILE, TILE))
            under = (pl.ds(j * TILE, TILE), pl.ds(i * TILE, TILE))
            both = joined_ref[over] + joined_ref[under].T
            joined_ref[over] = both
            if i != j:
                joined_ref[under] = both.T


def join_pairs(turned):
    return pl.pallas_call(
        pairs_kernel,
        in_specs=[vmem],
        out_specs=vmem,
        out_shape=jax.ShapeDtypeStruct((ROWS, ROWS), jnp.float32),
        scratch_shapes=[pltpu.VMEM((ROWS, ROWS), jnp.float8_e4m3fn)] * 2,
        compiler_params=params(),
        cost_estimate=cost(3 * 10**9, 4 * 2**20),
        name="join_pairs",
    )(turned)


def held_row(index_ref, slot):
    step = jnp.minimum(index_ref[0, slot], STEPS - 1)
    return pl.multiple_of(step * ROWS + index_ref[2, slot] * TILE, TILE)


def gather_kernel(index_ref, tile_a, tile_b, *refs):
    blocks, (out_ref, held, total, sem) = refs[:STEPS], refs[STEPS:]
    copies = [
        pltpu.make_async_copy(block, held.at[pl.ds(k * ROWS, ROWS)], sem.at[k])
        for k, block in enumerate(blocks)
    ]
    for copy in copies:
        copy.start()
    total[...] = jnp.zeros_like(total)
    for copy in copies:
        copy.wait()
    for slot in range(TILES):
        tile = (tile_a if slot < TILES // 2 else tile_b)[slot % (TILES // 2)]
        source = held_row(index_ref, slot)
        target = pl.multiple_of(index_ref[1, slot] * TILE, TILE)
        total[pl.ds(target, TILE), :] += jnp.dot(
            tile, held[pl.ds(source, TILE), :], preferred_element_type=jnp.float32
        )
    out_ref[...] = total[...].astype(jnp.bfloat16)


def gather_tiles(index, tiles, blocks):
    return pl.pallas_call(
        gather_kernel,
        in_specs=[smem, vmem, vmem] + [anywhere] * STEPS,
        out_specs=vmem,
        out_shape=jax.ShapeDtypeStruct((ROWS, FEAT), jnp.bfloat16),
        scratch_shapes=[
            pltpu.VMEM((STEPS * ROWS, FEAT), jnp.bfloat16),
            pltpu.VMEM((ROWS, FEAT), jnp.float32),
            pltpu.SemaphoreType.DMA((STEPS,)),
        ],
        compiler_params=params(),
        cost_estimate=cost(10**9, 4 * 2**20),
        name="gather_tiles",
    )(index, *tiles, *blocks)


def layer_kernel(
    info_ref, mine_ref, other_ref, deg_mine, deg_other, feat_ref, w_self, w_neigh, bias,
    joined_pos, joined_neg,
    emb_ref, d_self_ref, d_mean_ref, d_weight_ref,
    counts, hidden, scaled, mean, inverse, grad, bias_sum, sem,
):
    copies = [
        pltpu.make_async_copy(ref, counts.at[k], sem.at[k])
        for k, ref in enumerate((joined_pos, joined_neg))
    ]
    for copy in copies:
        copy.start()
    factor = -math.log2(math.e) / math.sqrt(HID)

    def divisor_of(i):
        rows = []
        for k in range(i * PANEL // TILE, (i + 1) * PANEL // TILE):
            row = deg_mine[pl.ds(k, 1), :] + deg_other[pl.ds(k, 1), :]
            rows.append(jnp.broadcast_to(jnp.maximum(row, 1.0), (TILE, TILE)).T)
        return jnp.concatenate(rows, axis=0)

    for i in range(ROWS // PANEL):
        at = pl.ds(i * PANEL, PANEL)
        total = mine_ref[at, :].astype(jnp.float32) + other_ref[at, :].astype(jnp.float32)
        low = (total / divisor_of(i)).astype(jnp.bfloat16)
        mean[at, :] = low
        preact = (
            jnp.dot(feat_ref[at, :], w_self[...], preferred_element_type=jnp.float32)
            + jnp.dot(low, w_neigh[...], preferred_element_type=jnp.float32)
            + bias[...]
        )
        inv = lax.rsqrt(jnp.mean(preact * preact, axis=1, keepdims=True) + norm_eps)
        hid = preact * inv
        hidden[at, :] = hid
        inverse[at, :] = inv
        emb_ref[at, :] = hid.astype(jnp.bfloat16)
        scaled[at, :] = (hid * factor).astype(jnp.bfloat16)

    for copy in copies:
        copy.wait()
    bias_sum[...] = jnp.zeros_like(bias_sum)
    diagonal = lax.broadcasted_iota(jnp.int32, (PANEL, PANEL), 0) == lax.broadcasted_iota(
        jnp.int32, (PANEL, PANEL), 1
    )
    for i in range(ROWS // PANEL):
        at = pl.ds(i * PANEL, PANEL)
        d_hidden = jnp.zeros((PANEL, HID), jnp.float32)
        for j in range(ROWS // PANEL):
            to = pl.ds(j * PANEL, PANEL)
            power = lax.dot_general(
                scaled[at, :], emb_ref[to, :], across, preferred_element_type=jnp.float32
            )
            grown = jnp.exp2(power)
            coef = (counts[1, at, to] - counts[0, at, to] * grown) * pl.reciprocal(
                1.0 + grown, approx=True
            )
            if i == j:
                own = jnp.where(diagonal, coef, 0.0)
                coef = coef - own
                d_hidden += jnp.sum(own, axis=1, keepdims=True) * hidden[at, :]
            d_hidden += jnp.dot(
                coef.astype(jnp.bfloat16), emb_ref[to, :], preferred_element_type=jnp.float32
            )
        d_hidden *= 1.0 / math.sqrt(HID)
        hid = hidden[at, :]
        d_preact = inverse[at, :] * (
            d_hidden - hid * jnp.mean(d_hidden * hid, axis=1, keepdims=True)
        )
        bias_sum[...] += jnp.sum(d_preact.reshape(PANEL // 8, 8, HID), axis=0)
        low = d_preact.astype(jnp.bfloat16)
        grad[at, :] = low
        d_self_ref[at, :] = lax.dot_general(
            low, w_self[...], across, preferred_element_type=jnp.float32
        )
        d_mean_ref[at, :] = (
            lax.dot_general(low, w_neigh[...], across, preferred_element_type=jnp.float32)
            / divisor_of(i)
        ).astype(jnp.bfloat16)
    chosen = jnp.where(
        info_ref[0] == 0, feat_ref[...].astype(jnp.float32), mean[...].astype(jnp.float32)
    )
    d_weight_ref[0:FEAT, :] = lax.dot_general(
        chosen.astype(jnp.bfloat16), grad[...], down, preferred_element_type=jnp.float32
    )
    d_weight_ref[FEAT : FEAT + 8, :] = jnp.broadcast_to(
        jnp.sum(bias_sum[...], axis=0, keepdims=True), (8, HID)
    )
    d_weight_ref[FEAT + 8 :, :] = jnp.zeros((WROWS - FEAT - 8, HID), jnp.float32)


def layer(info, mine, other, deg_mine, deg_other, features, w_self, w_neigh, bias, joined):
    shapes = [
        jax.ShapeDtypeStruct((ROWS, HID), jnp.bfloat16),
        jax.ShapeDtypeStruct((ROWS, FEAT), jnp.float32),
        jax.ShapeDtypeStruct((ROWS, FEAT), jnp.bfloat16),
        jax.ShapeDtypeStruct((WROWS, HID), jnp.float32),
    ]
    return pl.pallas_call(
        layer_kernel,
        in_specs=[smem] + [vmem] * 8 + [anywhere] * 2,
        out_specs=[vmem] * 4,
        out_shape=shapes,
        scratch_shapes=[
            pltpu.VMEM((2, ROWS, ROWS), jnp.float32),
            pltpu.VMEM((ROWS, HID), jnp.float32),
            pltpu.VMEM((ROWS, HID), jnp.bfloat16),
            pltpu.VMEM((ROWS, FEAT), jnp.bfloat16),
            pltpu.VMEM((ROWS, 1), jnp.float32),
            pltpu.VMEM((ROWS, HID), jnp.bfloat16),
            pltpu.VMEM((8, HID), jnp.float32),
            pltpu.SemaphoreType.DMA((2,)),
        ],
        compiler_params=params(),
        cost_estimate=cost(2 * 10**9, 12 * 2**20),
        name="layer",
    )(info, mine, other, deg_mine, deg_other, features, w_self, w_neigh, bias, *joined)


def spread_kernel(index_ref, turned_a, turned_b, grad_ref, *refs):
    outs, (total,) = refs[:STEPS], refs[STEPS:]
    total[...] = jnp.zeros_like(total)
    for slot in range(TILES):
        tile = (turned_a if slot < TILES // 2 else turned_b)[slot % (TILES // 2)]
        target = held_row(index_ref, slot)
        source = pl.multiple_of(index_ref[1, slot] * TILE, TILE)
        total[pl.ds(target, TILE), :] += jnp.dot(
            tile, grad_ref[pl.ds(source, TILE), :], preferred_element_type=jnp.float32
        )
    for k, out in enumerate(outs):
        out[...] = total[k * ROWS : (k + 1) * ROWS, :].astype(jnp.bfloat16)


def spread_tiles(index, turned, d_mean):
    return pl.pallas_call(
        spread_kernel,
        in_specs=[smem, vmem, vmem, vmem],
        out_specs=[vmem] * STEPS,
        out_shape=[jax.ShapeDtypeStruct((ROWS, FEAT), jnp.bfloat16)] * STEPS,
        scratch_shapes=[pltpu.VMEM((STEPS * ROWS, FEAT), jnp.float32)],
        compiler_params=params(),
        cost_estimate=cost(10**9, 4 * 2**20),
        name="spread_tiles",
    )(index, *turned, d_mean)


def flipped(value, mask):
    return shifted(value, lambda block, rep: (block ^ mask, rep))


def added(left, right):
    return (left.astype(jnp.float32) + right.astype(jnp.float32)).astype(jnp.bfloat16)


def body(features, tile_index, tile_counts, w_self, w_neigh, bias, pos_pairs, neg_pairs):
    block, rep = lax.axis_index("blk"), lax.axis_index("rep")
    core = block & 1
    index, counts = tile_index[0, 0], tile_counts[0, 0]
    info = rep.reshape(1).astype(jnp.int32)
    pos_turned, neg_turned = pos_pairs.T, neg_pairs.T

    held = {s: from_step(features, s) for s in (4, 1, 3, 2, 0)}
    tiles_a, turned_a, degree = prepare_tiles(index, jnp.zeros((8, TILE), jnp.float32), counts, 0, 2)
    tiles_b, turned_b, degree = prepare_tiles(index, degree, counts, 1, 2)
    held[1], degree = tied((held[1], degree), turned_b)
    held[5] = from_before(held[1])
    (held[3],) = tied((held[3],), held[4])
    held[7] = from_before(held[3])
    (held[2],) = tied((held[2],), held[5], held[3])
    held[6] = from_before(held[2])
    (pos_turned,) = tied((pos_turned,), held[2])
    joined_pos = join_pairs(pos_turned)
    (degree,) = tied((degree,), joined_pos)
    degree_other = shifted(degree, lambda b, r: (b, 1 - r))
    mine = gather_tiles(index, (tiles_a, tiles_b), [held[s] for s in range(STEPS)])
    other = shifted(mine, lambda b, r: (b, 1 - r))
    (neg_turned,) = tied((neg_turned,), mine)
    joined_neg = join_pairs(neg_turned)

    embeddings, d_self, d_mean, d_weight = layer(
        info, mine, other, degree, degree_other,
        features, w_self, w_neigh, bias.reshape(1, HID), (joined_pos, joined_neg),
    )

    rows = d_weight.shape[0] // 2
    kept = lax.dynamic_slice_in_dim(d_weight, core * rows, rows, 0)
    given = lax.dynamic_slice_in_dim(d_weight, (1 - core) * rows, rows, 0)
    given = flipped(given, 1)
    (d_mean,) = tied((d_mean,), given)
    spread = spread_tiles(index, (turned_a, turned_b), d_mean)
    order = (2, 1, 3)
    back = {s: to_before(spread[s + NEAR]) for s in order}
    landed = {NEAR: to_step(spread[NEAR], NEAR)}
    once = 1 + jnp.minimum(rep, 0)

    def summed_over(value, *shifts):
        def one_pass(_, value):
            for shift in shifts:
                value = value + flipped(value, 1 << shift)
            return value

        return lax.fori_loop(0, once, one_pass, value)

    summed = summed_over(kept + given, 5, 6, 1, 2)
    later = tied([back[s] for s in order], landed[NEAR], summed)
    near = {s: added(spread[s], value) for s, value in zip(order, later)}
    near[0] = spread[0]
    landed.update({s: to_step(value, s) for s, value in near.items()})
    (summed,) = tied((summed,), *near.values())

    def last_pass(_, state):
        value = state[0][:rows]
        for shift in (3, 4):
            value = value + flipped(value, 1 << shift)
        traded = flipped(value, 1)
        value = jnp.concatenate(
            [jnp.where(core == 0, value, traded), jnp.where(core == 0, traded, value)], axis=0
        )
        return value, shifted(value[:FEAT], lambda b, r: (b, 1 - r))

    d_here = jnp.concatenate([summed, summed], axis=0)
    d_here, d_there = lax.fori_loop(0, once, last_pass, (d_here, d_here[:FEAT]))
    arrived = tied([landed[s] for s in (0, 4, 2, 1, 3)], d_there)
    arrived = [value.astype(jnp.float32) for value in arrived]
    partial = (arrived[0] + arrived[1]) + arrived[2] + (arrived[3] + arrived[4])
    partial = partial.astype(jnp.bfloat16)
    partial_other = shifted(partial, lambda b, r: (b, 1 - r))
    d_features = d_self + (partial.astype(jnp.float32) + partial_other.astype(jnp.float32))
    (d_there,) = tied((d_there,), partial)
    d_w_self = jnp.where(rep == 0, d_here[:FEAT], d_there)
    d_w_neigh = jnp.where(rep == 0, d_there, d_here[:FEAT])
    return (embeddings, d_features, d_w_self, d_w_neigh, d_here[FEAT])


def solution(mesh):
    return jax.shard_map(
        body,
        mesh=mesh,
        in_specs=(
            P("blk", None),
            P("blk", "rep", None, None),
            P("blk", "rep", None, None, None),
            P(),
            P(),
            P(),
            P("blk", None),
            P("blk", None),
        ),
        out_specs=(P("blk", None), P("blk", None), P(), P(), P()),
        check_vma=False,
    )
```

```python
import math

import jax
import jax.numpy as jnp
from jax import lax
from jax.experimental import pallas as pl
from jax.experimental.pallas import tpu as pltpu
from jax.sharding import PartitionSpec as P

STEPS = 8
TILE = 128
ROWS = 1024
FEAT = 128
HID = 256
TILES = 64
BLOCKS = 128
REPS = 2
GROUP = 8
NEAR = STEPS // 2
WROWS = 144
PANEL = 256
norm_eps = 1e-05
VMEM_LIMIT = 56 * 1024 * 1024
across = (((1,), (1,)), ((), ()))
down = (((0,), (0,)), ((), ()))

vmem = pl.BlockSpec(memory_space=pltpu.VMEM)
smem = pl.BlockSpec(memory_space=pltpu.SMEM)
anywhere = pl.BlockSpec(memory_space=pl.ANY)


def params():
    return pltpu.CompilerParams(vmem_limit_bytes=VMEM_LIMIT)


def cost(flops, bytes_accessed):
    return pl.CostEstimate(flops=flops, bytes_accessed=bytes_accessed, transcendentals=0)


def shifted(value, source_of):
    route = []
    for block in range(BLOCKS):
        for rep in range(REPS):
            source = source_of(block, rep)
            if source is not None:
                route.append(((source[0] % BLOCKS) * REPS + source[1], block * REPS + rep))
    return lax.ppermute(value, ("blk", "rep"), route)


def from_step(value, step):
    return shifted(value, lambda block, rep: (block - rep - 2 * step, rep))


def to_step(value, step):
    return shifted(value, lambda block, rep: (block + rep + 2 * step, rep))


def from_before(value):
    return shifted(value, lambda block, rep: (block - STEPS, rep))


def to_before(value):
    return shifted(value, lambda block, rep: (block + STEPS, rep))


def tied(values, *others):
    flat = lax.optimization_barrier(tuple(values) + tuple(others))
    return flat[: len(values)]


def tiles_kernel(first, index_ref, before_ref, counts_ref, tile_ref, turned_ref, degree_ref, sums):
    group = pl.program_id(0)

    @pl.when(group == 0)
    def _():
        sums[...] = jnp.zeros_like(sums)

    ones = jnp.ones((8, TILE), jnp.bfloat16)
    for k in range(GROUP):
        slot = first + group * GROUP + k
        used = index_ref[0, slot] < STEPS
        counts = jnp.where(used, counts_ref[k], 0).astype(jnp.float32)
        turned = counts.T.astype(jnp.bfloat16)
        tile_ref[k] = counts.astype(jnp.bfloat16)
        turned_ref[k] = turned
        row = index_ref[1, slot]
        sums[row] += jnp.dot(ones, turned, preferred_element_type=jnp.float32)

    @pl.when(group == pl.num_programs(0) - 1)
    def _():
        degree_ref[...] = before_ref[...] + sums[:, 0, :]


def prepare_tiles(index, before, counts, part, parts):
    share = TILES // parts
    spec = pl.BlockSpec((GROUP, TILE, TILE), lambda g: (g, 0, 0))
    shape = jax.ShapeDtypeStruct((share, TILE, TILE), jnp.bfloat16)
    whole = pl.BlockSpec((8, TILE), lambda g: (0, 0))
    return pl.pallas_call(
        lambda *refs: tiles_kernel(part * share, *refs),
        grid=(share // GROUP,),
        in_specs=[
            smem,
            whole,
            pl.BlockSpec((GROUP, TILE, TILE), lambda g: (g + part * share // GROUP, 0, 0)),
        ],
        out_specs=[spec, spec, whole],
        out_shape=[shape, shape, jax.ShapeDtypeStruct((8, TILE), jnp.float32)],
        scratch_shapes=[pltpu.VMEM((8, 8, TILE), jnp.float32)],
        compiler_params=params(),
        cost_estimate=cost(10**9, 8 * 2**20),
        name="prepare_tiles",
    )(index, before, counts)


def pairs_kernel(turned, joined_ref, left, right):
    def fill(i, carry):
        at = pl.ds(pl.multiple_of(i * TILE, TILE), TILE)
        rows = lax.broadcasted_iota(jnp.int32, (TILE, ROWS), 0) + i * TILE
        left[at, :] = (turned[0:1, :] == rows).astype(jnp.float32).astype(left.dtype)
        right[at, :] = (turned[1:2, :] == rows).astype(jnp.float32).astype(right.dtype)
        return carry

    lax.fori_loop(0, ROWS // TILE, fill, 0)
    for i in range(ROWS // PANEL):
        at = pl.ds(i * PANEL, PANEL)
        joined_ref[at, :] = lax.dot_general(
            left[at, :], right[...], across, preferred_element_type=jnp.float32
        )
    for i in range(ROWS // TILE):
        for j in range(i, ROWS // TILE):
            over = (pl.ds(i * TILE, TILE), pl.ds(j * TILE, TILE))
            under = (pl.ds(j * TILE, TILE), pl.ds(i * TILE, TILE))
            both = joined_ref[over] + joined_ref[under].T
            joined_ref[over] = both
            if i != j:
                joined_ref[under] = both.T


def join_pairs(turned):
    return pl.pallas_call(
        pairs_kernel,
        in_specs=[vmem],
        out_specs=vmem,
        out_shape=jax.ShapeDtypeStruct((ROWS, ROWS), jnp.float32),
        scratch_shapes=[pltpu.VMEM((ROWS, ROWS), jnp.float8_e4m3fn)] * 2,
        compiler_params=params(),
        cost_estimate=cost(3 * 10**9, 4 * 2**20),
        name="join_pairs",
    )(turned)


def held_row(index_ref, slot):
    step = jnp.minimum(index_ref[0, slot], STEPS - 1)
    return pl.multiple_of(step * ROWS + index_ref[2, slot] * TILE, TILE)


def gather_kernel(index_ref, tile_a, tile_b, *refs):
    blocks, (out_ref, held, total, sem) = refs[:STEPS], refs[STEPS:]
    copies = [
        pltpu.make_async_copy(block, held.at[pl.ds(k * ROWS, ROWS)], sem.at[k])
        for k, block in enumerate(blocks)
    ]
    for copy in copies:
        copy.start()
    total[...] = jnp.zeros_like(total)
    for copy in copies:
        copy.wait()
    for slot in range(TILES):
        tile = (tile_a if slot < TILES // 2 else tile_b)[slot % (TILES // 2)]
        source = held_row(index_ref, slot)
        target = pl.multiple_of(index_ref[1, slot] * TILE, TILE)
        total[pl.ds(target, TILE), :] += jnp.dot(
            tile, held[pl.ds(source, TILE), :], preferred_element_type=jnp.float32
        )
    out_ref[...] = total[...].astype(jnp.bfloat16)


def gather_tiles(index, tiles, blocks):
    return pl.pallas_call(
        gather_kernel,
        in_specs=[smem, vmem, vmem] + [anywhere] * STEPS,
        out_specs=vmem,
        out_shape=jax.ShapeDtypeStruct((ROWS, FEAT), jnp.bfloat16),
        scratch_shapes=[
            pltpu.VMEM((STEPS * ROWS, FEAT), jnp.bfloat16),
            pltpu.VMEM((ROWS, FEAT), jnp.float32),
            pltpu.SemaphoreType.DMA((STEPS,)),
        ],
        compiler_params=params(),
        cost_estimate=cost(10**9, 4 * 2**20),
        name="gather_tiles",
    )(index, *tiles, *blocks)


def layer_kernel(
    info_ref, mine_ref, other_ref, deg_mine, deg_other, feat_ref, w_self, w_neigh, bias,
    joined_pos, joined_neg,
    emb_ref, d_self_ref, d_mean_ref, d_weight_ref,
    counts, hidden, scaled, mean, inverse, grad, bias_sum, sem,
):
    copies = [
        pltpu.make_async_copy(ref, counts.at[k], sem.at[k])
        for k, ref in enumerate((joined_pos, joined_neg))
    ]
    for copy in copies:
        copy.start()
    factor = -math.log2(math.e) / math.sqrt(HID)

    def divisor_of(i):
        rows = []
        for k in range(i * PANEL // TILE, (i + 1) * PANEL // TILE):
            row = deg_mine[pl.ds(k, 1), :] + deg_other[pl.ds(k, 1), :]
            rows.append(jnp.broadcast_to(jnp.maximum(row, 1.0), (TILE, TILE)).T)
        return jnp.concatenate(rows, axis=0)

    for i in range(ROWS // PANEL):
        at = pl.ds(i * PANEL, PANEL)
        total = mine_ref[at, :].astype(jnp.float32) + other_ref[at, :].astype(jnp.float32)
        low = (total / divisor_of(i)).astype(jnp.bfloat16)
        mean[at, :] = low
        preact = (
            jnp.dot(feat_ref[at, :], w_self[...], preferred_element_type=jnp.float32)
            + jnp.dot(low, w_neigh[...], preferred_element_type=jnp.float32)
            + bias[...]
        )
        inv = lax.rsqrt(jnp.mean(preact * preact, axis=1, keepdims=True) + norm_eps)
        hid = preact * inv
        hidden[at, :] = hid
        inverse[at, :] = inv
        emb_ref[at, :] = hid.astype(jnp.bfloat16)
        scaled[at, :] = (hid * factor).astype(jnp.bfloat16)

    for copy in copies:
        copy.wait()
    bias_sum[...] = jnp.zeros_like(bias_sum)
    diagonal = lax.broadcasted_iota(jnp.int32, (PANEL, PANEL), 0) == lax.broadcasted_iota(
        jnp.int32, (PANEL, PANEL), 1
    )
    for i in range(ROWS // PANEL):
        at = pl.ds(i * PANEL, PANEL)
        d_hidden = jnp.zeros((PANEL, HID), jnp.float32)
        for j in range(ROWS // PANEL):
            to = pl.ds(j * PANEL, PANEL)
            power = lax.dot_general(
                scaled[at, :], emb_ref[to, :], across, preferred_element_type=jnp.float32
            )
            grown = jnp.exp2(power)
            coef = (counts[1, at, to] - counts[0, at, to] * grown) * pl.reciprocal(
                1.0 + grown, approx=True
            )
            if i == j:
                own = jnp.where(diagonal, coef, 0.0)
                coef = coef - own
                d_hidden += jnp.sum(own, axis=1, keepdims=True) * hidden[at, :]
            d_hidden += jnp.dot(
                coef.astype(jnp.bfloat16), emb_ref[to, :], preferred_element_type=jnp.float32
            )
        d_hidden *= 1.0 / math.sqrt(HID)
        hid = hidden[at, :]
        d_preact = inverse[at, :] * (
            d_hidden - hid * jnp.mean(d_hidden * hid, axis=1, keepdims=True)
        )
        bias_sum[...] += jnp.sum(d_preact.reshape(PANEL // 8, 8, HID), axis=0)
        low = d_preact.astype(jnp.bfloat16)
        grad[at, :] = low
        d_self_ref[at, :] = lax.dot_general(
            low, w_self[...], across, preferred_element_type=jnp.float32
        )
        d_mean_ref[at, :] = (
            lax.dot_general(low, w_neigh[...], across, preferred_element_type=jnp.float32)
            / divisor_of(i)
        ).astype(jnp.bfloat16)
    chosen = jnp.where(
        info_ref[0] == 0, feat_ref[...].astype(jnp.float32), mean[...].astype(jnp.float32)
    )
    d_weight_ref[0:FEAT, :] = lax.dot_general(
        chosen.astype(jnp.bfloat16), grad[...], down, preferred_element_type=jnp.float32
    )
    d_weight_ref[FEAT : FEAT + 8, :] = jnp.broadcast_to(
        jnp.sum(bias_sum[...], axis=0, keepdims=True), (8, HID)
    )
    d_weight_ref[FEAT + 8 :, :] = jnp.zeros((WROWS - FEAT - 8, HID), jnp.float32)


def layer(info, mine, other, deg_mine, deg_other, features, w_self, w_neigh, bias, joined):
    shapes = [
        jax.ShapeDtypeStruct((ROWS, HID), jnp.bfloat16),
        jax.ShapeDtypeStruct((ROWS, FEAT), jnp.float32),
        jax.ShapeDtypeStruct((ROWS, FEAT), jnp.bfloat16),
        jax.ShapeDtypeStruct((WROWS, HID), jnp.float32),
    ]
    return pl.pallas_call(
        layer_kernel,
        in_specs=[smem] + [vmem] * 8 + [anywhere] * 2,
        out_specs=[vmem] * 4,
        out_shape=shapes,
        scratch_shapes=[
            pltpu.VMEM((2, ROWS, ROWS), jnp.float32),
            pltpu.VMEM((ROWS, HID), jnp.float32),
            pltpu.VMEM((ROWS, HID), jnp.bfloat16),
            pltpu.VMEM((ROWS, FEAT), jnp.bfloat16),
            pltpu.VMEM((ROWS, 1), jnp.float32),
            pltpu.VMEM((ROWS, HID), jnp.bfloat16),
            pltpu.VMEM((8, HID), jnp.float32),
            pltpu.SemaphoreType.DMA((2,)),
        ],
        compiler_params=params(),
        cost_estimate=cost(2 * 10**9, 12 * 2**20),
        name="layer",
    )(info, mine, other, deg_mine, deg_other, features, w_self, w_neigh, bias, *joined)


def spread_kernel(index_ref, turned_a, turned_b, grad_ref, *refs):
    outs, (total,) = refs[:STEPS], refs[STEPS:]
    total[...] = jnp.zeros_like(total)
    for slot in range(TILES):
        tile = (turned_a if slot < TILES // 2 else turned_b)[slot % (TILES // 2)]
        target = held_row(index_ref, slot)
        source = pl.multiple_of(index_ref[1, slot] * TILE, TILE)
        total[pl.ds(target, TILE), :] += jnp.dot(
            tile, grad_ref[pl.ds(source, TILE), :], preferred_element_type=jnp.float32
        )
    for k, out in enumerate(outs):
        out[...] = total[k * ROWS : (k + 1) * ROWS, :].astype(jnp.bfloat16)


def spread_tiles(index, turned, d_mean):
    return pl.pallas_call(
        spread_kernel,
        in_specs=[smem, vmem, vmem, vmem],
        out_specs=[vmem] * STEPS,
        out_shape=[jax.ShapeDtypeStruct((ROWS, FEAT), jnp.bfloat16)] * STEPS,
        scratch_shapes=[pltpu.VMEM((STEPS * ROWS, FEAT), jnp.float32)],
        compiler_params=params(),
        cost_estimate=cost(10**9, 4 * 2**20),
        name="spread_tiles",
    )(index, *turned, d_mean)


def flipped(value, mask):
    return shifted(value, lambda block, rep: (block ^ mask, rep))


def added(left, right):
    return (left.astype(jnp.float32) + right.astype(jnp.float32)).astype(jnp.bfloat16)


def body(features, tile_index, tile_counts, w_self, w_neigh, bias, pos_pairs, neg_pairs):
    block, rep = lax.axis_index("blk"), lax.axis_index("rep")
    core = block & 1
    index, counts = tile_index[0, 0], tile_counts[0, 0]
    info = rep.reshape(1).astype(jnp.int32)
    pos_turned, neg_turned = pos_pairs.T, neg_pairs.T

    held = {s: from_step(features, s) for s in (4, 1, 3, 2, 0)}
    tiles_a, turned_a, degree = prepare_tiles(index, jnp.zeros((8, TILE), jnp.float32), counts, 0, 2)
    tiles_b, turned_b, degree = prepare_tiles(index, degree, counts, 1, 2)
    held[1], degree = tied((held[1], degree), turned_b)
    held[5] = from_before(held[1])
    (held[3],) = tied((held[3],), held[4])
    held[7] = from_before(held[3])
    (held[2],) = tied((held[2],), held[5], held[3])
    held[6] = from_before(held[2])
    (pos_turned,) = tied((pos_turned,), held[2])
    joined_pos = join_pairs(pos_turned)
    (degree,) = tied((degree,), joined_pos)
    degree_other = shifted(degree, lambda b, r: (b, 1 - r))
    mine = gather_tiles(index, (tiles_a, tiles_b), [held[s] for s in range(STEPS)])
    other = shifted(mine, lambda b, r: (b, 1 - r))
    (neg_turned,) = tied((neg_turned,), mine)
    joined_neg = join_pairs(neg_turned)

    embeddings, d_self, d_mean, d_weight = layer(
        info, mine, other, degree, degree_other,
        features, w_self, w_neigh, bias.reshape(1, HID), (joined_pos, joined_neg),
    )

    rows = d_weight.shape[0] // 2
    kept = lax.dynamic_slice_in_dim(d_weight, core * rows, rows, 0)
    given = lax.dynamic_slice_in_dim(d_weight, (1 - core) * rows, rows, 0)
    summed = kept + flipped(given, 1)
    over_x = [flipped(summed, k << 5) for k in range(1, 4)]
    spread = spread_tiles(index, (turned_a, turned_b), d_mean)
    order = (2, 1, 3)
    back = {s: to_before(spread[s + NEAR]) for s in order}
    landed = {NEAR: to_step(spread[NEAR], NEAR)}
    summed = (summed + over_x[0]) + (over_x[1] + over_x[2])

    def over_z(_, value):
        for shift in (1, 2):
            value = value + flipped(value, 1 << shift)
        return value

    summed = lax.fori_loop(0, 1 + jnp.minimum(rep, 0), over_z, summed)
    later = tied([back[s] for s in order], landed[NEAR], summed)
    near = {s: added(spread[s], value) for s, value in zip(order, later)}
    near[0] = spread[0]
    landed.update({s: to_step(value, s) for s, value in near.items()})
    arrived = [landed[s].astype(jnp.float32) for s in (0, 4, 2, 1, 3)]
    partial = (arrived[0] + arrived[1]) + arrived[2] + (arrived[3] + arrived[4])
    partial = partial.astype(jnp.bfloat16)
    partial_other = shifted(partial, lambda b, r: (b, 1 - r))
    (summed,) = tied((summed,), partial)
    over_y = [flipped(summed, k << 3) for k in range(1, 4)]
    summed = (summed + over_y[0]) + (over_y[1] + over_y[2])
    traded = flipped(summed, 1)
    there = shifted(summed, lambda b, r: (b, 1 - r))
    aside = shifted(summed, lambda b, r: (b ^ 1, 1 - r))
    d_features = d_self + (partial.astype(jnp.float32) + partial_other.astype(jnp.float32))

    def whole(mine, others):
        return jnp.concatenate(
            [jnp.where(core == 0, mine, others), jnp.where(core == 0, others, mine)], axis=0
        )

    d_here, d_there = whole(summed, traded), whole(there, aside)
    d_w_self = jnp.where(rep == 0, d_here, d_there)[:FEAT]
    d_w_neigh = jnp.where(rep == 0, d_there, d_here)[:FEAT]
    return (embeddings, d_features, d_w_self, d_w_neigh, d_here[FEAT])


def solution(mesh):
    return jax.shard_map(
        body,
        mesh=mesh,
        in_specs=(
            P("blk", None),
            P("blk", "rep", None, None),
            P("blk", "rep", None, None, None),
            P(),
            P(),
            P(),
            P("blk", None),
            P("blk", None),
        ),
        out_specs=(P("blk", None), P("blk", None), P(), P(), P()),
        check_vma=False,
    )
```

```python
import math

import jax
import jax.numpy as jnp
from jax import lax
from jax.experimental import pallas as pl
from jax.experimental.pallas import tpu as pltpu
from jax.sharding import PartitionSpec as P

STEPS = 8
TILE = 128
ROWS = 1024
FEAT = 128
HID = 256
TILES = 64
BLOCKS = 128
REPS = 2
GROUP = 8
NEAR = STEPS // 2
WROWS = 144
PANEL = 256
norm_eps = 1e-05
VMEM_LIMIT = 56 * 1024 * 1024
across = (((1,), (1,)), ((), ()))
down = (((0,), (0,)), ((), ()))

vmem = pl.BlockSpec(memory_space=pltpu.VMEM)
smem = pl.BlockSpec(memory_space=pltpu.SMEM)
anywhere = pl.BlockSpec(memory_space=pl.ANY)


def params():
    return pltpu.CompilerParams(vmem_limit_bytes=VMEM_LIMIT)


def cost(flops, bytes_accessed):
    return pl.CostEstimate(flops=flops, bytes_accessed=bytes_accessed, transcendentals=0)


def shifted(value, source_of):
    route = []
    for block in range(BLOCKS):
        for rep in range(REPS):
            source = source_of(block, rep)
            if source is not None:
                route.append(((source[0] % BLOCKS) * REPS + source[1], block * REPS + rep))
    return lax.ppermute(value, ("blk", "rep"), route)


def from_step(value, step):
    return shifted(value, lambda block, rep: (block - rep - 2 * step, rep))


def to_step(value, step):
    return shifted(value, lambda block, rep: (block + rep + 2 * step, rep))


def from_before(value):
    return shifted(value, lambda block, rep: (block - STEPS, rep))


def to_before(value):
    return shifted(value, lambda block, rep: (block + STEPS, rep))


def tied(values, *others):
    flat = lax.optimization_barrier(tuple(values) + tuple(others))
    return flat[: len(values)]


def tiles_kernel(first, index_ref, before_ref, counts_ref, tile_ref, turned_ref, degree_ref, sums):
    group = pl.program_id(0)

    @pl.when(group == 0)
    def _():
        sums[...] = jnp.zeros_like(sums)

    ones = jnp.ones((8, TILE), jnp.bfloat16)
    for k in range(GROUP):
        slot = first + group * GROUP + k
        used = index_ref[0, slot] < STEPS
        counts = jnp.where(used, counts_ref[k], 0).astype(jnp.float32)
        turned = counts.T.astype(jnp.bfloat16)
        tile_ref[k] = counts.astype(jnp.bfloat16)
        turned_ref[k] = turned
        row = index_ref[1, slot]
        sums[row] += jnp.dot(ones, turned, preferred_element_type=jnp.float32)

    @pl.when(group == pl.num_programs(0) - 1)
    def _():
        degree_ref[...] = before_ref[...] + sums[:, 0, :]


def prepare_tiles(index, before, counts, part, parts):
    share = TILES // parts
    spec = pl.BlockSpec((GROUP, TILE, TILE), lambda g: (g, 0, 0))
    shape = jax.ShapeDtypeStruct((share, TILE, TILE), jnp.bfloat16)
    whole = pl.BlockSpec((8, TILE), lambda g: (0, 0))
    return pl.pallas_call(
        lambda *refs: tiles_kernel(part * share, *refs),
        grid=(share // GROUP,),
        in_specs=[
            smem,
            whole,
            pl.BlockSpec((GROUP, TILE, TILE), lambda g: (g + part * share // GROUP, 0, 0)),
        ],
        out_specs=[spec, spec, whole],
        out_shape=[shape, shape, jax.ShapeDtypeStruct((8, TILE), jnp.float32)],
        scratch_shapes=[pltpu.VMEM((8, 8, TILE), jnp.float32)],
        compiler_params=params(),
        cost_estimate=cost(10**9, 8 * 2**20),
        name="prepare_tiles",
    )(index, before, counts)


def pairs_kernel(turned, joined_ref, left, right):
    def fill(i, carry):
        at = pl.ds(pl.multiple_of(i * TILE, TILE), TILE)
        rows = lax.broadcasted_iota(jnp.int32, (TILE, ROWS), 0) + i * TILE
        left[at, :] = (turned[0:1, :] == rows).astype(jnp.float32).astype(left.dtype)
        right[at, :] = (turned[1:2, :] == rows).astype(jnp.float32).astype(right.dtype)
        return carry

    lax.fori_loop(0, ROWS // TILE, fill, 0)
    for i in range(ROWS // PANEL):
        at = pl.ds(i * PANEL, PANEL)
        joined_ref[at, :] = lax.dot_general(
            left[at, :], right[...], across, preferred_element_type=jnp.float32
        )
    for i in range(ROWS // TILE):
        for j in range(i, ROWS // TILE):
            over = (pl.ds(i * TILE, TILE), pl.ds(j * TILE, TILE))
            under = (pl.ds(j * TILE, TILE), pl.ds(i * TILE, TILE))
            both = joined_ref[over] + joined_ref[under].T
            joined_ref[over] = both
            if i != j:
                joined_ref[under] = both.T


def join_pairs(turned):
    return pl.pallas_call(
        pairs_kernel,
        in_specs=[vmem],
        out_specs=vmem,
        out_shape=jax.ShapeDtypeStruct((ROWS, ROWS), jnp.float32),
        scratch_shapes=[pltpu.VMEM((ROWS, ROWS), jnp.float8_e4m3fn)] * 2,
        compiler_params=params(),
        cost_estimate=cost(3 * 10**9, 4 * 2**20),
        name="join_pairs",
    )(turned)


def held_row(index_ref, slot):
    step = jnp.minimum(index_ref[0, slot], STEPS - 1)
    return pl.multiple_of(step * ROWS + index_ref[2, slot] * TILE, TILE)


def gather_kernel(index_ref, tile_a, tile_b, *refs):
    blocks, (out_ref, held, total, sem) = refs[:STEPS], refs[STEPS:]
    copies = [
        pltpu.make_async_copy(block, held.at[pl.ds(k * ROWS, ROWS)], sem.at[k])
        for k, block in enumerate(blocks)
    ]
    for copy in copies:
        copy.start()
    total[...] = jnp.zeros_like(total)
    for copy in copies:
        copy.wait()
    for slot in range(TILES):
        tile = (tile_a if slot < TILES // 2 else tile_b)[slot % (TILES // 2)]
        source = held_row(index_ref, slot)
        target = pl.multiple_of(index_ref[1, slot] * TILE, TILE)
        total[pl.ds(target, TILE), :] += jnp.dot(
            tile, held[pl.ds(source, TILE), :], preferred_element_type=jnp.float32
        )
    out_ref[...] = total[...].astype(jnp.bfloat16)


def gather_tiles(index, tiles, blocks):
    return pl.pallas_call(
        gather_kernel,
        in_specs=[smem, vmem, vmem] + [anywhere] * STEPS,
        out_specs=vmem,
        out_shape=jax.ShapeDtypeStruct((ROWS, FEAT), jnp.bfloat16),
        scratch_shapes=[
            pltpu.VMEM((STEPS * ROWS, FEAT), jnp.bfloat16),
            pltpu.VMEM((ROWS, FEAT), jnp.float32),
            pltpu.SemaphoreType.DMA((STEPS,)),
        ],
        compiler_params=params(),
        cost_estimate=cost(10**9, 4 * 2**20),
        name="gather_tiles",
    )(index, *tiles, *blocks)


def layer_kernel(
    info_ref, mine_ref, other_ref, deg_mine, deg_other, feat_ref, w_self, w_neigh, bias,
    joined_pos, joined_neg,
    emb_ref, d_self_ref, d_mean_ref, d_weight_ref,
    counts, hidden, scaled, mean, inverse, grad, bias_sum, sem,
):
    copies = [
        pltpu.make_async_copy(ref, counts.at[k], sem.at[k])
        for k, ref in enumerate((joined_pos, joined_neg))
    ]
    for copy in copies:
        copy.start()
    factor = -math.log2(math.e) / math.sqrt(HID)

    def divisor_of(i):
        rows = []
        for k in range(i * PANEL // TILE, (i + 1) * PANEL // TILE):
            row = deg_mine[pl.ds(k, 1), :] + deg_other[pl.ds(k, 1), :]
            rows.append(jnp.broadcast_to(jnp.maximum(row, 1.0), (TILE, TILE)).T)
        return jnp.concatenate(rows, axis=0)

    for i in range(ROWS // PANEL):
        at = pl.ds(i * PANEL, PANEL)
        total = mine_ref[at, :].astype(jnp.float32) + other_ref[at, :].astype(jnp.float32)
        low = (total / divisor_of(i)).astype(jnp.bfloat16)
        mean[at, :] = low
        preact = (
            jnp.dot(feat_ref[at, :], w_self[...], preferred_element_type=jnp.float32)
            + jnp.dot(low, w_neigh[...], preferred_element_type=jnp.float32)
            + bias[...]
        )
        inv = lax.rsqrt(jnp.mean(preact * preact, axis=1, keepdims=True) + norm_eps)
        hid = preact * inv
        hidden[at, :] = hid
        inverse[at, :] = inv
        emb_ref[at, :] = hid.astype(jnp.bfloat16)
        scaled[at, :] = (hid * factor).astype(jnp.bfloat16)

    for copy in copies:
        copy.wait()
    bias_sum[...] = jnp.zeros_like(bias_sum)
    diagonal = lax.broadcasted_iota(jnp.int32, (PANEL, PANEL), 0) == lax.broadcasted_iota(
        jnp.int32, (PANEL, PANEL), 1
    )
    for i in range(ROWS // PANEL):
        at = pl.ds(i * PANEL, PANEL)
        d_hidden = jnp.zeros((PANEL, HID), jnp.float32)
        for j in range(ROWS // PANEL):
            to = pl.ds(j * PANEL, PANEL)
            power = lax.dot_general(
                scaled[at, :], emb_ref[to, :], across, preferred_element_type=jnp.float32
            )
            grown = jnp.exp2(power)
            coef = (counts[1, at, to] - counts[0, at, to] * grown) * pl.reciprocal(
                1.0 + grown, approx=True
            )
            if i == j:
                own = jnp.where(diagonal, coef, 0.0)
                coef = coef - own
                d_hidden += jnp.sum(own, axis=1, keepdims=True) * hidden[at, :]
            d_hidden += jnp.dot(
                coef.astype(jnp.bfloat16), emb_ref[to, :], preferred_element_type=jnp.float32
            )
        d_hidden *= 1.0 / math.sqrt(HID)
        hid = hidden[at, :]
        d_preact = inverse[at, :] * (
            d_hidden - hid * jnp.mean(d_hidden * hid, axis=1, keepdims=True)
        )
        bias_sum[...] += jnp.sum(d_preact.reshape(PANEL // 8, 8, HID), axis=0)
        low = d_preact.astype(jnp.bfloat16)
        grad[at, :] = low
        d_self_ref[at, :] = lax.dot_general(
            low, w_self[...], across, preferred_element_type=jnp.float32
        )
        d_mean_ref[at, :] = (
            lax.dot_general(low, w_neigh[...], across, preferred_element_type=jnp.float32)
            / divisor_of(i)
        ).astype(jnp.bfloat16)
    chosen = jnp.where(
        info_ref[0] == 0, feat_ref[...].astype(jnp.float32), mean[...].astype(jnp.float32)
    )
    d_weight_ref[0:FEAT, :] = lax.dot_general(
        chosen.astype(jnp.bfloat16), grad[...], down, preferred_element_type=jnp.float32
    )
    d_weight_ref[FEAT : FEAT + 8, :] = jnp.broadcast_to(
        jnp.sum(bias_sum[...], axis=0, keepdims=True), (8, HID)
    )
    d_weight_ref[FEAT + 8 :, :] = jnp.zeros((WROWS - FEAT - 8, HID), jnp.float32)


def layer(info, mine, other, deg_mine, deg_other, features, w_self, w_neigh, bias, joined):
    shapes = [
        jax.ShapeDtypeStruct((ROWS, HID), jnp.bfloat16),
        jax.ShapeDtypeStruct((ROWS, FEAT), jnp.float32),
        jax.ShapeDtypeStruct((ROWS, FEAT), jnp.bfloat16),
        jax.ShapeDtypeStruct((WROWS, HID), jnp.float32),
    ]
    return pl.pallas_call(
        layer_kernel,
        in_specs=[smem] + [vmem] * 8 + [anywhere] * 2,
        out_specs=[vmem] * 4,
        out_shape=shapes,
        scratch_shapes=[
            pltpu.VMEM((2, ROWS, ROWS), jnp.float32),
            pltpu.VMEM((ROWS, HID), jnp.float32),
            pltpu.VMEM((ROWS, HID), jnp.bfloat16),
            pltpu.VMEM((ROWS, FEAT), jnp.bfloat16),
            pltpu.VMEM((ROWS, 1), jnp.float32),
            pltpu.VMEM((ROWS, HID), jnp.bfloat16),
            pltpu.VMEM((8, HID), jnp.float32),
            pltpu.SemaphoreType.DMA((2,)),
        ],
        compiler_params=params(),
        cost_estimate=cost(2 * 10**9, 12 * 2**20),
        name="layer",
    )(info, mine, other, deg_mine, deg_other, features, w_self, w_neigh, bias, *joined)


def spread_kernel(index_ref, turned_a, turned_b, grad_ref, *refs):
    outs, (total,) = refs[:STEPS], refs[STEPS:]
    total[...] = jnp.zeros_like(total)
    for slot in range(TILES):
        tile = (turned_a if slot < TILES // 2 else turned_b)[slot % (TILES // 2)]
        target = held_row(index_ref, slot)
        source = pl.multiple_of(index_ref[1, slot] * TILE, TILE)
        total[pl.ds(target, TILE), :] += jnp.dot(
            tile, grad_ref[pl.ds(source, TILE), :], preferred_element_type=jnp.float32
        )
    for k, out in enumerate(outs):
        out[...] = total[k * ROWS : (k + 1) * ROWS, :].astype(jnp.bfloat16)


def spread_tiles(index, turned, d_mean):
    return pl.pallas_call(
        spread_kernel,
        in_specs=[smem, vmem, vmem, vmem],
        out_specs=[vmem] * STEPS,
        out_shape=[jax.ShapeDtypeStruct((ROWS, FEAT), jnp.bfloat16)] * STEPS,
        scratch_shapes=[pltpu.VMEM((STEPS * ROWS, FEAT), jnp.float32)],
        compiler_params=params(),
        cost_estimate=cost(10**9, 4 * 2**20),
        name="spread_tiles",
    )(index, *turned, d_mean)


def flipped(value, mask):
    return shifted(value, lambda block, rep: (block ^ mask, rep))


def added(left, right):
    return (left.astype(jnp.float32) + right.astype(jnp.float32)).astype(jnp.bfloat16)


def body(features, tile_index, tile_counts, w_self, w_neigh, bias, pos_pairs, neg_pairs):
    block, rep = lax.axis_index("blk"), lax.axis_index("rep")
    core = block & 1
    index, counts = tile_index[0, 0], tile_counts[0, 0]
    info = rep.reshape(1).astype(jnp.int32)
    pos_turned, neg_turned = pos_pairs.T, neg_pairs.T

    held = {s: from_step(features, s) for s in (4, 1, 3, 2, 0)}
    tiles_a, turned_a, degree = prepare_tiles(index, jnp.zeros((8, TILE), jnp.float32), counts, 0, 2)
    tiles_b, turned_b, degree = prepare_tiles(index, degree, counts, 1, 2)
    held[1], degree = tied((held[1], degree), turned_b)
    held[5] = from_before(held[1])
    (held[3],) = tied((held[3],), held[4])
    held[7] = from_before(held[3])
    (held[2],) = tied((held[2],), held[5], held[3])
    held[6] = from_before(held[2])
    (pos_turned,) = tied((pos_turned,), held[2])
    joined_pos = join_pairs(pos_turned)
    (degree,) = tied((degree,), joined_pos)
    degree_other = shifted(degree, lambda b, r: (b, 1 - r))
    mine = gather_tiles(index, (tiles_a, tiles_b), [held[s] for s in range(STEPS)])
    other = shifted(mine, lambda b, r: (b, 1 - r))
    (neg_turned,) = tied((neg_turned,), mine)
    joined_neg = join_pairs(neg_turned)

    embeddings, d_self, d_mean, d_weight = layer(
        info, mine, other, degree, degree_other,
        features, w_self, w_neigh, bias.reshape(1, HID), (joined_pos, joined_neg),
    )

    rows = d_weight.shape[0] // 2
    kept = lax.dynamic_slice_in_dim(d_weight, core * rows, rows, 0)
    given = lax.dynamic_slice_in_dim(d_weight, (1 - core) * rows, rows, 0)
    summed = kept + flipped(given, 1)
    over_x = [flipped(summed, k << 5) for k in range(1, 4)]
    spread = spread_tiles(index, (turned_a, turned_b), d_mean)
    order = (2, 1, 3)
    back = {s: to_before(spread[s + NEAR]) for s in order}
    landed = {NEAR: to_step(spread[NEAR], NEAR)}
    summed = (summed + over_x[0]) + (over_x[1] + over_x[2])

    def over_z(_, value):
        for shift in (1, 2):
            value = value + flipped(value, 1 << shift)
        return value

    summed = lax.fori_loop(0, 1 + jnp.minimum(rep, 0), over_z, summed)
    later = tied([back[s] for s in order], landed[NEAR], summed)
    near = {s: added(spread[s], value) for s, value in zip(order, later)}
    near[0] = spread[0]
    landed.update({s: to_step(value, s) for s, value in near.items()})
    arrived = [landed[s].astype(jnp.float32) for s in (0, 4, 2, 1, 3)]
    partial = (arrived[0] + arrived[1]) + arrived[2] + (arrived[3] + arrived[4])
    partial = partial.astype(jnp.bfloat16)
    partial_other = shifted(partial, lambda b, r: (b, 1 - r))
    (summed,) = tied((summed,), partial)
    over_y = [flipped(summed, k << 3) for k in range(1, 4)]
    summed = (summed + over_y[0]) + (over_y[1] + over_y[2])
    (summed,) = tied((summed,), partial_other)
    traded = flipped(summed, 1)
    there = shifted(summed, lambda b, r: (b, 1 - r))
    aside = shifted(summed, lambda b, r: (b ^ 1, 1 - r))
    d_features = d_self + (partial.astype(jnp.float32) + partial_other.astype(jnp.float32))

    def whole(mine, others):
        return jnp.concatenate(
            [jnp.where(core == 0, mine, others), jnp.where(core == 0, others, mine)], axis=0
        )

    d_here, d_there = whole(summed, traded), whole(there, aside)
    d_w_self = jnp.where(rep == 0, d_here, d_there)[:FEAT]
    d_w_neigh = jnp.where(rep == 0, d_there, d_here)[:FEAT]
    return (embeddings, d_features, d_w_self, d_w_neigh, d_here[FEAT])


def solution(mesh):
    return jax.shard_map(
        body,
        mesh=mesh,
        in_specs=(
            P("blk", None),
            P("blk", "rep", None, None),
            P("blk", "rep", None, None, None),
            P(),
            P(),
            P(),
            P("blk", None),
            P("blk", None),
        ),
        out_specs=(P("blk", None), P("blk", None), P(), P(), P()),
        check_vma=False,
    )
```
